32 devices in a mesh: req: 8 (over z, y), tp: 4 (over x, core).
Axes of the slice: x: 2, y: 2, z: 4, core: 2. Of those that a mesh axis runs over, the one named last changes fastest.
Arguments:
- q_pre: bfloat16 [4096, 1024], P(('req', 'tp')), may hold values from -6 to 6
- gate_pre: bfloat16 [4096, 8], P(('req', 'tp')), may hold values from -6 to 6
- k_pre: bfloat16 [4096, 512], P(('req', 'tp')), may hold values from -6 to 6
- v_pre: bfloat16 [4096, 512], P(('req', 'tp')), may hold values from -6 to 6
- q_gain: float32 [128], replicated, may hold values from 0.1 to 1.9
- k_gain: float32 [128], replicated, may hold values from 0.1 to 1.9
- lengths: int32 [8, 3], P('req'), may hold values from 1 to 256, 512 in all within a row
- q_new: bfloat16 [24, 1024], P('req'), may hold values from -6 to 6
- gate_new: bfloat16 [24, 8], P('req'), may hold values from -6 to 6
- k_new: bfloat16 [24, 512], P('req'), may hold values from -6 to 6
- v_new: bfloat16 [24, 512], P('req'), may hold values from -6 to 6
- resid: bfloat16 [24, 2048], P('req'), may hold values from -5 to 5
- w_out: bfloat16 [1024, 2048], P('tp'), may hold values from -0.1875 to 0.1875
- norm_gain: float32 [2048], replicated, may hold values from 0.1 to 1.9
- w_gate: bfloat16 [2048, 3072], P('req', 'tp'), may hold values from -0.125 to 0.125
- w_up: bfloat16 [2048, 3072], P('req', 'tp'), may hold values from -0.125 to 0.125
- w_down: bfloat16 [3072, 2048], P('tp', 'req'), may hold values from -0.109375 to 0.109375
Outputs:
- prefill_out: bfloat16 [4096, 1024], P(('req', 'tp'))
- decode_out: bfloat16 [24, 2048], P('req')
The draws below stay inside these ranges and needn't reach their ends.
Inputs may be any that keep to these rules, and one draw needn't show every extreme that they name: Each row holds the prompt lengths of one group's 3 requests; they sum to 512 and the longest is exactly 256.
All inputs are finite; a program needn't handle non-finite values.
Results may differ from the reference program's by a relative error of at most 0.0065.
Values may be sent and summed in bfloat16 or wider, within the bound.
No kernel may reach another device: no remote copies, remote signals or barrier semaphores. Data moves between devices by JAX's collectives and lax.ppermute only.
A program may use at most 64 MiB of HBM per device.

```python
import math
import jax
import jax.numpy as jnp
import numpy as np
from jax import lax

D = 2048
FF = 3072
HD = 128
Q_HEADS = 8
KV_HEADS = 4
SEQ = 512
MAX_LEN = 256
RPG = 3
TOKENS = 4096
REQUESTS = 24
N_REQ = 8


def block_scale(own_key, shape, shards, least, top_value):
    level = 1.0
    for dim, shards_of in shards:
        draws = jax.random.uniform(jax.random.fold_in(jax.random.fold_in(own_key, 6), dim), (shards_of,), jnp.float32, least / len(shards), top_value / len(shards))
        level = level * jnp.repeat(jnp.exp(draws), shape[dim] // shards_of).reshape((-1,) + (1,) * (len(shape) - 1 - dim))
    return level


def split_up(number_of, total, bound, slope):
    weights = [(1 << 20) // math.isqrt(grade ** slope) + 1 for grade in range(2, number_of + 1)]
    rest, given = total - bound - (number_of - 1), [1] * (number_of - 1)
    while rest > 0:
        movable = [i for i in range(number_of - 1) if given[i] < bound]
        whole, remaining = sum([weights[i] for i in movable]), rest
        for i in movable:
            more = min(bound - given[i], max(1, remaining * weights[i] // whole), rest)
            given[i] = given[i] + more
            rest = rest - more
    return np.array([bound] + given)


def uneven_parts(key, count, total, limit, skew):
    if count == 2:
        one = jax.random.randint(key, (), max(1, total - limit), min(limit, total - 1) + 1)
        return jnp.stack([one, total - one])
    sizes = jnp.asarray(split_up(count, total, limit, skew), jnp.int32)
    pairs = (count - 1) // 2
    source_of, taker = sizes[1:1 + 2 * pairs:2], sizes[2:2 + 2 * pairs:2]
    margin = jnp.minimum(source_of - 1, limit - taker)
    moved = jax.random.randint(jax.random.fold_in(key, 1), (pairs,), 0, 1 << 20) % (margin + 1)
    sizes = sizes.at[1:1 + 2 * pairs:2].set(source_of - moved).at[2:2 + 2 * pairs:2].set(taker + moved)
    return sizes[jax.random.permutation(jax.random.fold_in(key, 2), count)]


def normal_values(own_key, shape, spread, reach, split=(), kind=jnp.bfloat16):
    entries = spread * jax.random.normal(own_key, shape, jnp.float32)
    if split:
        entries = entries * block_scale(own_key, shape, split, -0.22, 0.18)
    return jnp.clip(entries, -reach, reach).astype(kind)


def setup_inputs(seed: int = 0) -> dict:
    streams_of = jax.random.split(jax.random.key(seed), 18)
    return {
        "q_pre": normal_values(streams_of[0], (TOKENS, Q_HEADS * HD), 1.0, 6.0, ((0, 32),)),
        "gate_pre": normal_values(streams_of[1], (TOKENS, Q_HEADS), 1.5, 6.0, ((0, 32),)),
        "k_pre": normal_values(streams_of[2], (TOKENS, KV_HEADS * HD), 1.0, 6.0, ((0, 32),)),
        "v_pre": normal_values(streams_of[3], (TOKENS, KV_HEADS * HD), 1.0, 6.0, ((0, 32),)),
        "q_gain": jnp.clip(1.0 + 0.18 * jax.random.normal(streams_of[4], (HD,), jnp.float32), 0.1, 1.9),
        "k_gain": jnp.clip(1.0 + 0.18 * jax.random.normal(streams_of[5], (HD,), jnp.float32), 0.1, 1.9),
        "lengths": jax.vmap(lambda own: uneven_parts(own, RPG, SEQ, MAX_LEN, 2))(jax.random.split(streams_of[6], N_REQ)).reshape((N_REQ, RPG)).astype(jnp.int32),
        "q_new": normal_values(streams_of[7], (REQUESTS, Q_HEADS * HD), 1.0, 6.0, ((0, 8),)),
        "gate_new": normal_values(streams_of[8], (REQUESTS, Q_HEADS), 1.5, 6.0, ((0, 8),)),
        "k_new": normal_values(streams_of[9], (REQUESTS, KV_HEADS * HD), 1.0, 6.0, ((0, 8),)),
        "v_new": normal_values(streams_of[10], (REQUESTS, KV_HEADS * HD), 1.0, 6.0, ((0, 8),)),
        "resid": normal_values(streams_of[11], (REQUESTS, D), 0.7, 5.0, ((0, 8),)),
        "w_out": normal_values(streams_of[12], (Q_HEADS * HD, D), (Q_HEADS * HD) ** -0.5, 0.1875, ((0, 4),)),
        "norm_gain": jnp.clip(1.0 + 0.18 * jax.random.normal(streams_of[13], (D,), jnp.float32), 0.1, 1.9),
        "w_gate": normal_values(streams_of[14], (D, FF), D ** -0.5, 0.125, ((0, 8), (1, 4))),
        "w_up": normal_values(streams_of[15], (D, FF), D ** -0.5, 0.125, ((0, 8), (1, 4))),
        "w_down": normal_values(streams_of[16], (FF, D), FF ** -0.5, 0.109375, ((0, 4), (1, 8))),
    }


rope_base = 1000000.0
norm_eps = 1e-06

def group_layout(lengths_row, total):
    req_ends = jnp.cumsum(lengths_row).astype(jnp.int32)
    req_starts = (req_ends - lengths_row).astype(jnp.int32)
    indices = jnp.arange(total, dtype=jnp.int32)
    segment = lax.optimization_barrier(jnp.sum((indices[:, None] >= req_ends[None, :]).astype(jnp.int32), axis=1)).astype(jnp.int32)
    onehot = segment[:, None] == jnp.arange(lengths_row.shape[0], dtype=jnp.int32)[None, :]
    offsets = lax.optimization_barrier(jnp.sum(jnp.where(onehot, req_starts[None, :], 0), axis=1)).astype(jnp.int32)
    return (segment, (indices - offsets).astype(jnp.int32))

def head_norm(values, gain):
    mean_sq = lax.optimization_barrier(jnp.mean(values * values, axis=-1, keepdims=True))
    return values * lax.rsqrt(mean_sq + norm_eps) * gain

def rotate(values, position):
    half_size = values.shape[-1] // 2
    freqs = rope_base ** (-(jnp.arange(half_size, dtype=jnp.float32) * 2.0 / (2 * half_size)))
    angles = position.astype(jnp.float32)[:, None] * freqs[None, :]
    shaped = (values.shape[0],) + (1,) * (values.ndim - 2) + (half_size,)
    cosine = jnp.cos(angles).reshape(shaped)
    sine = jnp.sin(angles).reshape(shaped)
    first_half = values[..., :half_size]
    second_half = values[..., half_size:]
    return jnp.concatenate([first_half * cosine - second_half * sine, second_half * cosine + first_half * sine], axis=-1)

def reference(q_pre, gate_pre, k_pre, v_pre, q_gain, k_gain, lengths, q_new, gate_new, k_new, v_new, resid, w_out, norm_gain, w_gate, w_up, w_down):
    groups_per = Q_HEADS // KV_HEADS
    score_scale = HD ** (-0.5)

    def one_group(inputs):
        q_grp, g_grp, k_grp, v_grp, lengths_row, qn_grp, gn_grp, kn_grp, vn_grp = inputs
        segment, position = group_layout(lengths_row, SEQ)
        indices = jnp.arange(SEQ, dtype=jnp.int32)
        queries = rotate(head_norm(q_grp.reshape(SEQ, Q_HEADS, HD).astype(jnp.float32), q_gain), position).astype(jnp.bfloat16)
        keys = rotate(head_norm(k_grp.reshape(SEQ, KV_HEADS, HD).astype(jnp.float32), k_gain), position).astype(jnp.bfloat16)
        values = v_grp.reshape(SEQ, KV_HEADS, HD).astype(jnp.float32)
        query_f = lax.optimization_barrier(queries).astype(jnp.float32).reshape(SEQ, KV_HEADS, groups_per, HD)
        key_f = lax.optimization_barrier(keys).astype(jnp.float32)
        scores = jnp.einsum('qkgd,pkd->qkgp', query_f, key_f) * score_scale
        allowed = (segment[:, None] == segment[None, :]) & (indices[:, None] >= indices[None, :])
        weights = jnp.where(allowed[:, None, None, :], jnp.exp(scores), 0.0)
        totals = lax.optimization_barrier(jnp.sum(weights, axis=-1))
        rounded = lax.optimization_barrier(weights.astype(jnp.bfloat16)).astype(jnp.float32)
        mixed = jnp.einsum('qkgp,pkd->qkgd', rounded, values)
        gates = jax.nn.sigmoid(g_grp.astype(jnp.float32)).reshape(SEQ, KV_HEADS, groups_per)
        prefill = (mixed / totals[..., None] * gates[..., None]).astype(jnp.bfloat16).reshape(SEQ, Q_HEADS * HD)
        new_queries = rotate(head_norm(qn_grp.reshape(RPG, Q_HEADS, HD).astype(jnp.float32), q_gain), lengths_row).astype(jnp.bfloat16)
        new_keys = rotate(head_norm(kn_grp.reshape(RPG, KV_HEADS, HD).astype(jnp.float32), k_gain), lengths_row).astype(jnp.bfloat16)
        nq_f = lax.optimization_barrier(new_queries).astype(jnp.float32).reshape(RPG, KV_HEADS, groups_per, HD)
        nk_f = lax.optimization_barrier(new_keys).astype(jnp.float32)
        cache_scores = jnp.einsum('rkgd,pkd->rkgp', nq_f, key_f) * score_scale
        owned = segment[None, :] == jnp.arange(RPG, dtype=jnp.int32)[:, None]
        cache_weights = jnp.where(owned[:, None, None, :], jnp.exp(cache_scores), 0.0)
        self_weight = jnp.exp(jnp.einsum('rkgd,rkd->rkg', nq_f, nk_f) * score_scale)
        dec_totals = lax.optimization_barrier(jnp.sum(cache_weights, axis=-1)) + self_weight
        cache_rounded = lax.optimization_barrier(cache_weights.astype(jnp.bfloat16)).astype(jnp.float32)
        dec_mixed = jnp.einsum('rkgp,pkd->rkgd', cache_rounded, values)
        dec_mixed = dec_mixed + self_weight[..., None] * vn_grp.reshape(RPG, KV_HEADS, 1, HD).astype(jnp.float32)
        dec_gates = jax.nn.sigmoid(gn_grp.astype(jnp.float32)).reshape(RPG, KV_HEADS, groups_per)
        decoded = (dec_mixed / dec_totals[..., None] * dec_gates[..., None]).astype(jnp.bfloat16).reshape(RPG, Q_HEADS * HD)
        return (prefill, decoded)
    prefill_all, decode_heads = lax.map(one_group, (q_pre.reshape(N_REQ, SEQ, Q_HEADS * HD), gate_pre.reshape(N_REQ, SEQ, Q_HEADS), k_pre.reshape(N_REQ, SEQ, KV_HEADS * HD), v_pre.reshape(N_REQ, SEQ, KV_HEADS * HD), lengths, q_new.reshape(N_REQ, RPG, Q_HEADS * HD), gate_new.reshape(N_REQ, RPG, Q_HEADS), k_new.reshape(N_REQ, RPG, KV_HEADS * HD), v_new.reshape(N_REQ, RPG, KV_HEADS * HD)))
    decode_heads = decode_heads.reshape(REQUESTS, Q_HEADS * HD)
    hidden_state = resid.astype(jnp.float32) + jnp.dot(decode_heads, w_out, preferred_element_type=jnp.float32)
    mean_sq = lax.optimization_barrier(jnp.mean(hidden_state * hidden_state, axis=-1, keepdims=True))
    normed = (hidden_state * lax.rsqrt(mean_sq + norm_eps) * norm_gain).astype(jnp.bfloat16)
    gate_part = jnp.dot(normed, w_gate, preferred_element_type=jnp.float32)
    up_part = jnp.dot(normed, w_up, preferred_element_type=jnp.float32)
    hidden_units = (jax.nn.silu(gate_part) * up_part).astype(jnp.bfloat16)
    decode_out = (hidden_state + jnp.dot(hidden_units, w_down, preferred_element_type=jnp.float32)).astype(jnp.bfloat16)
    return (prefill_all.reshape(TOKENS, Q_HEADS * HD), decode_out)
```

```python
import jax
import jax.numpy as jnp
import numpy as np
from jax import lax
from jax.experimental import pallas as pl
from jax.experimental.pallas import tpu as pltpu
from jax.sharding import PartitionSpec as P

rope_base = 1000000.0
norm_eps = 1e-06


def group_layout(lengths_row, total):
    req_ends = jnp.cumsum(lengths_row)
    req_starts = req_ends - lengths_row
    indices = jnp.arange(total, dtype=jnp.int32)
    segment = jnp.sum((indices[:, None] >= req_ends[None, :]).astype(jnp.int32), axis=1)
    onehot = segment[:, None] == jnp.arange(lengths_row.shape[0], dtype=jnp.int32)[None, :]
    offsets = jnp.sum(jnp.where(onehot, req_starts[None, :], 0), axis=1)
    return (segment, indices - offsets)


def head_norm(values, gain):
    mean_sq = jnp.mean(values * values, axis=-1, keepdims=True)
    return values * lax.rsqrt(mean_sq + norm_eps) * gain


def rotate(values, position):
    half_size = values.shape[-1] // 2
    freqs = rope_base ** (-(jnp.arange(half_size, dtype=jnp.float32) * 2.0 / (2 * half_size)))
    angles = position.astype(jnp.float32)[:, None] * freqs[None, :]
    shaped = (values.shape[0],) + (1,) * (values.ndim - 2) + (half_size,)
    cosine = jnp.cos(angles).reshape(shaped)
    sine = jnp.sin(angles).reshape(shaped)
    first_half = values[..., :half_size]
    second_half = values[..., half_size:]
    return jnp.concatenate(
        [first_half * cosine - second_half * sine, second_half * cosine + first_half * sine],
        axis=-1,
    )


def general(
    q_pre,
    gate_pre,
    k_pre,
    v_pre,
    q_gain,
    k_gain,
    lengths,
    q_new,
    gate_new,
    k_new,
    v_new,
    resid,
    w_out,
    norm_gain,
    w_gate,
    w_up,
    w_down,
):
    tok_rows = q_pre.shape[0]
    tp_count = lax.axis_size("tp")
    tp_index = lax.axis_index("tp")
    head_size = q_gain.shape[0]
    query_heads = gate_pre.shape[1]
    kv_heads = k_pre.shape[1] // head_size
    groups_per = query_heads // kv_heads
    kv_local = kv_heads // tp_count
    req_count = lengths.shape[1]
    score_scale = head_size ** (-0.5)
    segment, position = group_layout(lengths[0], tok_rows * tp_count)
    row_offset = tp_index * tok_rows
    seg_local = lax.dynamic_slice_in_dim(segment, row_offset, tok_rows)
    pos_local = lax.dynamic_slice_in_dim(position, row_offset, tok_rows)
    query_index = row_offset + jnp.arange(tok_rows, dtype=jnp.int32)
    queries = rotate(
        head_norm(q_pre.reshape(tok_rows, query_heads, head_size).astype(jnp.float32), q_gain),
        pos_local,
    )
    queries = queries.astype(jnp.bfloat16).reshape(tok_rows, kv_heads, groups_per, head_size)
    keys = rotate(
        head_norm(k_pre.reshape(tok_rows, kv_heads, head_size).astype(jnp.float32), k_gain),
        pos_local,
    ).astype(jnp.bfloat16)
    values = v_pre.reshape(tok_rows, kv_heads, head_size)

    def key_block(running, key_piece, value_piece, first_row):
        key_count = key_piece.shape[0]
        key_index = first_row + jnp.arange(key_count, dtype=jnp.int32)
        allowed = (seg_local[:, None] == segment[None, :]) & (
            query_index[:, None] >= key_index[None, :]
        )
        scores = (
            jnp.einsum(
                "qkgd,pkd->qkgp",
                queries,
                key_piece.reshape(key_count, kv_heads, head_size),
                preferred_element_type=jnp.float32,
            )
            * score_scale
        )
        weights = jnp.where(allowed[:, None, None, :], jnp.exp(scores), 0.0)
        totals = running[0] + jnp.sum(weights, axis=-1)
        mixed = running[1] + jnp.einsum(
            "qkgp,pkd->qkgd",
            weights.astype(jnp.bfloat16),
            value_piece.reshape(key_count, kv_heads, head_size),
            preferred_element_type=jnp.float32,
        )
        return (totals, mixed)

    start_state = (
        jnp.zeros((tok_rows, kv_heads, groups_per), jnp.float32),
        jnp.zeros((tok_rows, kv_heads, groups_per, head_size), jnp.float32),
    )
    pieces = (
        lax.all_gather(keys.reshape(tok_rows, kv_heads * head_size), "tp", axis=0, tiled=True),
        lax.all_gather(v_pre, "tp", axis=0, tiled=True),
    )
    key_count = pieces[0].shape[0]
    block_rows = 512

    def one_block(number, carried):
        begin_at = number * block_rows
        return key_block(carried, pieces[0], pieces[1], begin_at)

    totals, mixed = lax.fori_loop(0, key_count // block_rows, one_block, start_state)
    gates = jax.nn.sigmoid(gate_pre.astype(jnp.float32)).reshape(tok_rows, kv_heads, groups_per)
    prefill_out = (
        (mixed / totals[..., None] * gates[..., None])
        .astype(jnp.bfloat16)
        .reshape(tok_rows, query_heads * head_size)
    )
    new_queries = rotate(
        head_norm(q_new.reshape(req_count, query_heads, head_size).astype(jnp.float32), q_gain),
        lengths[0],
    )
    new_queries = new_queries.astype(jnp.bfloat16).reshape(
        req_count, kv_heads, groups_per, head_size
    )
    new_keys = rotate(
        head_norm(k_new.reshape(req_count, kv_heads, head_size).astype(jnp.float32), k_gain),
        lengths[0],
    ).astype(jnp.bfloat16)
    new_values = v_new.reshape(req_count, kv_heads, head_size)
    new_gates = jax.nn.sigmoid(gate_new.astype(jnp.float32)).reshape(
        req_count, kv_heads, groups_per
    )
    head_first = tp_index * kv_local
    request_ids = jnp.arange(req_count, dtype=jnp.int32)
    own_queries = lax.dynamic_slice_in_dim(new_queries, head_first, kv_local, 1)
    cache_keys, cache_values = (
        lax.all_to_all(keys, "tp", split_axis=1, concat_axis=0, tiled=True),
        lax.all_to_all(values, "tp", split_axis=1, concat_axis=0, tiled=True),
    )
    scores = (
        jnp.einsum("rkgd,pkd->rkgp", own_queries, cache_keys, preferred_element_type=jnp.float32)
        * score_scale
    )
    owned = segment[None, :] == request_ids[:, None]
    weights = jnp.where(owned[:, None, None, :], jnp.exp(scores), 0.0)
    weighted = jnp.einsum(
        "rkgp,pkd->rkgd",
        weights.astype(jnp.bfloat16),
        cache_values,
        preferred_element_type=jnp.float32,
    )
    dec_totals = jnp.sum(weights, axis=-1)
    dec_mixed = weighted
    own_keys = lax.dynamic_slice_in_dim(new_keys, head_first, kv_local, 1)
    own_values = lax.dynamic_slice_in_dim(new_values, head_first, kv_local, 1)
    own_gates = lax.dynamic_slice_in_dim(new_gates, head_first, kv_local, 1)
    self_weight = jnp.exp(
        jnp.einsum("rkgd,rkd->rkg", own_queries, own_keys, preferred_element_type=jnp.float32)
        * score_scale
    )
    dec_totals = dec_totals + self_weight
    dec_mixed = dec_mixed + self_weight[..., None] * own_values.astype(jnp.float32)[:, :, None, :]
    attended = (
        (dec_mixed / dec_totals[..., None] * own_gates[..., None])
        .astype(jnp.bfloat16)
        .reshape(req_count, kv_local * groups_per * head_size)
    )
    partial_out = jnp.dot(attended, w_out, preferred_element_type=jnp.float32)
    attn_rows = lax.psum(partial_out, "tp")
    hidden_state = resid.astype(jnp.float32) + attn_rows
    mean_sq = jnp.mean(hidden_state * hidden_state, axis=-1, keepdims=True)
    normed = (hidden_state * lax.rsqrt(mean_sq + norm_eps) * norm_gain).astype(jnp.bfloat16)
    units_local = w_gate.shape[1]
    paired = jnp.concatenate([w_gate, w_up], axis=1)
    columns = lax.all_to_all(normed, "req", split_axis=1, concat_axis=0, tiled=True)
    whole_sums = lax.psum(jnp.dot(columns, paired, preferred_element_type=jnp.float32), "req")
    hidden_units = (jax.nn.silu(whole_sums[:, :units_local]) * whole_sums[:, units_local:]).astype(
        jnp.bfloat16
    )
    down_part = jnp.dot(hidden_units, w_down, preferred_element_type=jnp.float32)
    back_part = lax.all_to_all(down_part, "req", split_axis=0, concat_axis=1, tiled=True)
    mlp_rows = lax.psum(back_part, "tp")
    decode_out = (hidden_state + mlp_rows).astype(jnp.bfloat16)
    return (prefill_out, decode_out)


f32 = jnp.float32
bf16 = jnp.bfloat16
lanes = 128
pay_rows = 32
back_rows = 16


def dot(a, b):
    return jnp.dot(a, b, preferred_element_type=f32)


def dot_nt(a, b):
    return lax.dot_general(a, b, (((1,), (1,)), ((), ())), preferred_element_type=f32)


def iota(shape, dim):
    return lax.broadcasted_iota(jnp.int32, shape, dim)


def rope_factors(angles):
    turns = jnp.floor(angles * (2.0 / np.pi) + 0.5)
    rest = angles - turns * 1.5703125
    rest = rest - turns * 4.837512969970703125e-4
    rest = rest - turns * 7.549789948768648e-8
    sq = rest * rest
    sine = ((-1.9515295891e-4 * sq + 8.3321608736e-3) * sq - 1.6666654611e-1) * sq * rest + rest
    cosine = (
        ((2.443315711809948e-5 * sq - 1.388731625493765e-3) * sq + 4.166664568298827e-2) * sq * sq
        - 0.5 * sq
        + 1.0
    )
    low = iota(angles.shape, 1) < lanes // 2
    quarter = turns.astype(jnp.int32) + jnp.where(low, 1, 0)
    both = jnp.where((quarter & 1) == 1, cosine, sine)
    both = jnp.where((quarter & 2) == 2, -both, both)
    swapped = pltpu.roll(both, lanes // 2, 1)
    return jnp.where(low, both, swapped), jnp.where(low, -swapped, both)


def norm_rope(values, gain, factors):
    mean_sq = jnp.mean(values * values, axis=-1, keepdims=True)
    normed = values * lax.rsqrt(mean_sq + norm_eps) * gain
    return (normed * factors[0] + pltpu.roll(normed, lanes // 2, 1) * factors[1]).astype(bf16)


def begin_of(indices, len_ref):
    begin = jnp.zeros_like(indices)
    end = 0
    for j in range(len_ref.shape[1] - 1):
        end = end + len_ref[0, j]
        begin = jnp.where(indices >= end, end, begin)
    return begin


def partial_kernel(
    len_ref, k_ref, v_ref, qn_ref, kn_ref, vn_ref, gn_ref, resid_ref, qg_ref, kg_ref, freq_ref,
    kv_ref, pay_ref, row_q, row_k, row_v, row_g, pay,
):
    tp = lax.axis_index("tp")
    tok = k_ref.shape[0]
    rpg = qn_ref.shape[0]
    heads = qn_ref.shape[1] // lanes
    kvs = k_ref.shape[1] // lanes
    per = heads // kvs
    rows = heads * rpg
    freq = freq_ref[...]
    qg, kg = qg_ref[...], kg_ref[...]
    tok_index = tp * tok + iota((tok, lanes), 0)
    factors = rope_factors((tok_index - begin_of(tok_index, len_ref)).astype(f32) * freq)
    keys = []
    for k in range(kvs):
        at = slice(k * lanes, (k + 1) * lanes)
        keys.append(norm_rope(k_ref[:, at].astype(f32), kg, factors))
        kv_ref[:, at] = keys[-1]
    kv_ref[:, kvs * lanes :] = v_ref[...]
    qn, kn = qn_ref[...].astype(f32), kn_ref[...].astype(f32)
    vn, gn = vn_ref[...].astype(f32), gn_ref[...].astype(f32)
    for h in range(heads):
        at = slice(h * rpg, (h + 1) * rpg)
        kv = slice((h // per) * lanes, (h // per + 1) * lanes)
        row_q[at, :] = qn[:, h * lanes : (h + 1) * lanes]
        row_k[at, :] = kn[:, kv]
        row_v[at, :] = vn[:, kv]
        row_g[at, :] = jnp.broadcast_to(gn[:, h : h + 1], (rpg, lanes))
    row = iota((rows, lanes), 0)
    col = iota((rows, lanes), 1)
    head = row * 0
    for h in range(1, heads):
        head = jnp.where(row >= h * rpg, h, head)
    request = row - head * rpg
    length, first, last = row * 0, row * 0, row * 0
    end = 0
    for j in range(rpg):
        mine = request == j
        length = jnp.where(mine, len_ref[0, j], length)
        first = jnp.where(mine, end, first)
        end = end + len_ref[0, j]
        last = jnp.where(mine, end, last)
    new_factors = rope_factors(length.astype(f32) * freq)
    scale = lanes ** (-0.5)
    new_q = norm_rope(row_q[...], qg, new_factors)
    new_k = norm_rope(row_k[...], kg, new_factors)
    scores = jnp.zeros((rows, tok), f32)
    for k in range(kvs):
        mine = (head >= k * per) & (head < (k + 1) * per)
        scores = jnp.where(mine, dot_nt(new_q, keys[k]), scores)
    index = tp * tok + col
    weights = jnp.where((index >= first) & (index < last), jnp.exp(scores * scale), 0.0)
    totals = jnp.sum(weights, axis=-1, keepdims=True)
    rounded = weights.astype(bf16)
    mixed = jnp.zeros((rows, lanes), f32)
    for k in range(kvs):
        mine = (head >= k * per) & (head < (k + 1) * per)
        mixed = mixed + dot(
            jnp.where(mine, rounded, jnp.zeros_like(rounded)), v_ref[:, k * lanes : (k + 1) * lanes]
        )
    self_score = jnp.sum(new_q.astype(f32) * new_k.astype(f32), axis=-1, keepdims=True)
    self_weight = jnp.where(tp == 0, jnp.exp(self_score * scale), 0.0)
    totals = totals + self_weight
    mixed = (mixed + self_weight * row_v[...]) * jax.nn.sigmoid(row_g[...])
    total_row = jnp.sum(jnp.where(row == col, totals, 0.0), axis=0, keepdims=True)
    high = total_row.astype(bf16).astype(f32)
    pay[...] = jnp.zeros_like(pay)
    pay[0:rows, :] = mixed
    pay[rows + rpg : rows + rpg + 1, :] = high
    pay[rows + rpg + 1 : rows + rpg + 2, :] = total_row - high
    peers = pay_ref.shape[0]
    tps = lax.axis_size("tp")
    slices = resid_ref.shape[1] // (tps * lanes)
    for z in range(slices):
        at = pl.ds(pl.multiple_of((z * tps + tp) * lanes, lanes), lanes)
        pay[rows : rows + rpg, :] = resid_ref[:, at].astype(f32)
        out = pay[...].astype(bf16)
        for peer in range(z * peers // slices, (z + 1) * peers // slices):
            pay_ref[peer] = out


def hidden_kernel(
    pay_ref, w0_ref, w1_ref, w2_ref, w3_ref, gate_ref, up_ref, pair_ref, ng_ref,
    hid_ref, msg_ref, att, hid, xs, acc,
):
    tp = lax.axis_index("tp")
    req = lax.axis_index("req")
    tps = lax.axis_size("tp")
    z, y = lax.div(req, 2), lax.rem(req, 2)
    heads, toks, _ = att.shape
    groups = pay_ref.shape[0] // tps
    rpg = toks // groups
    rows = heads * rpg
    diag = iota((rows, lanes), 0) == iota((rows, lanes), 1)
    for r in range(groups):
        total = jnp.zeros(acc.shape, f32)
        for t in range(tps):
            piece = pay_ref[r * tps + t].astype(f32)
            total = total + piece
            acc[...] = piece
            hid[r * rpg : (r + 1) * rpg, t * lanes : (t + 1) * lanes] = acc[rows : rows + rpg, :]
        acc[...] = total
        total_row = acc[rows + rpg : rows + rpg + 1, :] + acc[rows + rpg + 1 : rows + rpg + 2, :]
        totals = jnp.sum(
            jnp.where(diag, jnp.broadcast_to(total_row, (rows, lanes)), 0.0), axis=-1, keepdims=True
        )
        acc[0:rows, :] = acc[0:rows, :] / totals
        for h in range(heads):
            att[h, r * rpg : (r + 1) * rpg, :] = acc[h * rpg : (h + 1) * rpg, :]
    state = hid[...]
    per = heads // tps
    for d, w_ref in enumerate((w0_ref, w1_ref, w2_ref, w3_ref)):
        source = lax.rem(tp + tps - d, tps)
        for j in range(per):
            state = state + dot(
                att[source * per + j].astype(bf16), w_ref[j * lanes : (j + 1) * lanes, :]
            )
    hid_ref[...] = state
    width = state.shape[1]
    half = width // 2
    sums = jnp.sum(state * state, axis=-1, keepdims=True)
    scaled = state * ng_ref[:, pl.ds(pl.multiple_of(z * width, lanes), width)]
    xs[0] = scaled[:, :half]
    xs[1] = scaled[:, half:]
    own, other = xs[y].astype(bf16), xs[1 - y].astype(bf16)
    units = pair_ref.shape[1] // 2
    at = pl.ds(pl.multiple_of(y * units, lanes), units)
    gate = dot(own, gate_ref[:, at]) + dot(other, pair_ref[:, :units])
    up = dot(own, up_ref[:, at]) + dot(other, pair_ref[:, units:])
    high = sums.astype(bf16).astype(f32)
    lane = iota((toks, lanes), 1)
    msg_ref[:, :units] = gate.astype(bf16)
    msg_ref[:, units : 2 * units] = up.astype(bf16)
    msg_ref[:, 2 * units :] = jnp.where(
        lane == 0, high, jnp.where(lane == 1, sums - high, 0.0)
    ).astype(bf16)


def down_kernel(m0_ref, m1_ref, m2_ref, m3_ref, hid_ref, down_ref, pair_ref, back_ref, part, pay):
    tp = lax.axis_index("tp")
    tps = lax.axis_size("tp")
    y = lax.rem(lax.axis_index("req"), 2)
    units, half = pair_ref.shape
    toks, width = hid_ref.shape
    total = m0_ref[...].astype(f32)
    for m_ref in (m1_ref, m2_ref, m3_ref):
        total = total + m_ref[...].astype(f32)
    sums = total[:, 2 * units : 2 * units + 1] + total[:, 2 * units + 1 : 2 * units + 2]
    factor = lax.rsqrt(sums / (width * 4) + norm_eps)
    gate = total[:, :units] * factor
    hidden = (gate / (1.0 + jnp.exp(-gate)) * (total[:, units : 2 * units] * factor)).astype(bf16)
    own_rows = pl.ds(pl.multiple_of(y * units, lanes), units)
    part[y] = dot(hidden, down_ref[own_rows, :])
    part[1 - y] = dot(hidden, pair_ref[...])
    chunks = width // lanes
    groups = pay.shape[0]
    rpg = toks // groups
    piece = hid_ref[:, pl.ds(pl.multiple_of(tp * lanes, lanes), lanes)]
    high = piece.astype(bf16).astype(f32)
    piece = jnp.where(y == 0, high, piece - high)
    pay[...] = jnp.zeros_like(pay)
    for c in range(chunks + 1):
        if c < chunks:
            at = (c * lanes) % half
            block = part[c * lanes // half][:, at : at + lanes]
        else:
            block = piece
        for r in range(groups):
            pay[r, c * rpg : (c + 1) * rpg, :] = block[r * rpg : (r + 1) * rpg, :]
    for r in range(groups):
        out = pay[r].astype(bf16)
        for t in range(tps):
            back_ref[r * tps + t] = out


def final_kernel(back_ref, out_ref, acc, tail, rows_out):
    tps = lax.axis_size("tp")
    peers = back_ref.shape[0]
    rpg, width = out_ref.shape
    chunks = tps
    slices = width // (chunks * lanes)
    group = peers // slices
    for z in range(slices):
        total = jnp.zeros(acc.shape, f32)
        by_tp = [jnp.zeros(acc.shape, f32) for _ in range(tps)]
        for p in range(group):
            piece = back_ref[z * group + p].astype(f32)
            total = total + piece
            by_tp[p % tps] = by_tp[p % tps] + piece
        acc[...] = total
        for c in range(chunks):
            tail[...] = by_tp[c]
            at = slice((z * chunks + c) * lanes, (z * chunks + c + 1) * lanes)
            rows_out[0:rpg, at] = (
                acc[c * rpg : (c + 1) * rpg, :] + tail[chunks * rpg : (chunks + 1) * rpg, :]
            )
    out_ref[...] = rows_out[0:rpg, :].astype(bf16)


def prefill_kernel(
    len_ref, q_ref, g_ref, kv0_ref, kv1_ref, kv2_ref, qg_ref, freq_ref, out_ref
):
    tp = lax.axis_index("tp")
    tok = q_ref.shape[0]
    heads = q_ref.shape[1] // lanes
    kvs = kv0_ref.shape[1] // (2 * lanes)
    per = heads // kvs
    blocks = (kv0_ref, kv1_ref, kv2_ref)
    tok_index = tp * tok + iota((tok, lanes), 0)
    begin = begin_of(tok_index, len_ref)
    factors = rope_factors((tok_index - begin).astype(f32) * freq_ref[...])
    col = iota((tok, tok), 1)
    allowed = []
    for b in range(len(blocks)):
        key_index = (tp - b) * tok + col
        allowed.append((key_index >= begin) & (key_index <= tok_index))
    gates = jax.nn.sigmoid(g_ref[...].astype(f32))
    qg = qg_ref[...]
    scale = lanes ** (-0.5)
    for h in range(heads):
        k = h // per
        at = slice(h * lanes, (h + 1) * lanes)
        query = norm_rope(q_ref[:, at].astype(f32), qg, factors)
        totals = jnp.zeros((tok, 1), f32)
        mixed = jnp.zeros((tok, lanes), f32)
        for b, kv_ref in enumerate(blocks):
            scores = dot_nt(query, kv_ref[:, k * lanes : (k + 1) * lanes])
            weights = jnp.where(allowed[b], jnp.exp(scores * scale), 0.0)
            totals = totals + jnp.sum(weights, axis=-1, keepdims=True)
            mixed = mixed + dot(
                weights.astype(bf16), kv_ref[:, (kvs + k) * lanes : (kvs + k + 1) * lanes]
            )
        out_ref[:, at] = (mixed / totals * gates[:, h : h + 1]).astype(bf16)


def call(body, out_shape, args, scratch=(), smem=0, flops=0, limit=12):
    specs = [pl.BlockSpec(memory_space=pltpu.SMEM)] * smem
    specs += [pl.BlockSpec(memory_space=pltpu.VMEM)] * (len(args) - smem)
    size = sum(a.size * a.dtype.itemsize for a in args)
    return pl.pallas_call(
        body,
        out_shape=out_shape,
        in_specs=specs,
        out_specs=jax.tree.map(lambda _: pl.BlockSpec(memory_space=pltpu.VMEM), out_shape),
        scratch_shapes=[pltpu.VMEM(s, f32) for s in scratch],
        compiler_params=pltpu.CompilerParams(vmem_limit_bytes=limit * 2**20),
        cost_estimate=pl.CostEstimate(flops=flops, bytes_accessed=size, transcendentals=0),
    )(*args)


def local(
    q_pre,
    gate_pre,
    k_pre,
    v_pre,
    q_gain,
    k_gain,
    lengths,
    q_new,
    gate_new,
    k_new,
    v_new,
    resid,
    w_out,
    norm_gain,
    w_gate,
    w_up,
    w_down,
):
    tps, reqs = lax.axis_size("tp"), lax.axis_size("req")
    tok = q_pre.shape[0]
    rpg, width = resid.shape
    slices = reqs // 2
    head_size = q_gain.shape[0]
    heads = gate_pre.shape[1]
    part = width // slices if slices else 0
    if not (slices == 4 and tps == 4 and head_size == lanes == tok and part == tps * lanes):
        return general(
            q_pre, gate_pre, k_pre, v_pre, q_gain, k_gain, lengths, q_new, gate_new, k_new, v_new,
            resid, w_out, norm_gain, w_gate, w_up, w_down,
        )
    peers = tps * reqs
    toks = rpg * reqs
    units = w_gate.shape[1] // 2
    req = lax.axis_index("req")
    z, y = req // 2, req % 2
    freqs = rope_base ** (-(np.arange(head_size // 2) * 2.0 / head_size))
    freqs = jnp.asarray(np.concatenate([freqs, freqs])[None, :], f32)
    qg, kg = q_gain[None, :], k_gain[None, :]

    def turn(array, by):
        return lax.ppermute(array, "tp", [(i, (i + by) % tps) for i in range(tps)])

    def swap(array):
        return lax.ppermute(array, "req", [(i, i ^ 1) for i in range(reqs)])

    def along(array, by):
        return lax.ppermute(array, "req", [(i, (i + 2 * by) % reqs) for i in range(reqs)])

    w_own = lax.dynamic_slice_in_dim(w_out, z * part, part, 1)
    w_pieces = [w_own] + [turn(w_own, d) for d in range(1, tps)]
    pair = jnp.concatenate(
        [lax.dynamic_slice_in_dim(w, (1 - y) * units, units, 1) for w in (w_gate, w_up)], axis=1
    )
    pair = swap(pair)
    down_pair = swap(lax.dynamic_slice_in_dim(w_down, (1 - y) * units, units, 0))

    kv, pay = call(
        partial_kernel,
        (
            jax.ShapeDtypeStruct((tok, 2 * k_pre.shape[1]), bf16),
            jax.ShapeDtypeStruct((peers, pay_rows, lanes), bf16),
        ),
        (lengths, k_pre, v_pre, q_new, k_new, v_new, gate_new, resid, qg, kg, freqs),
        scratch=[(heads * rpg, lanes)] * 4 + [(pay_rows, lanes)],
        smem=1,
        flops=10**7,
    )
    kv1, kv2 = turn(kv, 1), turn(kv, 2)
    got = lax.all_to_all(pay, ("req", "tp"), 0, 0, tiled=True)
    hid, msg = call(
        hidden_kernel,
        (
            jax.ShapeDtypeStruct((toks, part), f32),
            jax.ShapeDtypeStruct((toks, 2 * units + lanes), bf16),
        ),
        (got, *w_pieces, w_gate, w_up, pair, norm_gain[None, :]),
        scratch=[
            (heads, toks, lanes),
            (toks, part),
            (2, toks, part // 2),
            (pay_rows, lanes),
        ],
        flops=10**7,
    )
    prefill_out = call(
        prefill_kernel,
        jax.ShapeDtypeStruct(q_pre.shape, bf16),
        (lengths, q_pre, gate_pre, kv, kv1, kv2, qg, freqs),
        smem=1,
        flops=10**9,
    )
    msgs = [msg] + [along(msg, d) for d in range(1, slices)]
    back = call(
        down_kernel,
        jax.ShapeDtypeStruct((peers, back_rows, lanes), bf16),
        (*msgs, hid, w_down, down_pair),
        scratch=[(2, toks, part // 2), (reqs, back_rows, lanes)],
        flops=10**7,
    )
    returned = lax.all_to_all(back, ("req", "tp"), 0, 0, tiled=True)
    decode_out = call(
        final_kernel,
        jax.ShapeDtypeStruct((rpg, width), bf16),
        (returned,),
        scratch=[(back_rows, lanes), (back_rows, lanes), (8, width)],
        flops=10**6,
    )
    return (prefill_out, decode_out)


def solution(mesh):
    return jax.shard_map(
        local,
        mesh=mesh,
        in_specs=(
            P(("req", "tp"), None),
            P(("req", "tp"), None),
            P(("req", "tp"), None),
            P(("req", "tp"), None),
            P(),
            P(),
            P("req", None),
            P("req", None),
            P("req", None),
            P("req", None),
            P("req", None),
            P("req", None),
            P("tp", None),
            P(),
            P("req", "tp"),
            P("req", "tp"),
            P("tp", "req"),
        ),
        out_specs=(P(("req", "tp"), None), P("req", None)),
        check_vma=False,
    )
```

```python
import jax
import jax.numpy as jnp
import numpy as np
from jax import lax
from jax.experimental import pallas as pl
from jax.experimental.pallas import tpu as pltpu
from jax.sharding import PartitionSpec as P

rope_base = 1000000.0
norm_eps = 1e-06


def group_layout(lengths_row, total):
    req_ends = jnp.cumsum(lengths_row)
    req_starts = req_ends - lengths_row
    indices = jnp.arange(total, dtype=jnp.int32)
    segment = jnp.sum((indices[:, None] >= req_ends[None, :]).astype(jnp.int32), axis=1)
    onehot = segment[:, None] == jnp.arange(lengths_row.shape[0], dtype=jnp.int32)[None, :]
    offsets = jnp.sum(jnp.where(onehot, req_starts[None, :], 0), axis=1)
    return (segment, indices - offsets)


def head_norm(values, gain):
    mean_sq = jnp.mean(values * values, axis=-1, keepdims=True)
    return values * lax.rsqrt(mean_sq + norm_eps) * gain


def rotate(values, position):
    half_size = values.shape[-1] // 2
    freqs = rope_base ** (-(jnp.arange(half_size, dtype=jnp.float32) * 2.0 / (2 * half_size)))
    angles = position.astype(jnp.float32)[:, None] * freqs[None, :]
    shaped = (values.shape[0],) + (1,) * (values.ndim - 2) + (half_size,)
    cosine = jnp.cos(angles).reshape(shaped)
    sine = jnp.sin(angles).reshape(shaped)
    first_half = values[..., :half_size]
    second_half = values[..., half_size:]
    return jnp.concatenate(
        [first_half * cosine - second_half * sine, second_half * cosine + first_half * sine],
        axis=-1,
    )


def general(
    q_pre,
    gate_pre,
    k_pre,
    v_pre,
    q_gain,
    k_gain,
    lengths,
    q_new,
    gate_new,
    k_new,
    v_new,
    resid,
    w_out,
    norm_gain,
    w_gate,
    w_up,
    w_down,
):
    tok_rows = q_pre.shape[0]
    tp_count = lax.axis_size("tp")
    tp_index = lax.axis_index("tp")
    head_size = q_gain.shape[0]
    query_heads = gate_pre.shape[1]
    kv_heads = k_pre.shape[1] // head_size
    groups_per = query_heads // kv_heads
    kv_local = kv_heads // tp_count
    req_count = lengths.shape[1]
    score_scale = head_size ** (-0.5)
    segment, position = group_layout(lengths[0], tok_rows * tp_count)
    row_offset = tp_index * tok_rows
    seg_local = lax.dynamic_slice_in_dim(segment, row_offset, tok_rows)
    pos_local = lax.dynamic_slice_in_dim(position, row_offset, tok_rows)
    query_index = row_offset + jnp.arange(tok_rows, dtype=jnp.int32)
    queries = rotate(
        head_norm(q_pre.reshape(tok_rows, query_heads, head_size).astype(jnp.float32), q_gain),
        pos_local,
    )
    queries = queries.astype(jnp.bfloat16).reshape(tok_rows, kv_heads, groups_per, head_size)
    keys = rotate(
        head_norm(k_pre.reshape(tok_rows, kv_heads, head_size).astype(jnp.float32), k_gain),
        pos_local,
    ).astype(jnp.bfloat16)
    values = v_pre.reshape(tok_rows, kv_heads, head_size)

    def key_block(running, key_piece, value_piece, first_row):
        key_count = key_piece.shape[0]
        key_index = first_row + jnp.arange(key_count, dtype=jnp.int32)
        allowed = (seg_local[:, None] == segment[None, :]) & (
            query_index[:, None] >= key_index[None, :]
        )
        scores = (
            jnp.einsum(
                "qkgd,pkd->qkgp",
                queries,
                key_piece.reshape(key_count, kv_heads, head_size),
                preferred_element_type=jnp.float32,
            )
            * score_scale
        )
        weights = jnp.where(allowed[:, None, None, :], jnp.exp(scores), 0.0)
        totals = running[0] + jnp.sum(weights, axis=-1)
        mixed = running[1] + jnp.einsum(
            "qkgp,pkd->qkgd",
            weights.astype(jnp.bfloat16),
            value_piece.reshape(key_count, kv_heads, head_size),
            preferred_element_type=jnp.float32,
        )
        return (totals, mixed)

    start_state = (
        jnp.zeros((tok_rows, kv_heads, groups_per), jnp.float32),
        jnp.zeros((tok_rows, kv_heads, groups_per, head_size), jnp.float32),
    )
    pieces = (
        lax.all_gather(keys.reshape(tok_rows, kv_heads * head_size), "tp", axis=0, tiled=True),
        lax.all_gather(v_pre, "tp", axis=0, tiled=True),
    )
    key_count = pieces[0].shape[0]
    block_rows = 512

    def one_block(number, carried):
        begin_at = number * block_rows
        return key_block(carried, pieces[0], pieces[1], begin_at)

    totals, mixed = lax.fori_loop(0, key_count // block_rows, one_block, start_state)
    gates = jax.nn.sigmoid(gate_pre.astype(jnp.float32)).reshape(tok_rows, kv_heads, groups_per)
    prefill_out = (
        (mixed / totals[..., None] * gates[..., None])
        .astype(jnp.bfloat16)
        .reshape(tok_rows, query_heads * head_size)
    )
    new_queries = rotate(
        head_norm(q_new.reshape(req_count, query_heads, head_size).astype(jnp.float32), q_gain),
        lengths[0],
    )
    new_queries = new_queries.astype(jnp.bfloat16).reshape(
        req_count, kv_heads, groups_per, head_size
    )
    new_keys = rotate(
        head_norm(k_new.reshape(req_count, kv_heads, head_size).astype(jnp.float32), k_gain),
        lengths[0],
    ).astype(jnp.bfloat16)
    new_values = v_new.reshape(req_count, kv_heads, head_size)
    new_gates = jax.nn.sigmoid(gate_new.astype(jnp.float32)).reshape(
        req_count, kv_heads, groups_per
    )
    head_first = tp_index * kv_local
    request_ids = jnp.arange(req_count, dtype=jnp.int32)
    own_queries = lax.dynamic_slice_in_dim(new_queries, head_first, kv_local, 1)
    cache_keys, cache_values = (
        lax.all_to_all(keys, "tp", split_axis=1, concat_axis=0, tiled=True),
        lax.all_to_all(values, "tp", split_axis=1, concat_axis=0, tiled=True),
    )
    scores = (
        jnp.einsum("rkgd,pkd->rkgp", own_queries, cache_keys, preferred_element_type=jnp.float32)
        * score_scale
    )
    owned = segment[None, :] == request_ids[:, None]
    weights = jnp.where(owned[:, None, None, :], jnp.exp(scores), 0.0)
    weighted = jnp.einsum(
        "rkgp,pkd->rkgd",
        weights.astype(jnp.bfloat16),
        cache_values,
        preferred_element_type=jnp.float32,
    )
    dec_totals = jnp.sum(weights, axis=-1)
    dec_mixed = weighted
    own_keys = lax.dynamic_slice_in_dim(new_keys, head_first, kv_local, 1)
    own_values = lax.dynamic_slice_in_dim(new_values, head_first, kv_local, 1)
    own_gates = lax.dynamic_slice_in_dim(new_gates, head_first, kv_local, 1)
    self_weight = jnp.exp(
        jnp.einsum("rkgd,rkd->rkg", own_queries, own_keys, preferred_element_type=jnp.float32)
        * score_scale
    )
    dec_totals = dec_totals + self_weight
    dec_mixed = dec_mixed + self_weight[..., None] * own_values.astype(jnp.float32)[:, :, None, :]
    attended = (
        (dec_mixed / dec_totals[..., None] * own_gates[..., None])
        .astype(jnp.bfloat16)
        .reshape(req_count, kv_local * groups_per * head_size)
    )
    partial_out = jnp.dot(attended, w_out, preferred_element_type=jnp.float32)
    attn_rows = lax.psum(partial_out, "tp")
    hidden_state = resid.astype(jnp.float32) + attn_rows
    mean_sq = jnp.mean(hidden_state * hidden_state, axis=-1, keepdims=True)
    normed = (hidden_state * lax.rsqrt(mean_sq + norm_eps) * norm_gain).astype(jnp.bfloat16)
    units_local = w_gate.shape[1]
    paired = jnp.concatenate([w_gate, w_up], axis=1)
    columns = lax.all_to_all(normed, "req", split_axis=1, concat_axis=0, tiled=True)
    whole_sums = lax.psum(jnp.dot(columns, paired, preferred_element_type=jnp.float32), "req")
    hidden_units = (jax.nn.silu(whole_sums[:, :units_local]) * whole_sums[:, units_local:]).astype(
        jnp.bfloat16
    )
    down_part = jnp.dot(hidden_units, w_down, preferred_element_type=jnp.float32)
    back_part = lax.all_to_all(down_part, "req", split_axis=0, concat_axis=1, tiled=True)
    mlp_rows = lax.psum(back_part, "tp")
    decode_out = (hidden_state + mlp_rows).astype(jnp.bfloat16)
    return (prefill_out, decode_out)


f32 = jnp.float32
bf16 = jnp.bfloat16
lanes = 128
pay_rows = 32
back_rows = 16


def dot(a, b):
    return jnp.dot(a, b, preferred_element_type=f32)


def dot_nt(a, b):
    return lax.dot_general(a, b, (((1,), (1,)), ((), ())), preferred_element_type=f32)


def iota(shape, dim):
    return lax.broadcasted_iota(jnp.int32, shape, dim)


def rope_factors(angles):
    turns = jnp.floor(angles * (2.0 / np.pi) + 0.5)
    rest = angles - turns * 1.5703125
    rest = rest - turns * 4.837512969970703125e-4
    rest = rest - turns * 7.549789948768648e-8
    sq = rest * rest
    sine = ((-1.9515295891e-4 * sq + 8.3321608736e-3) * sq - 1.6666654611e-1) * sq * rest + rest
    cosine = (
        ((2.443315711809948e-5 * sq - 1.388731625493765e-3) * sq + 4.166664568298827e-2) * sq * sq
        - 0.5 * sq
        + 1.0
    )
    low = iota(angles.shape, 1) < lanes // 2
    quarter = turns.astype(jnp.int32) + jnp.where(low, 1, 0)
    both = jnp.where((quarter & 1) == 1, cosine, sine)
    both = jnp.where((quarter & 2) == 2, -both, both)
    swapped = pltpu.roll(both, lanes // 2, 1)
    return jnp.where(low, both, swapped), jnp.where(low, -swapped, both)


def norm_rope(values, gain, factors):
    mean_sq = jnp.mean(values * values, axis=-1, keepdims=True)
    normed = values * lax.rsqrt(mean_sq + norm_eps) * gain
    return (normed * factors[0] + pltpu.roll(normed, lanes // 2, 1) * factors[1]).astype(bf16)


def begin_of(indices, len_ref):
    begin = jnp.zeros_like(indices)
    end = 0
    for j in range(len_ref.shape[1] - 1):
        end = end + len_ref[0, j]
        begin = jnp.where(indices >= end, end, begin)
    return begin


def partial_kernel(
    len_hbm, k_hbm, v_hbm, qn_hbm, kn_hbm, vn_hbm, gn_hbm, resid_hbm, qg_hbm, kg_hbm, freq_hbm,
    w_hbm, gate_hbm, up_hbm, down_hbm,
    kv_ref, pay_ref, own_ref, pair_ref, down_pair_ref, row_q, row_k, row_v, row_g, pay, len_ref, k_ref, v_ref, qn_ref, kn_ref, vn_ref, gn_ref,
    resid_ref, qg_ref, kg_ref, freq_ref, sems,
):
    tp = lax.axis_index("tp")
    req = lax.axis_index("req")
    z, other = lax.div(req, 2), 1 - lax.rem(req, 2)
    width = own_ref.shape[1]
    units = down_pair_ref.shape[0]
    cols = pl.ds(pl.multiple_of(z * width, lanes), width)
    theirs = pl.ds(pl.multiple_of(other * units, lanes), units)
    moves = (
        (len_hbm, len_ref), (freq_hbm, freq_ref), (k_hbm, k_ref), (kg_hbm, kg_ref),
        (qn_hbm, qn_ref), (kn_hbm, kn_ref), (vn_hbm, vn_ref), (gn_hbm, gn_ref), (qg_hbm, qg_ref),
        (v_hbm, v_ref), (resid_hbm, resid_ref),
        (gate_hbm.at[:, theirs], pair_ref.at[:, pl.ds(0, units)]),
        (up_hbm.at[:, theirs], pair_ref.at[:, pl.ds(units, units)]),
        (w_hbm.at[:, cols], own_ref),
        (down_hbm.at[theirs, :], down_pair_ref),
    )
    copies = [pltpu.make_async_copy(a, b, sems.at[i]) for i, (a, b) in enumerate(moves)]
    for copy in copies:
        copy.start()
    tok = k_ref.shape[0]
    rpg = qn_ref.shape[0]
    heads = qn_ref.shape[1] // lanes
    kvs = k_ref.shape[1] // lanes
    per = heads // kvs
    rows = heads * rpg
    for copy in copies[:2]:
        copy.wait()
    freq = freq_ref[...]
    tok_index = tp * tok + iota((tok, lanes), 0)
    factors = rope_factors((tok_index - begin_of(tok_index, len_ref)).astype(f32) * freq)
    for copy in copies[2:11]:
        copy.wait()
    qg, kg = qg_ref[...], kg_ref[...]
    keys = []
    for k in range(kvs):
        at = slice(k * lanes, (k + 1) * lanes)
        keys.append(norm_rope(k_ref[:, at].astype(f32), kg, factors))
        kv_ref[:, at] = keys[-1]
    kv_ref[:, kvs * lanes :] = v_ref[...]
    qn, kn = qn_ref[...].astype(f32), kn_ref[...].astype(f32)
    vn, gn = vn_ref[...].astype(f32), gn_ref[...].astype(f32)
    for h in range(heads):
        at = slice(h * rpg, (h + 1) * rpg)
        kv = slice((h // per) * lanes, (h // per + 1) * lanes)
        row_q[at, :] = qn[:, h * lanes : (h + 1) * lanes]
        row_k[at, :] = kn[:, kv]
        row_v[at, :] = vn[:, kv]
        row_g[at, :] = jnp.broadcast_to(gn[:, h : h + 1], (rpg, lanes))
    row = iota((rows, lanes), 0)
    col = iota((rows, lanes), 1)
    head = row * 0
    for h in range(1, heads):
        head = jnp.where(row >= h * rpg, h, head)
    request = row - head * rpg
    length, first, last = row * 0, row * 0, row * 0
    end = 0
    for j in range(rpg):
        mine = request == j
        length = jnp.where(mine, len_ref[0, j], length)
        first = jnp.where(mine, end, first)
        end = end + len_ref[0, j]
        last = jnp.where(mine, end, last)
    new_factors = rope_factors(length.astype(f32) * freq)
    scale = lanes ** (-0.5)
    new_q = norm_rope(row_q[...], qg, new_factors)
    new_k = norm_rope(row_k[...], kg, new_factors)
    scores = jnp.zeros((rows, tok), f32)
    for k in range(kvs):
        mine = (head >= k * per) & (head < (k + 1) * per)
        scores = jnp.where(mine, dot_nt(new_q, keys[k]), scores)
    index = tp * tok + col
    weights = jnp.where((index >= first) & (index < last), jnp.exp(scores * scale), 0.0)
    totals = jnp.sum(weights, axis=-1, keepdims=True)
    rounded = weights.astype(bf16)
    mixed = jnp.zeros((rows, lanes), f32)
    for k in range(kvs):
        mine = (head >= k * per) & (head < (k + 1) * per)
        mixed = mixed + dot(
            jnp.where(mine, rounded, jnp.zeros_like(rounded)), v_ref[:, k * lanes : (k + 1) * lanes]
        )
    self_score = jnp.sum(new_q.astype(f32) * new_k.astype(f32), axis=-1, keepdims=True)
    self_weight = jnp.where(tp == 0, jnp.exp(self_score * scale), 0.0)
    totals = totals + self_weight
    mixed = (mixed + self_weight * row_v[...]) * jax.nn.sigmoid(row_g[...])
    total_row = jnp.sum(jnp.where(row == col, totals, 0.0), axis=0, keepdims=True)
    high = total_row.astype(bf16).astype(f32)
    pay[...] = jnp.zeros_like(pay)
    pay[0:rows, :] = mixed
    pay[rows + rpg : rows + rpg + 1, :] = high
    pay[rows + rpg + 1 : rows + rpg + 2, :] = total_row - high
    peers = pay_ref.shape[0]
    tps = lax.axis_size("tp")
    slices = resid_ref.shape[1] // (tps * lanes)
    for z in range(slices):
        at = pl.ds(pl.multiple_of((z * tps + tp) * lanes, lanes), lanes)
        pay[rows : rows + rpg, :] = resid_ref[:, at].astype(f32)
        out = pay[...].astype(bf16)
        for peer in range(z * peers // slices, (z + 1) * peers // slices):
            pay_ref[peer] = out
    for copy in copies[11:]:
        copy.wait()


def ready_kernel(*refs):
    refs[-1][...] = jnp.zeros_like(refs[-1])


def hidden_kernel(
    pay_ref, w0_ref, w1_ref, w2_ref, w3_ref, gate_ref, up_ref, pair_ref, ng_ref, _,
    hid_ref, msg_ref, att, hid, xs, acc,
):
    tp = lax.axis_index("tp")
    req = lax.axis_index("req")
    tps = lax.axis_size("tp")
    z, y = lax.div(req, 2), lax.rem(req, 2)
    heads, toks, _ = att.shape
    groups = pay_ref.shape[0] // tps
    rpg = toks // groups
    rows = heads * rpg
    diag = iota((rows, lanes), 0) == iota((rows, lanes), 1)
    for r in range(groups):
        total = jnp.zeros(acc.shape, f32)
        for t in range(tps):
            piece = pay_ref[r * tps + t].astype(f32)
            total = total + piece
            acc[...] = piece
            hid[r * rpg : (r + 1) * rpg, t * lanes : (t + 1) * lanes] = acc[rows : rows + rpg, :]
        acc[...] = total
        total_row = acc[rows + rpg : rows + rpg + 1, :] + acc[rows + rpg + 1 : rows + rpg + 2, :]
        totals = jnp.sum(
            jnp.where(diag, jnp.broadcast_to(total_row, (rows, lanes)), 0.0), axis=-1, keepdims=True
        )
        acc[0:rows, :] = acc[0:rows, :] / totals
        for h in range(heads):
            att[h, r * rpg : (r + 1) * rpg, :] = acc[h * rpg : (h + 1) * rpg, :]
    state = hid[...]
    per = heads // tps
    for d, w_ref in enumerate((w0_ref, w1_ref, w2_ref, w3_ref)):
        source = tp ^ d
        for j in range(per):
            state = state + dot(
                att[source * per + j].astype(bf16), w_ref[j * lanes : (j + 1) * lanes, :]
            )
    hid_ref[...] = state
    width = state.shape[1]
    half = width // 2
    sums = jnp.sum(state * state, axis=-1, keepdims=True)
    scaled = state * ng_ref[:, pl.ds(pl.multiple_of(z * width, lanes), width)]
    xs[0] = scaled[:, :half]
    xs[1] = scaled[:, half:]
    own, other = xs[y].astype(bf16), xs[1 - y].astype(bf16)
    units = pair_ref.shape[1] // 2
    at = pl.ds(pl.multiple_of(y * units, lanes), units)
    gate = dot(own, gate_ref[:, at]) + dot(other, pair_ref[:, :units])
    up = dot(own, up_ref[:, at]) + dot(other, pair_ref[:, units:])
    high = sums.astype(bf16).astype(f32)
    lane = iota((toks, lanes), 1)
    msg_ref[:, :units] = gate.astype(bf16)
    msg_ref[:, units : 2 * units] = up.astype(bf16)
    msg_ref[:, 2 * units :] = jnp.where(
        lane == 0, high, jnp.where(lane == 1, sums - high, 0.0)
    ).astype(bf16)


def down_kernel(m0_ref, m1_ref, m2_ref, m3_ref, hid_ref, down_ref, pair_ref, back_ref, part, pay):
    tp = lax.axis_index("tp")
    tps = lax.axis_size("tp")
    y = lax.rem(lax.axis_index("req"), 2)
    units, half = pair_ref.shape
    toks, width = hid_ref.shape
    total = m0_ref[...].astype(f32)
    for m_ref in (m1_ref, m2_ref, m3_ref):
        total = total + m_ref[...].astype(f32)
    sums = total[:, 2 * units : 2 * units + 1] + total[:, 2 * units + 1 : 2 * units + 2]
    factor = lax.rsqrt(sums / (width * 4) + norm_eps)
    gate = total[:, :units] * factor
    hidden = (gate / (1.0 + jnp.exp(-gate)) * (total[:, units : 2 * units] * factor)).astype(bf16)
    own_rows = pl.ds(pl.multiple_of(y * units, lanes), units)
    part[y] = dot(hidden, down_ref[own_rows, :])
    part[1 - y] = dot(hidden, pair_ref[...])
    chunks = width // lanes
    groups = pay.shape[0]
    rpg = toks // groups
    piece = hid_ref[:, pl.ds(pl.multiple_of(tp * lanes, lanes), lanes)]
    high = piece.astype(bf16).astype(f32)
    piece = jnp.where(y == 0, high, piece - high)
    pay[...] = jnp.zeros_like(pay)
    for c in range(chunks + 1):
        if c < chunks:
            at = (c * lanes) % half
            block = part[c * lanes // half][:, at : at + lanes]
        else:
            block = piece
        for r in range(groups):
            pay[r, c * rpg : (c + 1) * rpg, :] = block[r * rpg : (r + 1) * rpg, :]
    for r in range(groups):
        out = pay[r].astype(bf16)
        for t in range(tps):
            back_ref[r * tps + t] = out


def final_kernel(back_ref, out_ref, acc, tail, rows_out):
    tps = lax.axis_size("tp")
    peers = back_ref.shape[0]
    rpg, width = out_ref.shape
    chunks = tps
    slices = width // (chunks * lanes)
    group = peers // slices
    for z in range(slices):
        total = jnp.zeros(acc.shape, f32)
        by_tp = [jnp.zeros(acc.shape, f32) for _ in range(tps)]
        for p in range(group):
            piece = back_ref[z * group + p].astype(f32)
            total = total + piece
            by_tp[p % tps] = by_tp[p % tps] + piece
        acc[...] = total
        for c in range(chunks):
            tail[...] = by_tp[c]
            at = slice((z * chunks + c) * lanes, (z * chunks + c + 1) * lanes)
            rows_out[0:rpg, at] = (
                acc[c * rpg : (c + 1) * rpg, :] + tail[chunks * rpg : (chunks + 1) * rpg, :]
            )
    out_ref[...] = rows_out[0:rpg, :].astype(bf16)


def prefill_kernel(
    len_ref, q_ref, g_ref, kv0_ref, kv1_ref, kv2_ref, kv3_ref, qg_ref, freq_ref, out_ref, mid_ref
):
    tp = lax.axis_index("tp")
    tok = q_ref.shape[0]
    heads = q_ref.shape[1] // lanes
    kvs = kv0_ref.shape[1] // (2 * lanes)
    per = heads // kvs
    third = tp == 2
    mid_ref[...] = jnp.where(third, kv3_ref[...], kv1_ref[...])
    blocks = ((tp, kv0_ref), (jnp.where(third, tp ^ 3, tp ^ 1), mid_ref), (tp ^ 2, kv2_ref))
    tok_index = tp * tok + iota((tok, lanes), 0)
    begin = begin_of(tok_index, len_ref)
    factors = rope_factors((tok_index - begin).astype(f32) * freq_ref[...])
    col = iota((tok, tok), 1)
    allowed = []
    for block, _ in blocks:
        key_index = block * tok + col
        allowed.append((key_index >= begin) & (key_index <= tok_index))
    gates = jax.nn.sigmoid(g_ref[...].astype(f32))
    qg = qg_ref[...]
    scale = lanes ** (-0.5)
    for h in range(heads):
        k = h // per
        at = slice(h * lanes, (h + 1) * lanes)
        query = norm_rope(q_ref[:, at].astype(f32), qg, factors)
        totals = jnp.zeros((tok, 1), f32)
        mixed = jnp.zeros((tok, lanes), f32)
        for b, (_, kv_ref) in enumerate(blocks):
            scores = dot_nt(query, kv_ref[:, k * lanes : (k + 1) * lanes])
            weights = jnp.where(allowed[b], jnp.exp(scores * scale), 0.0)
            totals = totals + jnp.sum(weights, axis=-1, keepdims=True)
            mixed = mixed + dot(
                weights.astype(bf16), kv_ref[:, (kvs + k) * lanes : (kvs + k + 1) * lanes]
            )
        out_ref[:, at] = (mixed / totals * gates[:, h : h + 1]).astype(bf16)


def call(body, out_shape, args, scratch=(), hbm=False, smem=0, flops=0, limit=12, **more):
    specs = [pl.BlockSpec(memory_space=pltpu.SMEM)] * smem
    space = pltpu.HBM if hbm else pltpu.VMEM
    specs += [pl.BlockSpec(memory_space=space)] * (len(args) - smem)
    size = sum(a.size * a.dtype.itemsize for a in args)
    return pl.pallas_call(
        body,
        out_shape=out_shape,
        in_specs=specs,
        out_specs=jax.tree.map(lambda _: pl.BlockSpec(memory_space=pltpu.VMEM), out_shape),
        scratch_shapes=[pltpu.VMEM(s, f32) if isinstance(s, tuple) else s for s in scratch],
        compiler_params=pltpu.CompilerParams(vmem_limit_bytes=limit * 2**20),
        cost_estimate=pl.CostEstimate(flops=flops, bytes_accessed=size, transcendentals=0),
    )(*args)


def hold(arrays, flops):
    return pl.pallas_call(
        ready_kernel,
        out_shape=jax.ShapeDtypeStruct((8, lanes), f32),
        in_specs=[pl.BlockSpec(memory_space=pl.ANY)] * len(arrays),
        out_specs=pl.BlockSpec(memory_space=pltpu.VMEM),
        compiler_params=pltpu.CompilerParams(vmem_limit_bytes=2**20),
        cost_estimate=pl.CostEstimate(flops=flops, bytes_accessed=0, transcendentals=0),
    )(*arrays)


def local(
    q_pre,
    gate_pre,
    k_pre,
    v_pre,
    q_gain,
    k_gain,
    lengths,
    q_new,
    gate_new,
    k_new,
    v_new,
    resid,
    w_out,
    norm_gain,
    w_gate,
    w_up,
    w_down,
):
    tps, reqs = lax.axis_size("tp"), lax.axis_size("req")
    tok = q_pre.shape[0]
    rpg, width = resid.shape
    slices = reqs // 2
    head_size = q_gain.shape[0]
    heads = gate_pre.shape[1]
    part = width // slices if slices else 0
    if not (slices == 4 and tps == 4 and head_size == lanes == tok and part == tps * lanes):
        return general(
            q_pre, gate_pre, k_pre, v_pre, q_gain, k_gain, lengths, q_new, gate_new, k_new, v_new,
            resid, w_out, norm_gain, w_gate, w_up, w_down,
        )
    peers = tps * reqs
    toks = rpg * reqs
    units = w_gate.shape[1] // 2
    req = lax.axis_index("req")
    z, y = req // 2, req % 2
    freqs = rope_base ** (-(np.arange(head_size // 2) * 2.0 / head_size))
    freqs = jnp.asarray(np.concatenate([freqs, freqs])[None, :], f32)
    qg, kg = q_gain[None, :], k_gain[None, :]

    def cross(array, by):
        return lax.ppermute(array, "tp", [(i, i ^ by) for i in range(tps)])

    def swap(array):
        return lax.ppermute(array, "req", [(i, i ^ 1) for i in range(reqs)])

    def along(array, by):
        return lax.ppermute(array, "req", [(i, (i + 2 * by) % reqs) for i in range(reqs)])

    inputs = (
        lengths, k_pre, v_pre, q_new, k_new, v_new, gate_new, resid, qg, kg, freqs,
        w_out, w_gate, w_up, w_down,
    )
    kv, pay, w_own, pair, down_pair = call(
        partial_kernel,
        (
            jax.ShapeDtypeStruct((tok, 2 * k_pre.shape[1]), bf16),
            jax.ShapeDtypeStruct((peers, pay_rows, lanes), bf16),
            jax.ShapeDtypeStruct((w_out.shape[0], part), bf16),
            jax.ShapeDtypeStruct((w_gate.shape[0], 2 * units), bf16),
            jax.ShapeDtypeStruct((units, w_down.shape[1]), bf16),
        ),
        inputs,
        scratch=[(heads * rpg, lanes)] * 4
        + [(pay_rows, lanes), pltpu.SMEM(lengths.shape, jnp.int32)]
        + [pltpu.VMEM(a.shape, a.dtype) for a in inputs[1:11]]
        + [pltpu.SemaphoreType.DMA((len(inputs),))],
        hbm=True,
        flops=10**7,
        limit=56,
    )
    w_far = cross(w_own, 2)
    pair = swap(pair)
    w_near, w_both = cross(w_own, 1), cross(w_far, 1)
    late_kv, _ = lax.optimization_barrier((kv, w_far))
    kv_far, kv_near = cross(late_kv, 2), cross(kv, 1)
    late_down, _ = lax.optimization_barrier((down_pair, pair))
    down_pair = swap(late_down)
    got = lax.all_to_all(pay, ("req", "tp"), 0, 0, tiled=True)
    token = hold((pair, w_near, w_both, kv_near), 2 * 10**9)
    hid, msg = call(
        hidden_kernel,
        (
            jax.ShapeDtypeStruct((toks, part), f32),
            jax.ShapeDtypeStruct((toks, 2 * units + lanes), bf16),
        ),
        (got, w_own, w_near, w_far, w_both, w_gate, w_up, pair, norm_gain[None, :], token),
        scratch=[
            (heads, toks, lanes),
            (toks, part),
            (2, toks, part // 2),
            (pay_rows, lanes),
        ],
        flops=10**7,
    )
    msgs = [msg] + [along(msg, d) for d in range(1, slices)]
    kv_far, *_ = lax.optimization_barrier((kv_far, *msgs[1:]))
    kv_both = cross(kv_far, 1)
    prefill_out = call(
        prefill_kernel,
        jax.ShapeDtypeStruct(q_pre.shape, bf16),
        (lengths, q_pre, gate_pre, kv, kv_near, kv_far, kv_both, qg, freqs),
        scratch=[pltpu.VMEM(kv.shape, bf16)],
        smem=1,
        flops=10**9,
    )
    back = call(
        down_kernel,
        jax.ShapeDtypeStruct((peers, back_rows, lanes), bf16),
        (*msgs, hid, w_down, down_pair),
        scratch=[(2, toks, part // 2), (reqs, back_rows, lanes)],
        flops=10**7,
    )
    returned = lax.all_to_all(back, ("req", "tp"), 0, 0, tiled=True)
    returned, prefill_out = lax.optimization_barrier((returned, prefill_out))
    decode_out = call(
        final_kernel,
        jax.ShapeDtypeStruct((rpg, width), bf16),
        (returned,),
        scratch=[(back_rows, lanes), (back_rows, lanes), (8, width)],
        flops=10**6,
    )
    return (prefill_out, decode_out)


def solution(mesh):
    return jax.shard_map(
        local,
        mesh=mesh,
        in_specs=(
            P(("req", "tp"), None),
            P(("req", "tp"), None),
            P(("req", "tp"), None),
            P(("req", "tp"), None),
            P(),
            P(),
            P("req", None),
            P("req", None),
            P("req", None),
            P("req", None),
            P("req", None),
            P("req", None),
            P("tp", None),
            P(),
            P("req", "tp"),
            P("req", "tp"),
            P("tp", "req"),
        ),
        out_specs=(P(("req", "tp"), None), P("req", None)),
        check_vma=False,
    )
```

```python
import jax
import jax.numpy as jnp
import numpy as np
from jax import lax
from jax.experimental import pallas as pl
from jax.experimental.pallas import tpu as pltpu
from jax.sharding import PartitionSpec as P

rope_base = 1000000.0
norm_eps = 1e-06


def group_layout(lengths_row, total):
    req_ends = jnp.cumsum(lengths_row)
    req_starts = req_ends - lengths_row
    indices = jnp.arange(total, dtype=jnp.int32)
    segment = jnp.sum((indices[:, None] >= req_ends[None, :]).astype(jnp.int32), axis=1)
    onehot = segment[:, None] == jnp.arange(lengths_row.shape[0], dtype=jnp.int32)[None, :]
    offsets = jnp.sum(jnp.where(onehot, req_starts[None, :], 0), axis=1)
    return (segment, indices - offsets)


def head_norm(values, gain):
    mean_sq = jnp.mean(values * values, axis=-1, keepdims=True)
    return values * lax.rsqrt(mean_sq + norm_eps) * gain


def rotate(values, position):
    half_size = values.shape[-1] // 2
    freqs = rope_base ** (-(jnp.arange(half_size, dtype=jnp.float32) * 2.0 / (2 * half_size)))
    angles = position.astype(jnp.float32)[:, None] * freqs[None, :]
    shaped = (values.shape[0],) + (1,) * (values.ndim - 2) + (half_size,)
    cosine = jnp.cos(angles).reshape(shaped)
    sine = jnp.sin(angles).reshape(shaped)
    first_half = values[..., :half_size]
    second_half = values[..., half_size:]
    return jnp.concatenate(
        [first_half * cosine - second_half * sine, second_half * cosine + first_half * sine],
        axis=-1,
    )


def general(
    q_pre,
    gate_pre,
    k_pre,
    v_pre,
    q_gain,
    k_gain,
    lengths,
    q_new,
    gate_new,
    k_new,
    v_new,
    resid,
    w_out,
    norm_gain,
    w_gate,
    w_up,
    w_down,
):
    tok_rows = q_pre.shape[0]
    tp_count = lax.axis_size("tp")
    tp_index = lax.axis_index("tp")
    head_size = q_gain.shape[0]
    query_heads = gate_pre.shape[1]
    kv_heads = k_pre.shape[1] // head_size
    groups_per = query_heads // kv_heads
    kv_local = kv_heads // tp_count
    req_count = lengths.shape[1]
    score_scale = head_size ** (-0.5)
    segment, position = group_layout(lengths[0], tok_rows * tp_count)
    row_offset = tp_index * tok_rows
    seg_local = lax.dynamic_slice_in_dim(segment, row_offset, tok_rows)
    pos_local = lax.dynamic_slice_in_dim(position, row_offset, tok_rows)
    query_index = row_offset + jnp.arange(tok_rows, dtype=jnp.int32)
    queries = rotate(
        head_norm(q_pre.reshape(tok_rows, query_heads, head_size).astype(jnp.float32), q_gain),
        pos_local,
    )
    queries = queries.astype(jnp.bfloat16).reshape(tok_rows, kv_heads, groups_per, head_size)
    keys = rotate(
        head_norm(k_pre.reshape(tok_rows, kv_heads, head_size).astype(jnp.float32), k_gain),
        pos_local,
    ).astype(jnp.bfloat16)
    values = v_pre.reshape(tok_rows, kv_heads, head_size)

    def key_block(running, key_piece, value_piece, first_row):
        key_count = key_piece.shape[0]
        key_index = first_row + jnp.arange(key_count, dtype=jnp.int32)
        allowed = (seg_local[:, None] == segment[None, :]) & (
            query_index[:, None] >= key_index[None, :]
        )
        scores = (
            jnp.einsum(
                "qkgd,pkd->qkgp",
                queries,
                key_piece.reshape(key_count, kv_heads, head_size),
                preferred_element_type=jnp.float32,
            )
            * score_scale
        )
        weights = jnp.where(allowed[:, None, None, :], jnp.exp(scores), 0.0)
        totals = running[0] + jnp.sum(weights, axis=-1)
        mixed = running[1] + jnp.einsum(
            "qkgp,pkd->qkgd",
            weights.astype(jnp.bfloat16),
            value_piece.reshape(key_count, kv_heads, head_size),
            preferred_element_type=jnp.float32,
        )
        return (totals, mixed)

    start_state = (
        jnp.zeros((tok_rows, kv_heads, groups_per), jnp.float32),
        jnp.zeros((tok_rows, kv_heads, groups_per, head_size), jnp.float32),
    )
    pieces = (
        lax.all_gather(keys.reshape(tok_rows, kv_heads * head_size), "tp", axis=0, tiled=True),
        lax.all_gather(v_pre, "tp", axis=0, tiled=True),
    )
    key_count = pieces[0].shape[0]
    block_rows = 512

    def one_block(number, carried):
        begin_at = number * block_rows
        return key_block(carried, pieces[0], pieces[1], begin_at)

    totals, mixed = lax.fori_loop(0, key_count // block_rows, one_block, start_state)
    gates = jax.nn.sigmoid(gate_pre.astype(jnp.float32)).reshape(tok_rows, kv_heads, groups_per)
    prefill_out = (
        (mixed / totals[..., None] * gates[..., None])
        .astype(jnp.bfloat16)
        .reshape(tok_rows, query_heads * head_size)
    )
    new_queries = rotate(
        head_norm(q_new.reshape(req_count, query_heads, head_size).astype(jnp.float32), q_gain),
        lengths[0],
    )
    new_queries = new_queries.astype(jnp.bfloat16).reshape(
        req_count, kv_heads, groups_per, head_size
    )
    new_keys = rotate(
        head_norm(k_new.reshape(req_count, kv_heads, head_size).astype(jnp.float32), k_gain),
        lengths[0],
    ).astype(jnp.bfloat16)
    new_values = v_new.reshape(req_count, kv_heads, head_size)
    new_gates = jax.nn.sigmoid(gate_new.astype(jnp.float32)).reshape(
        req_count, kv_heads, groups_per
    )
    head_first = tp_index * kv_local
    request_ids = jnp.arange(req_count, dtype=jnp.int32)
    own_queries = lax.dynamic_slice_in_dim(new_queries, head_first, kv_local, 1)
    cache_keys, cache_values = (
        lax.all_to_all(keys, "tp", split_axis=1, concat_axis=0, tiled=True),
        lax.all_to_all(values, "tp", split_axis=1, concat_axis=0, tiled=True),
    )
    scores = (
        jnp.einsum("rkgd,pkd->rkgp", own_queries, cache_keys, preferred_element_type=jnp.float32)
        * score_scale
    )
    owned = segment[None, :] == request_ids[:, None]
    weights = jnp.where(owned[:, None, None, :], jnp.exp(scores), 0.0)
    weighted = jnp.einsum(
        "rkgp,pkd->rkgd",
        weights.astype(jnp.bfloat16),
        cache_values,
        preferred_element_type=jnp.float32,
    )
    dec_totals = jnp.sum(weights, axis=-1)
    dec_mixed = weighted
    own_keys = lax.dynamic_slice_in_dim(new_keys, head_first, kv_local, 1)
    own_values = lax.dynamic_slice_in_dim(new_values, head_first, kv_local, 1)
    own_gates = lax.dynamic_slice_in_dim(new_gates, head_first, kv_local, 1)
    self_weight = jnp.exp(
        jnp.einsum("rkgd,rkd->rkg", own_queries, own_keys, preferred_element_type=jnp.float32)
        * score_scale
    )
    dec_totals = dec_totals + self_weight
    dec_mixed = dec_mixed + self_weight[..., None] * own_values.astype(jnp.float32)[:, :, None, :]
    attended = (
        (dec_mixed / dec_totals[..., None] * own_gates[..., None])
        .astype(jnp.bfloat16)
        .reshape(req_count, kv_local * groups_per * head_size)
    )
    partial_out = jnp.dot(attended, w_out, preferred_element_type=jnp.float32)
    attn_rows = lax.psum(partial_out, "tp")
    hidden_state = resid.astype(jnp.float32) + attn_rows
    mean_sq = jnp.mean(hidden_state * hidden_state, axis=-1, keepdims=True)
    normed = (hidden_state * lax.rsqrt(mean_sq + norm_eps) * norm_gain).astype(jnp.bfloat16)
    units_local = w_gate.shape[1]
    paired = jnp.concatenate([w_gate, w_up], axis=1)
    columns = lax.all_to_all(normed, "req", split_axis=1, concat_axis=0, tiled=True)
    whole_sums = lax.psum(jnp.dot(columns, paired, preferred_element_type=jnp.float32), "req")
    hidden_units = (jax.nn.silu(whole_sums[:, :units_local]) * whole_sums[:, units_local:]).astype(
        jnp.bfloat16
    )
    down_part = jnp.dot(hidden_units, w_down, preferred_element_type=jnp.float32)
    back_part = lax.all_to_all(down_part, "req", split_axis=0, concat_axis=1, tiled=True)
    mlp_rows = lax.psum(back_part, "tp")
    decode_out = (hidden_state + mlp_rows).astype(jnp.bfloat16)
    return (prefill_out, decode_out)


f32 = jnp.float32
bf16 = jnp.bfloat16
lanes = 128
pay_rows = 32
back_rows = 16


def dot(a, b):
    return jnp.dot(a, b, preferred_element_type=f32)


def dot_nt(a, b):
    return lax.dot_general(a, b, (((1,), (1,)), ((), ())), preferred_element_type=f32)


def iota(shape, dim):
    return lax.broadcasted_iota(jnp.int32, shape, dim)


def rope_factors(angles):
    turns = jnp.floor(angles * (2.0 / np.pi) + 0.5)
    rest = angles - turns * 1.5703125
    rest = rest - turns * 4.837512969970703125e-4
    rest = rest - turns * 7.549789948768648e-8
    sq = rest * rest
    sine = ((-1.9515295891e-4 * sq + 8.3321608736e-3) * sq - 1.6666654611e-1) * sq * rest + rest
    cosine = (
        ((2.443315711809948e-5 * sq - 1.388731625493765e-3) * sq + 4.166664568298827e-2) * sq * sq
        - 0.5 * sq
        + 1.0
    )
    low = iota(angles.shape, 1) < lanes // 2
    quarter = turns.astype(jnp.int32) + jnp.where(low, 1, 0)
    both = jnp.where((quarter & 1) == 1, cosine, sine)
    both = jnp.where((quarter & 2) == 2, -both, both)
    swapped = pltpu.roll(both, lanes // 2, 1)
    return jnp.where(low, both, swapped), jnp.where(low, -swapped, both)


def norm_rope(values, gain, factors):
    mean_sq = jnp.mean(values * values, axis=-1, keepdims=True)
    normed = values * lax.rsqrt(mean_sq + norm_eps) * gain
    return (normed * factors[0] + pltpu.roll(normed, lanes // 2, 1) * factors[1]).astype(bf16)


def begin_of(indices, len_ref):
    begin = jnp.zeros_like(indices)
    end = 0
    for j in range(len_ref.shape[1] - 1):
        end = end + len_ref[0, j]
        begin = jnp.where(indices >= end, end, begin)
    return begin


def partial_kernel(
    len_hbm, k_hbm, v_hbm, qn_hbm, kn_hbm, vn_hbm, gn_hbm, resid_hbm, qg_hbm, kg_hbm, freq_hbm,
    w_hbm, gate_hbm, up_hbm, down_hbm,
    kv_ref, pay_ref, own_ref, pair_ref, down_pair_ref, row_q, row_k, row_v, row_g, pay, len_ref, k_ref, v_ref, qn_ref, kn_ref, vn_ref, gn_ref,
    resid_ref, qg_ref, kg_ref, freq_ref, sems,
):
    tp = lax.axis_index("tp")
    req = lax.axis_index("req")
    z, other = lax.div(req, 2), 1 - lax.rem(req, 2)
    width = own_ref.shape[1]
    units = down_pair_ref.shape[0]
    cols = pl.ds(pl.multiple_of(z * width, lanes), width)
    theirs = pl.ds(pl.multiple_of(other * units, lanes), units)
    moves = (
        (len_hbm, len_ref), (freq_hbm, freq_ref), (k_hbm, k_ref), (kg_hbm, kg_ref),
        (qn_hbm, qn_ref), (kn_hbm, kn_ref), (vn_hbm, vn_ref), (gn_hbm, gn_ref), (qg_hbm, qg_ref),
        (v_hbm, v_ref), (resid_hbm, resid_ref),
        (gate_hbm.at[:, theirs], pair_ref.at[:, pl.ds(0, units)]),
        (up_hbm.at[:, theirs], pair_ref.at[:, pl.ds(units, units)]),
        (w_hbm.at[:, cols], own_ref),
        (down_hbm.at[theirs, :], down_pair_ref),
    )
    copies = [pltpu.make_async_copy(a, b, sems.at[i]) for i, (a, b) in enumerate(moves)]
    for copy in copies:
        copy.start()
    tok = k_ref.shape[0]
    rpg = qn_ref.shape[0]
    heads = qn_ref.shape[1] // lanes
    kvs = k_ref.shape[1] // lanes
    per = heads // kvs
    rows = heads * rpg
    for copy in copies[:2]:
        copy.wait()
    freq = freq_ref[...]
    tok_index = tp * tok + iota((tok, lanes), 0)
    factors = rope_factors((tok_index - begin_of(tok_index, len_ref)).astype(f32) * freq)
    for copy in copies[2:11]:
        copy.wait()
    qg, kg = qg_ref[...], kg_ref[...]
    keys = []
    for k in range(kvs):
        at = slice(k * lanes, (k + 1) * lanes)
        keys.append(norm_rope(k_ref[:, at].astype(f32), kg, factors))
        kv_ref[:, at] = keys[-1]
    kv_ref[:, kvs * lanes :] = v_ref[...]
    qn, kn = qn_ref[...].astype(f32), kn_ref[...].astype(f32)
    vn, gn = vn_ref[...].astype(f32), gn_ref[...].astype(f32)
    for h in range(heads):
        at = slice(h * rpg, (h + 1) * rpg)
        kv = slice((h // per) * lanes, (h // per + 1) * lanes)
        row_q[at, :] = qn[:, h * lanes : (h + 1) * lanes]
        row_k[at, :] = kn[:, kv]
        row_v[at, :] = vn[:, kv]
        row_g[at, :] = jnp.broadcast_to(gn[:, h : h + 1], (rpg, lanes))
    row = iota((rows, lanes), 0)
    col = iota((rows, lanes), 1)
    head = row * 0
    for h in range(1, heads):
        head = jnp.where(row >= h * rpg, h, head)
    request = row - head * rpg
    length, first, last = row * 0, row * 0, row * 0
    end = 0
    for j in range(rpg):
        mine = request == j
        length = jnp.where(mine, len_ref[0, j], length)
        first = jnp.where(mine, end, first)
        end = end + len_ref[0, j]
        last = jnp.where(mine, end, last)
    new_factors = rope_factors(length.astype(f32) * freq)
    scale = lanes ** (-0.5)
    new_q = norm_rope(row_q[...], qg, new_factors)
    new_k = norm_rope(row_k[...], kg, new_factors)
    scores = jnp.zeros((rows, tok), f32)
    for k in range(kvs):
        mine = (head >= k * per) & (head < (k + 1) * per)
        scores = jnp.where(mine, dot_nt(new_q, keys[k]), scores)
    index = tp * tok + col
    weights = jnp.where((index >= first) & (index < last), jnp.exp(scores * scale), 0.0)
    totals = jnp.sum(weights, axis=-1, keepdims=True)
    rounded = weights.astype(bf16)
    mixed = jnp.zeros((rows, lanes), f32)
    for k in range(kvs):
        mine = (head >= k * per) & (head < (k + 1) * per)
        mixed = mixed + dot(
            jnp.where(mine, rounded, jnp.zeros_like(rounded)), v_ref[:, k * lanes : (k + 1) * lanes]
        )
    self_score = jnp.sum(new_q.astype(f32) * new_k.astype(f32), axis=-1, keepdims=True)
    self_weight = jnp.where(tp == 0, jnp.exp(self_score * scale), 0.0)
    totals = totals + self_weight
    mixed = (mixed + self_weight * row_v[...]) * jax.nn.sigmoid(row_g[...])
    total_row = jnp.sum(jnp.where(row == col, totals, 0.0), axis=0, keepdims=True)
    high = total_row.astype(bf16).astype(f32)
    pay[...] = jnp.zeros_like(pay)
    pay[0:rows, :] = mixed
    pay[rows + rpg : rows + rpg + 1, :] = high
    pay[rows + rpg + 1 : rows + rpg + 2, :] = total_row - high
    peers = pay_ref.shape[0]
    tps = lax.axis_size("tp")
    slices = resid_ref.shape[1] // (tps * lanes)
    for z in range(slices):
        at = pl.ds(pl.multiple_of((z * tps + tp) * lanes, lanes), lanes)
        pay[rows : rows + rpg, :] = resid_ref[:, at].astype(f32)
        out = pay[...].astype(bf16)
        for peer in range(z * peers // slices, (z + 1) * peers // slices):
            pay_ref[peer] = out
    for copy in copies[11:]:
        copy.wait()


def fetch_kernel(gate_hbm, up_hbm, ng_hbm, mine_ref, ng_ref, sems):
    units = mine_ref.shape[1] // 2
    width = ng_ref.shape[1]
    req = lax.axis_index("req")
    at = pl.ds(pl.multiple_of(lax.rem(req, 2) * units, lanes), units)
    cols = pl.ds(pl.multiple_of(lax.div(req, 2) * width, lanes), width)
    copies = (
        pltpu.make_async_copy(gate_hbm.at[:, at], mine_ref.at[:, pl.ds(0, units)], sems.at[0]),
        pltpu.make_async_copy(up_hbm.at[:, at], mine_ref.at[:, pl.ds(units, units)], sems.at[1]),
        pltpu.make_async_copy(ng_hbm.at[:, cols], ng_ref, sems.at[2]),
    )
    for copy in copies:
        copy.start()
    for copy in copies:
        copy.wait()


def columns_kernel(w_hbm, w_ref, sems):
    width = w_ref.shape[1]
    z = lax.div(lax.axis_index("req"), 2)
    copy = pltpu.make_async_copy(
        w_hbm.at[:, pl.ds(pl.multiple_of(z * width, lanes), width)], w_ref, sems.at[0]
    )
    copy.start()
    copy.wait()


def ready_kernel(*refs):
    refs[-1][...] = jnp.zeros_like(refs[-1])


def hidden_kernel(
    pay_ref, w0_ref, w1_ref, w2_ref, w3_ref, mine_ref, pair_ref, ng_ref, _,
    hid_ref, msg_ref, att, hid, xs, acc,
):
    tp = lax.axis_index("tp")
    req = lax.axis_index("req")
    tps = lax.axis_size("tp")
    z, y = lax.div(req, 2), lax.rem(req, 2)
    heads, toks, _ = att.shape
    groups = pay_ref.shape[0] // tps
    rpg = toks // groups
    rows = heads * rpg
    diag = iota((rows, lanes), 0) == iota((rows, lanes), 1)
    for r in range(groups):
        total = jnp.zeros(acc.shape, f32)
        for t in range(tps):
            piece = pay_ref[r * tps + t].astype(f32)
            total = total + piece
            acc[...] = piece
            hid[r * rpg : (r + 1) * rpg, t * lanes : (t + 1) * lanes] = acc[rows : rows + rpg, :]
        acc[...] = total
        total_row = acc[rows + rpg : rows + rpg + 1, :] + acc[rows + rpg + 1 : rows + rpg + 2, :]
        totals = jnp.sum(
            jnp.where(diag, jnp.broadcast_to(total_row, (rows, lanes)), 0.0), axis=-1, keepdims=True
        )
        acc[0:rows, :] = acc[0:rows, :] / totals
        for h in range(heads):
            att[h, r * rpg : (r + 1) * rpg, :] = acc[h * rpg : (h + 1) * rpg, :]
    state = hid[...]
    per = heads // tps
    for d, w_ref in enumerate((w0_ref, w1_ref, w2_ref, w3_ref)):
        source = tp ^ d
        for j in range(per):
            state = state + dot(
                att[source * per + j].astype(bf16), w_ref[j * lanes : (j + 1) * lanes, :]
            )
    hid_ref[...] = state
    width = state.shape[1]
    half = width // 2
    sums = jnp.sum(state * state, axis=-1, keepdims=True)
    scaled = state * ng_ref[...]
    xs[0] = scaled[:, :half]
    xs[1] = scaled[:, half:]
    own, other = xs[y].astype(bf16), xs[1 - y].astype(bf16)
    units = pair_ref.shape[1] // 2
    gate = dot(own, mine_ref[:, :units]) + dot(other, pair_ref[:, :units])
    up = dot(own, mine_ref[:, units:]) + dot(other, pair_ref[:, units:])
    high = sums.astype(bf16).astype(f32)
    lane = iota((toks, lanes), 1)
    msg_ref[:, :units] = gate.astype(bf16)
    msg_ref[:, units : 2 * units] = up.astype(bf16)
    msg_ref[:, 2 * units :] = jnp.where(
        lane == 0, high, jnp.where(lane == 1, sums - high, 0.0)
    ).astype(bf16)


def down_kernel(m0_ref, m1_ref, m2_ref, m3_ref, hid_ref, down_ref, pair_ref, back_ref, part, pay):
    tp = lax.axis_index("tp")
    tps = lax.axis_size("tp")
    y = lax.rem(lax.axis_index("req"), 2)
    units, half = pair_ref.shape
    toks, width = hid_ref.shape
    total = m0_ref[...].astype(f32)
    for m_ref in (m1_ref, m2_ref, m3_ref):
        total = total + m_ref[...].astype(f32)
    sums = total[:, 2 * units : 2 * units + 1] + total[:, 2 * units + 1 : 2 * units + 2]
    factor = lax.rsqrt(sums / (width * 4) + norm_eps)
    gate = total[:, :units] * factor
    hidden = (gate / (1.0 + jnp.exp(-gate)) * (total[:, units : 2 * units] * factor)).astype(bf16)
    own_rows = pl.ds(pl.multiple_of(y * units, lanes), units)
    part[y] = dot(hidden, down_ref[own_rows, :])
    part[1 - y] = dot(hidden, pair_ref[...])
    chunks = width // lanes
    groups = pay.shape[0]
    rpg = toks // groups
    piece = hid_ref[:, pl.ds(pl.multiple_of(tp * lanes, lanes), lanes)]
    high = piece.astype(bf16).astype(f32)
    piece = jnp.where(y == 0, high, piece - high)
    pay[...] = jnp.zeros_like(pay)
    for c in range(chunks + 1):
        if c < chunks:
            at = (c * lanes) % half
            block = part[c * lanes // half][:, at : at + lanes]
        else:
            block = piece
        for r in range(groups):
            pay[r, c * rpg : (c + 1) * rpg, :] = block[r * rpg : (r + 1) * rpg, :]
    for r in range(groups):
        out = pay[r].astype(bf16)
        for t in range(tps):
            back_ref[r * tps + t] = out


def final_kernel(back_ref, out_ref, acc, tail, rows_out):
    tps = lax.axis_size("tp")
    peers = back_ref.shape[0]
    rpg, width = out_ref.shape
    chunks = tps
    slices = width // (chunks * lanes)
    group = peers // slices
    for z in range(slices):
        total = jnp.zeros(acc.shape, f32)
        by_tp = [jnp.zeros(acc.shape, f32) for _ in range(tps)]
        for p in range(group):
            piece = back_ref[z * group + p].astype(f32)
            total = total + piece
            by_tp[p % tps] = by_tp[p % tps] + piece
        acc[...] = total
        for c in range(chunks):
            tail[...] = by_tp[c]
            at = slice((z * chunks + c) * lanes, (z * chunks + c + 1) * lanes)
            rows_out[0:rpg, at] = (
                acc[c * rpg : (c + 1) * rpg, :] + tail[chunks * rpg : (chunks + 1) * rpg, :]
            )
    out_ref[...] = rows_out[0:rpg, :].astype(bf16)


def prefill_kernel(
    len_ref, q_ref, g_ref, kv0_ref, kv1_ref, kv2_ref, kv3_ref, qg_ref, freq_ref, out_ref, mid_ref
):
    tp = lax.axis_index("tp")
    tok = q_ref.shape[0]
    heads = q_ref.shape[1] // lanes
    kvs = kv0_ref.shape[1] // (2 * lanes)
    per = heads // kvs
    third = tp == 2
    mid_ref[...] = jnp.where(third, kv3_ref[...], kv1_ref[...])
    blocks = ((tp, kv0_ref), (jnp.where(third, tp ^ 3, tp ^ 1), mid_ref), (tp ^ 2, kv2_ref))
    tok_index = tp * tok + iota((tok, lanes), 0)
    begin = begin_of(tok_index, len_ref)
    factors = rope_factors((tok_index - begin).astype(f32) * freq_ref[...])
    col = iota((tok, tok), 1)
    allowed = []
    for block, _ in blocks:
        key_index = block * tok + col
        allowed.append((key_index >= begin) & (key_index <= tok_index))
    gates = jax.nn.sigmoid(g_ref[...].astype(f32))
    qg = qg_ref[...]
    scale = lanes ** (-0.5)
    for h in range(heads):
        k = h // per
        at = slice(h * lanes, (h + 1) * lanes)
        query = norm_rope(q_ref[:, at].astype(f32), qg, factors)
        totals = jnp.zeros((tok, 1), f32)
        mixed = jnp.zeros((tok, lanes), f32)
        for b, (_, kv_ref) in enumerate(blocks):
            scores = dot_nt(query, kv_ref[:, k * lanes : (k + 1) * lanes])
            weights = jnp.where(allowed[b], jnp.exp(scores * scale), 0.0)
            totals = totals + jnp.sum(weights, axis=-1, keepdims=True)
            mixed = mixed + dot(
                weights.astype(bf16), kv_ref[:, (kvs + k) * lanes : (kvs + k + 1) * lanes]
            )
        out_ref[:, at] = (mixed / totals * gates[:, h : h + 1]).astype(bf16)


def call(body, out_shape, args, scratch=(), hbm=False, smem=0, flops=0, limit=12, **more):
    specs = [pl.BlockSpec(memory_space=pltpu.SMEM)] * smem
    space = pltpu.HBM if hbm else pltpu.VMEM
    specs += [pl.BlockSpec(memory_space=space)] * (len(args) - smem)
    size = sum(a.size * a.dtype.itemsize for a in args)
    return pl.pallas_call(
        body,
        out_shape=out_shape,
        in_specs=specs,
        out_specs=jax.tree.map(lambda _: pl.BlockSpec(memory_space=pltpu.VMEM), out_shape),
        scratch_shapes=[pltpu.VMEM(s, f32) if isinstance(s, tuple) else s for s in scratch],
        compiler_params=pltpu.CompilerParams(vmem_limit_bytes=limit * 2**20),
        cost_estimate=pl.CostEstimate(flops=flops, bytes_accessed=size, transcendentals=0),
    )(*args)


def hold(arrays, flops):
    return pl.pallas_call(
        ready_kernel,
        out_shape=jax.ShapeDtypeStruct((8, lanes), f32),
        in_specs=[pl.BlockSpec(memory_space=pl.ANY)] * len(arrays),
        out_specs=pl.BlockSpec(memory_space=pltpu.VMEM),
        compiler_params=pltpu.CompilerParams(vmem_limit_bytes=2**20),
        cost_estimate=pl.CostEstimate(flops=flops, bytes_accessed=0, transcendentals=0),
    )(*arrays)


def local(
    q_pre,
    gate_pre,
    k_pre,
    v_pre,
    q_gain,
    k_gain,
    lengths,
    q_new,
    gate_new,
    k_new,
    v_new,
    resid,
    w_out,
    norm_gain,
    w_gate,
    w_up,
    w_down,
):
    tps, reqs = lax.axis_size("tp"), lax.axis_size("req")
    tok = q_pre.shape[0]
    rpg, width = resid.shape
    slices = reqs // 2
    head_size = q_gain.shape[0]
    heads = gate_pre.shape[1]
    part = width // slices if slices else 0
    if not (slices == 4 and tps == 4 and head_size == lanes == tok and part == tps * lanes):
        return general(
            q_pre, gate_pre, k_pre, v_pre, q_gain, k_gain, lengths, q_new, gate_new, k_new, v_new,
            resid, w_out, norm_gain, w_gate, w_up, w_down,
        )
    peers = tps * reqs
    toks = rpg * reqs
    units = w_gate.shape[1] // 2
    req = lax.axis_index("req")
    z, y = req // 2, req % 2
    freqs = rope_base ** (-(np.arange(head_size // 2) * 2.0 / head_size))
    freqs = jnp.asarray(np.concatenate([freqs, freqs])[None, :], f32)
    qg, kg = q_gain[None, :], k_gain[None, :]

    def cross(array, by):
        return lax.ppermute(array, "tp", [(i, i ^ by) for i in range(tps)])

    def swap(array):
        return lax.ppermute(array, "req", [(i, i ^ 1) for i in range(reqs)])

    def along(array, by):
        return lax.ppermute(array, "req", [(i, i ^ (2 * by)) for i in range(reqs)])

    inputs = (
        lengths, k_pre, v_pre, q_new, k_new, v_new, gate_new, resid, qg, kg, freqs,
        w_out, w_gate, w_up, w_down,
    )
    kv, pay, w_own, pair, down_pair = call(
        partial_kernel,
        (
            jax.ShapeDtypeStruct((tok, 2 * k_pre.shape[1]), bf16),
            jax.ShapeDtypeStruct((peers, pay_rows, lanes), bf16),
            jax.ShapeDtypeStruct((w_out.shape[0], part), bf16),
            jax.ShapeDtypeStruct((w_gate.shape[0], 2 * units), bf16),
            jax.ShapeDtypeStruct((units, w_down.shape[1]), bf16),
        ),
        inputs,
        scratch=[(heads * rpg, lanes)] * 4
        + [(pay_rows, lanes), pltpu.SMEM(lengths.shape, jnp.int32)]
        + [pltpu.VMEM(a.shape, a.dtype) for a in inputs[1:11]]
        + [pltpu.SemaphoreType.DMA((len(inputs),))],
        hbm=True,
        flops=10**7,
        limit=56,
    )
    w_far = cross(w_own, 2)
    pair = swap(pair)
    half = jax.ShapeDtypeStruct((w_gate.shape[0], 2 * units), bf16)
    mine, ng = call(
        fetch_kernel,
        (half, jax.ShapeDtypeStruct((1, part), f32)),
        (w_gate, w_up, norm_gain[None, :]),
        hbm=True,
        scratch=[pltpu.SemaphoreType.DMA((3,))],
    )
    w_here = call(
        columns_kernel,
        jax.ShapeDtypeStruct(w_own.shape, bf16),
        (w_out,),
        hbm=True,
        scratch=[pltpu.SemaphoreType.DMA((1,))],
    )
    late_far, _, _ = lax.optimization_barrier((w_far, mine, w_here))
    w_near, w_both = cross(w_own, 1), cross(late_far, 1)
    kv_near = cross(kv, 1)
    late_kv, _ = lax.optimization_barrier((kv, w_far))
    kv_far = cross(late_kv, 2)
    late_down, _ = lax.optimization_barrier((down_pair, w_far))
    down_pair = swap(late_down)
    got = lax.all_to_all(pay, ("req", "tp"), 0, 0, tiled=True)
    landed = hold((pair,), 2 * 10**9)
    token = hold((landed, w_near, w_both), 10**9)
    hid, msg = call(
        hidden_kernel,
        (
            jax.ShapeDtypeStruct((toks, part), f32),
            jax.ShapeDtypeStruct((toks, 2 * units + lanes), bf16),
        ),
        (got, w_here, w_near, w_far, w_both, mine, pair, ng, token),
        scratch=[
            (heads, toks, lanes),
            (toks, part),
            (2, toks, part // 2),
            (pay_rows, lanes),
        ],
        flops=10**7,
    )
    msgs = [msg] + [along(msg, d) for d in (3, 2, 1)]
    kv_both = cross(kv_far, 1)
    prefill_out = call(
        prefill_kernel,
        jax.ShapeDtypeStruct(q_pre.shape, bf16),
        (lengths, q_pre, gate_pre, kv, kv_near, kv_far, kv_both, qg, freqs),
        scratch=[pltpu.VMEM(kv.shape, bf16)],
        smem=1,
        flops=10**9,
    )
    back = call(
        down_kernel,
        jax.ShapeDtypeStruct((peers, back_rows, lanes), bf16),
        (*msgs, hid, w_down, down_pair),
        scratch=[(2, toks, part // 2), (reqs, back_rows, lanes)],
        flops=3 * 10**9,
    )
    returned = lax.all_to_all(back, ("req", "tp"), 0, 0, tiled=True)
    returned, prefill_out = lax.optimization_barrier((returned, prefill_out))
    decode_out = call(
        final_kernel,
        jax.ShapeDtypeStruct((rpg, width), bf16),
        (returned,),
        scratch=[(back_rows, lanes), (back_rows, lanes), (8, width)],
        flops=10**6,
    )
    return (prefill_out, decode_out)


def solution(mesh):
    return jax.shard_map(
        local,
        mesh=mesh,
        in_specs=(
            P(("req", "tp"), None),
            P(("req", "tp"), None),
            P(("req", "tp"), None),
            P(("req", "tp"), None),
            P(),
            P(),
            P("req", None),
            P("req", None),
            P("req", None),
            P("req", None),
            P("req", None),
            P("req", None),
            P("tp", None),
            P(),
            P("req", "tp"),
            P("req", "tp"),
            P("tp", "req"),
        ),
        out_specs=(P(("req", "tp"), None), P("req", None)),
        check_vma=False,
    )
```

```python
import jax
import jax.numpy as jnp
import numpy as np
from jax import lax
from jax.experimental import pallas as pl
from jax.experimental.pallas import tpu as pltpu
from jax.sharding import PartitionSpec as P

rope_base = 1000000.0
norm_eps = 1e-06


def group_layout(lengths_row, total):
    req_ends = jnp.cumsum(lengths_row)
    req_starts = req_ends - lengths_row
    indices = jnp.arange(total, dtype=jnp.int32)
    segment = jnp.sum((indices[:, None] >= req_ends[None, :]).astype(jnp.int32), axis=1)
    onehot = segment[:, None] == jnp.arange(lengths_row.shape[0], dtype=jnp.int32)[None, :]
    offsets = jnp.sum(jnp.where(onehot, req_starts[None, :], 0), axis=1)
    return (segment, indices - offsets)


def head_norm(values, gain):
    mean_sq = jnp.mean(values * values, axis=-1, keepdims=True)
    return values * lax.rsqrt(mean_sq + norm_eps) * gain


def rotate(values, position):
    half_size = values.shape[-1] // 2
    freqs = rope_base ** (-(jnp.arange(half_size, dtype=jnp.float32) * 2.0 / (2 * half_size)))
    angles = position.astype(jnp.float32)[:, None] * freqs[None, :]
    shaped = (values.shape[0],) + (1,) * (values.ndim - 2) + (half_size,)
    cosine = jnp.cos(angles).reshape(shaped)
    sine = jnp.sin(angles).reshape(shaped)
    first_half = values[..., :half_size]
    second_half = values[..., half_size:]
    return jnp.concatenate(
        [first_half * cosine - second_half * sine, second_half * cosine + first_half * sine],
        axis=-1,
    )


def general(
    q_pre,
    gate_pre,
    k_pre,
    v_pre,
    q_gain,
    k_gain,
    lengths,
    q_new,
    gate_new,
    k_new,
    v_new,
    resid,
    w_out,
    norm_gain,
    w_gate,
    w_up,
    w_down,
):
    tok_rows = q_pre.shape[0]
    tp_count = lax.axis_size("tp")
    tp_index = lax.axis_index("tp")
    head_size = q_gain.shape[0]
    query_heads = gate_pre.shape[1]
    kv_heads = k_pre.shape[1] // head_size
    groups_per = query_heads // kv_heads
    kv_local = kv_heads // tp_count
    req_count = lengths.shape[1]
    score_scale = head_size ** (-0.5)
    segment, position = group_layout(lengths[0], tok_rows * tp_count)
    row_offset = tp_index * tok_rows
    seg_local = lax.dynamic_slice_in_dim(segment, row_offset, tok_rows)
    pos_local = lax.dynamic_slice_in_dim(position, row_offset, tok_rows)
    query_index = row_offset + jnp.arange(tok_rows, dtype=jnp.int32)
    queries = rotate(
        head_norm(q_pre.reshape(tok_rows, query_heads, head_size).astype(jnp.float32), q_gain),
        pos_local,
    )
    queries = queries.astype(jnp.bfloat16).reshape(tok_rows, kv_heads, groups_per, head_size)
    keys = rotate(
        head_norm(k_pre.reshape(tok_rows, kv_heads, head_size).astype(jnp.float32), k_gain),
        pos_local,
    ).astype(jnp.bfloat16)
    values = v_pre.reshape(tok_rows, kv_heads, head_size)

    def key_block(running, key_piece, value_piece, first_row):
        key_count = key_piece.shape[0]
        key_index = first_row + jnp.arange(key_count, dtype=jnp.int32)
        allowed = (seg_local[:, None] == segment[None, :]) & (
            query_index[:, None] >= key_index[None, :]
        )
        scores = (
            jnp.einsum(
                "qkgd,pkd->qkgp",
                queries,
                key_piece.reshape(key_count, kv_heads, head_size),
                preferred_element_type=jnp.float32,
            )
            * score_scale
        )
        weights = jnp.where(allowed[:, None, None, :], jnp.exp(scores), 0.0)
        totals = running[0] + jnp.sum(weights, axis=-1)
        mixed = running[1] + jnp.einsum(
            "qkgp,pkd->qkgd",
            weights.astype(jnp.bfloat16),
            value_piece.reshape(key_count, kv_heads, head_size),
            preferred_element_type=jnp.float32,
        )
        return (totals, mixed)

    start_state = (
        jnp.zeros((tok_rows, kv_heads, groups_per), jnp.float32),
        jnp.zeros((tok_rows, kv_heads, groups_per, head_size), jnp.float32),
    )
    pieces = (
        lax.all_gather(keys.reshape(tok_rows, kv_heads * head_size), "tp", axis=0, tiled=True),
        lax.all_gather(v_pre, "tp", axis=0, tiled=True),
    )
    key_count = pieces[0].shape[0]
    block_rows = 512

    def one_block(number, carried):
        begin_at = number * block_rows
        return key_block(carried, pieces[0], pieces[1], begin_at)

    totals, mixed = lax.fori_loop(0, key_count // block_rows, one_block, start_state)
    gates = jax.nn.sigmoid(gate_pre.astype(jnp.float32)).reshape(tok_rows, kv_heads, groups_per)
    prefill_out = (
        (mixed / totals[..., None] * gates[..., None])
        .astype(jnp.bfloat16)
        .reshape(tok_rows, query_heads * head_size)
    )
    new_queries = rotate(
        head_norm(q_new.reshape(req_count, query_heads, head_size).astype(jnp.float32), q_gain),
        lengths[0],
    )
    new_queries = new_queries.astype(jnp.bfloat16).reshape(
        req_count, kv_heads, groups_per, head_size
    )
    new_keys = rotate(
        head_norm(k_new.reshape(req_count, kv_heads, head_size).astype(jnp.float32), k_gain),
        lengths[0],
    ).astype(jnp.bfloat16)
    new_values = v_new.reshape(req_count, kv_heads, head_size)
    new_gates = jax.nn.sigmoid(gate_new.astype(jnp.float32)).reshape(
        req_count, kv_heads, groups_per
    )
    head_first = tp_index * kv_local
    request_ids = jnp.arange(req_count, dtype=jnp.int32)
    own_queries = lax.dynamic_slice_in_dim(new_queries, head_first, kv_local, 1)
    cache_keys, cache_values = (
        lax.all_to_all(keys, "tp", split_axis=1, concat_axis=0, tiled=True),
        lax.all_to_all(values, "tp", split_axis=1, concat_axis=0, tiled=True),
    )
    scores = (
        jnp.einsum("rkgd,pkd->rkgp", own_queries, cache_keys, preferred_element_type=jnp.float32)
        * score_scale
    )
    owned = segment[None, :] == request_ids[:, None]
    weights = jnp.where(owned[:, None, None, :], jnp.exp(scores), 0.0)
    weighted = jnp.einsum(
        "rkgp,pkd->rkgd",
        weights.astype(jnp.bfloat16),
        cache_values,
        preferred_element_type=jnp.float32,
    )
    dec_totals = jnp.sum(weights, axis=-1)
    dec_mixed = weighted
    own_keys = lax.dynamic_slice_in_dim(new_keys, head_first, kv_local, 1)
    own_values = lax.dynamic_slice_in_dim(new_values, head_first, kv_local, 1)
    own_gates = lax.dynamic_slice_in_dim(new_gates, head_first, kv_local, 1)
    self_weight = jnp.exp(
        jnp.einsum("rkgd,rkd->rkg", own_queries, own_keys, preferred_element_type=jnp.float32)
        * score_scale
    )
    dec_totals = dec_totals + self_weight
    dec_mixed = dec_mixed + self_weight[..., None] * own_values.astype(jnp.float32)[:, :, None, :]
    attended = (
        (dec_mixed / dec_totals[..., None] * own_gates[..., None])
        .astype(jnp.bfloat16)
        .reshape(req_count, kv_local * groups_per * head_size)
    )
    partial_out = jnp.dot(attended, w_out, preferred_element_type=jnp.float32)
    attn_rows = lax.psum(partial_out, "tp")
    hidden_state = resid.astype(jnp.float32) + attn_rows
    mean_sq = jnp.mean(hidden_state * hidden_state, axis=-1, keepdims=True)
    normed = (hidden_state * lax.rsqrt(mean_sq + norm_eps) * norm_gain).astype(jnp.bfloat16)
    units_local = w_gate.shape[1]
    paired = jnp.concatenate([w_gate, w_up], axis=1)
    columns = lax.all_to_all(normed, "req", split_axis=1, concat_axis=0, tiled=True)
    whole_sums = lax.psum(jnp.dot(columns, paired, preferred_element_type=jnp.float32), "req")
    hidden_units = (jax.nn.silu(whole_sums[:, :units_local]) * whole_sums[:, units_local:]).astype(
        jnp.bfloat16
    )
    down_part = jnp.dot(hidden_units, w_down, preferred_element_type=jnp.float32)
    back_part = lax.all_to_all(down_part, "req", split_axis=0, concat_axis=1, tiled=True)
    mlp_rows = lax.psum(back_part, "tp")
    decode_out = (hidden_state + mlp_rows).astype(jnp.bfloat16)
    return (prefill_out, decode_out)


f32 = jnp.float32
bf16 = jnp.bfloat16
lanes = 128
pay_rows = 28
back_rows = 16


def dot(a, b):
    return jnp.dot(a, b, preferred_element_type=f32)


def dot_nt(a, b):
    return lax.dot_general(a, b, (((1,), (1,)), ((), ())), preferred_element_type=f32)


def iota(shape, dim):
    return lax.broadcasted_iota(jnp.int32, shape, dim)


def rope_factors(angles):
    turns = jnp.floor(angles * (2.0 / np.pi) + 0.5)
    rest = angles - turns * 1.5703125
    rest = rest - turns * 4.837512969970703125e-4
    rest = rest - turns * 7.549789948768648e-8
    sq = rest * rest
    sine = ((-1.9515295891e-4 * sq + 8.3321608736e-3) * sq - 1.6666654611e-1) * sq * rest + rest
    cosine = (
        ((2.443315711809948e-5 * sq - 1.388731625493765e-3) * sq + 4.166664568298827e-2) * sq * sq
        - 0.5 * sq
        + 1.0
    )
    low = iota(angles.shape, 1) < lanes // 2
    quarter = turns.astype(jnp.int32) + jnp.where(low, 1, 0)
    both = jnp.where((quarter & 1) == 1, cosine, sine)
    both = jnp.where((quarter & 2) == 2, -both, both)
    swapped = pltpu.roll(both, lanes // 2, 1)
    return jnp.where(low, both, swapped), jnp.where(low, -swapped, both)


def norm_rope(values, gain, factors):
    mean_sq = jnp.mean(values * values, axis=-1, keepdims=True)
    normed = values * lax.rsqrt(mean_sq + norm_eps) * gain
    return (normed * factors[0] + pltpu.roll(normed, lanes // 2, 1) * factors[1]).astype(bf16)


def begin_of(indices, len_ref):
    begin = jnp.zeros_like(indices)
    end = 0
    for j in range(len_ref.shape[1] - 1):
        end = end + len_ref[0, j]
        begin = jnp.where(indices >= end, end, begin)
    return begin


def partial_kernel(
    len_hbm, k_hbm, v_hbm, qn_hbm, kn_hbm, vn_hbm, gn_hbm, resid_hbm, qg_hbm, kg_hbm, freq_hbm,
    w_hbm, gate_hbm, up_hbm, down_hbm,
    kv_ref, pay_ref, own_ref, pair_ref, down_pair_ref, row_q, row_k, row_v, row_g, pay, len_ref, k_ref, v_ref, qn_ref, kn_ref, vn_ref, gn_ref,
    resid_ref, qg_ref, kg_ref, freq_ref, sems,
):
    tp = lax.axis_index("tp")
    req = lax.axis_index("req")
    z, other = lax.div(req, 2), 1 - lax.rem(req, 2)
    width = own_ref.shape[1]
    units = down_pair_ref.shape[0]
    cols = pl.ds(pl.multiple_of(z * width, lanes), width)
    theirs = pl.ds(pl.multiple_of(other * units, lanes), units)
    moves = (
        (len_hbm, len_ref), (freq_hbm, freq_ref), (k_hbm, k_ref), (kg_hbm, kg_ref),
        (qn_hbm, qn_ref), (kn_hbm, kn_ref), (vn_hbm, vn_ref), (gn_hbm, gn_ref), (qg_hbm, qg_ref),
        (v_hbm, v_ref), (resid_hbm, resid_ref),
        (gate_hbm.at[:, theirs], pair_ref.at[:, pl.ds(0, units)]),
        (up_hbm.at[:, theirs], pair_ref.at[:, pl.ds(units, units)]),
        (w_hbm.at[:, cols], own_ref),
        (down_hbm.at[theirs, :], down_pair_ref),
    )
    copies = [pltpu.make_async_copy(a, b, sems.at[i]) for i, (a, b) in enumerate(moves)]
    for copy in copies:
        copy.start()
    tok = k_ref.shape[0]
    rpg = qn_ref.shape[0]
    heads = qn_ref.shape[1] // lanes
    kvs = k_ref.shape[1] // lanes
    per = heads // kvs
    rows = heads * rpg
    for copy in copies[:2]:
        copy.wait()
    freq = freq_ref[...]
    tok_index = tp * tok + iota((tok, lanes), 0)
    factors = rope_factors((tok_index - begin_of(tok_index, len_ref)).astype(f32) * freq)
    for copy in copies[2:11]:
        copy.wait()
    qg, kg = qg_ref[...], kg_ref[...]
    keys = []
    for k in range(kvs):
        at = slice(k * lanes, (k + 1) * lanes)
        keys.append(norm_rope(k_ref[:, at].astype(f32), kg, factors))
        kv_ref[:, at] = keys[-1]
    kv_ref[:, kvs * lanes :] = v_ref[...]
    qn, kn = qn_ref[...].astype(f32), kn_ref[...].astype(f32)
    vn, gn = vn_ref[...].astype(f32), gn_ref[...].astype(f32)
    for h in range(heads):
        at = slice(h * rpg, (h + 1) * rpg)
        kv = slice((h // per) * lanes, (h // per + 1) * lanes)
        row_q[at, :] = qn[:, h * lanes : (h + 1) * lanes]
        row_k[at, :] = kn[:, kv]
        row_v[at, :] = vn[:, kv]
        row_g[at, :] = jnp.broadcast_to(gn[:, h : h + 1], (rpg, lanes))
    row = iota((rows, lanes), 0)
    col = iota((rows, lanes), 1)
    head = row * 0
    for h in range(1, heads):
        head = jnp.where(row >= h * rpg, h, head)
    request = row - head * rpg
    length, first, last = row * 0, row * 0, row * 0
    end = 0
    for j in range(rpg):
        mine = request == j
        length = jnp.where(mine, len_ref[0, j], length)
        first = jnp.where(mine, end, first)
        end = end + len_ref[0, j]
        last = jnp.where(mine, end, last)
    new_factors = rope_factors(length.astype(f32) * freq)
    scale = lanes ** (-0.5)
    new_q = norm_rope(row_q[...], qg, new_factors)
    new_k = norm_rope(row_k[...], kg, new_factors)
    scores = jnp.zeros((rows, tok), f32)
    for k in range(kvs):
        mine = (head >= k * per) & (head < (k + 1) * per)
        scores = jnp.where(mine, dot_nt(new_q, keys[k]), scores)
    index = tp * tok + col
    weights = jnp.where((index >= first) & (index < last), jnp.exp(scores * scale), 0.0)
    totals = jnp.sum(weights, axis=-1, keepdims=True)
    rounded = weights.astype(bf16)
    mixed = jnp.zeros((rows, lanes), f32)
    for k in range(kvs):
        mine = (head >= k * per) & (head < (k + 1) * per)
        mixed = mixed + dot(
            jnp.where(mine, rounded, jnp.zeros_like(rounded)), v_ref[:, k * lanes : (k + 1) * lanes]
        )
    self_score = jnp.sum(new_q.astype(f32) * new_k.astype(f32), axis=-1, keepdims=True)
    self_weight = jnp.where(tp == 0, jnp.exp(self_score * scale), 0.0)
    totals = totals + self_weight
    mixed = (mixed + self_weight * row_v[...]) * jax.nn.sigmoid(row_g[...])
    total_row = jnp.sum(jnp.where(row == col, totals, 0.0), axis=0, keepdims=True)
    high = total_row.astype(bf16).astype(f32)
    rest = pltpu.roll(jnp.broadcast_to(total_row - high, (8, lanes)), lanes // 2, 1)
    pay[0:rows, :] = mixed
    pay[rows + rpg : rows + rpg + 1, :] = jnp.where(
        iota((1, lanes), 1) < lanes // 2, high, rest[0:1, :]
    )
    peers = pay_ref.shape[0]
    tps = lax.axis_size("tp")
    slices = resid_ref.shape[1] // (tps * lanes)
    for z in range(slices):
        at = pl.ds(pl.multiple_of((z * tps + tp) * lanes, lanes), lanes)
        pay[rows : rows + rpg, :] = resid_ref[:, at].astype(f32)
        for g in range(pay_ref.shape[1]):
            out = pay[4 * g : 4 * g + 4, :].astype(bf16)
            for peer in range(z * peers // slices, (z + 1) * peers // slices):
                pay_ref[peer, g] = out
    for copy in copies[11:]:
        copy.wait()


def fetch_kernel(gate_hbm, up_hbm, ng_hbm, mine_ref, ng_ref, sems):
    units = mine_ref.shape[1] // 2
    width = ng_ref.shape[1]
    req = lax.axis_index("req")
    at = pl.ds(pl.multiple_of(lax.rem(req, 2) * units, lanes), units)
    cols = pl.ds(pl.multiple_of(lax.div(req, 2) * width, lanes), width)
    copies = (
        pltpu.make_async_copy(gate_hbm.at[:, at], mine_ref.at[:, pl.ds(0, units)], sems.at[0]),
        pltpu.make_async_copy(up_hbm.at[:, at], mine_ref.at[:, pl.ds(units, units)], sems.at[1]),
        pltpu.make_async_copy(ng_hbm.at[:, cols], ng_ref, sems.at[2]),
    )
    for copy in copies:
        copy.start()
    for copy in copies:
        copy.wait()


def columns_kernel(w_hbm, w_ref, sems):
    width = w_ref.shape[1]
    z = lax.div(lax.axis_index("req"), 2)
    copy = pltpu.make_async_copy(
        w_hbm.at[:, pl.ds(pl.multiple_of(z * width, lanes), width)], w_ref, sems.at[0]
    )
    copy.start()
    copy.wait()


def ready_kernel(*refs):
    refs[-1][...] = jnp.zeros_like(refs[-1])


def hidden_kernel(
    pay_ref, w0_ref, w1_ref, w2_ref, w3_ref, mine_ref, pair_ref, ng_ref, _,
    hid_ref, msg_ref, att, hid, xs, acc,
):
    tp = lax.axis_index("tp")
    req = lax.axis_index("req")
    tps = lax.axis_size("tp")
    z, y = lax.div(req, 2), lax.rem(req, 2)
    heads, toks, _ = att.shape
    groups = pay_ref.shape[0] // tps
    rpg = toks // groups
    rows = heads * rpg
    diag = iota((rows, lanes), 0) == iota((rows, lanes), 1)
    quads = pay_ref.shape[1]
    for r in range(groups):
        for g in range(quads):
            total = jnp.zeros((4, lanes), f32)
            for t in range(tps):
                piece = pay_ref[r * tps + t, g].astype(f32)
                total = total + piece
                if g == quads - 1:
                    hid[r * rpg : (r + 1) * rpg, t * lanes : (t + 1) * lanes] = piece[:rpg, :]
            acc[r, 4 * g : 4 * g + 4, :] = total
    for r in range(groups):
        total_row = jnp.broadcast_to(acc[r, pay_rows - 1 : pay_rows, :], (rows, lanes))
        total_row = total_row + pltpu.roll(total_row, lanes // 2, 1)
        totals = jnp.sum(jnp.where(diag, total_row, 0.0), axis=-1, keepdims=True)
        acc[r, 0:rows, :] = acc[r, 0:rows, :] / totals
    for r in range(groups):
        for h in range(heads):
            att[h, r * rpg : (r + 1) * rpg, :] = acc[r, h * rpg : (h + 1) * rpg, :]
    state = hid[...]
    per = heads // tps
    for d, w_ref in enumerate((w0_ref, w1_ref, w2_ref, w3_ref)):
        source = tp ^ d
        for j in range(per):
            state = state + dot(
                att[source * per + j].astype(bf16), w_ref[j * lanes : (j + 1) * lanes, :]
            )
    hid_ref[...] = state
    width = state.shape[1]
    half = width // 2
    sums = jnp.sum(state * state, axis=-1, keepdims=True)
    scaled = state * ng_ref[...]
    xs[0] = scaled[:, :half]
    xs[1] = scaled[:, half:]
    own, other = xs[y].astype(bf16), xs[1 - y].astype(bf16)
    units = pair_ref.shape[1] // 2
    gate = dot(own, mine_ref[:, :units]) + dot(other, pair_ref[:, :units])
    up = dot(own, mine_ref[:, units:]) + dot(other, pair_ref[:, units:])
    high = sums.astype(bf16).astype(f32)
    lane = iota((toks, lanes), 1)
    msg_ref[:, :units] = gate.astype(bf16)
    msg_ref[:, units : 2 * units] = up.astype(bf16)
    msg_ref[:, 2 * units :] = jnp.where(
        lane == 0, high, jnp.where(lane == 1, sums - high, 0.0)
    ).astype(bf16)


def down_kernel(m0_ref, m1_ref, m2_ref, m3_ref, hid_ref, down_ref, pair_ref, back_ref, part, pay):
    tp = lax.axis_index("tp")
    tps = lax.axis_size("tp")
    y = lax.rem(lax.axis_index("req"), 2)
    units, half = pair_ref.shape
    toks, width = hid_ref.shape
    total = m0_ref[...].astype(f32)
    for m_ref in (m1_ref, m2_ref, m3_ref):
        total = total + m_ref[...].astype(f32)
    sums = total[:, 2 * units : 2 * units + 1] + total[:, 2 * units + 1 : 2 * units + 2]
    factor = lax.rsqrt(sums / (width * 4) + norm_eps)
    gate = total[:, :units] * factor
    hidden = (gate / (1.0 + jnp.exp(-gate)) * (total[:, units : 2 * units] * factor)).astype(bf16)
    own_rows = pl.ds(pl.multiple_of(y * units, lanes), units)
    part[y] = dot(hidden, down_ref[own_rows, :])
    part[1 - y] = dot(hidden, pair_ref[...])
    chunks = width // lanes
    groups = pay.shape[0]
    rpg = toks // groups
    piece = hid_ref[:, pl.ds(pl.multiple_of(tp * lanes, lanes), lanes)]
    high = piece.astype(bf16).astype(f32)
    piece = jnp.where(y == 0, high, piece - high)
    pay[...] = jnp.zeros_like(pay)
    for c in range(chunks + 1):
        if c < chunks:
            at = (c * lanes) % half
            block = part[c * lanes // half][:, at : at + lanes]
        else:
            block = piece
        for r in range(groups):
            pay[r, c * rpg : (c + 1) * rpg, :] = block[r * rpg : (r + 1) * rpg, :]
    for r in range(groups):
        out = pay[r].astype(bf16)
        for t in range(tps):
            back_ref[r * tps + t] = out


def final_kernel(back_ref, out_ref, acc, tail, rows_out):
    tps = lax.axis_size("tp")
    peers = back_ref.shape[0]
    rpg, width = out_ref.shape
    chunks = tps
    slices = width // (chunks * lanes)
    group = peers // slices
    for z in range(slices):
        total = jnp.zeros(acc.shape, f32)
        by_tp = [jnp.zeros(acc.shape, f32) for _ in range(tps)]
        for p in range(group):
            piece = back_ref[z * group + p].astype(f32)
            total = total + piece
            by_tp[p % tps] = by_tp[p % tps] + piece
        acc[...] = total
        for c in range(chunks):
            tail[...] = by_tp[c]
            at = slice((z * chunks + c) * lanes, (z * chunks + c + 1) * lanes)
            rows_out[0:rpg, at] = (
                acc[c * rpg : (c + 1) * rpg, :] + tail[chunks * rpg : (chunks + 1) * rpg, :]
            )
    out_ref[...] = rows_out[0:rpg, :].astype(bf16)


def prefill_kernel(
    len_ref, q_ref, g_ref, kv0_ref, kv1_ref, kv2_ref, kv3_ref, qg_ref, freq_ref, out_ref, mid_ref
):
    tp = lax.axis_index("tp")
    tok = q_ref.shape[0]
    heads = q_ref.shape[1] // lanes
    kvs = kv0_ref.shape[1] // (2 * lanes)
    per = heads // kvs
    third = tp == 2
    mid_ref[...] = jnp.where(third, kv3_ref[...], kv1_ref[...])
    blocks = ((tp, kv0_ref), (jnp.where(third, tp ^ 3, tp ^ 1), mid_ref), (tp ^ 2, kv2_ref))
    tok_index = tp * tok + iota((tok, lanes), 0)
    begin = begin_of(tok_index, len_ref)
    factors = rope_factors((tok_index - begin).astype(f32) * freq_ref[...])
    col = iota((tok, tok), 1)
    allowed = []
    for block, _ in blocks:
        key_index = block * tok + col
        allowed.append((key_index >= begin) & (key_index <= tok_index))
    gates = jax.nn.sigmoid(g_ref[...].astype(f32))
    qg = qg_ref[...]
    scale = lanes ** (-0.5)
    for h in range(heads):
        k = h // per
        at = slice(h * lanes, (h + 1) * lanes)
        query = norm_rope(q_ref[:, at].astype(f32), qg, factors)
        totals = jnp.zeros((tok, 1), f32)
        mixed = jnp.zeros((tok, lanes), f32)
        for b, (_, kv_ref) in enumerate(blocks):
            scores = dot_nt(query, kv_ref[:, k * lanes : (k + 1) * lanes])
            weights = jnp.where(allowed[b], jnp.exp(scores * scale), 0.0)
            totals = totals + jnp.sum(weights, axis=-1, keepdims=True)
            mixed = mixed + dot(
                weights.astype(bf16), kv_ref[:, (kvs + k) * lanes : (kvs + k + 1) * lanes]
            )
        out_ref[:, at] = (mixed / totals * gates[:, h : h + 1]).astype(bf16)


def call(body, out_shape, args, scratch=(), hbm=False, smem=0, flops=0, limit=12, **more):
    specs = [pl.BlockSpec(memory_space=pltpu.SMEM)] * smem
    space = pltpu.HBM if hbm else pltpu.VMEM
    specs += [pl.BlockSpec(memory_space=space)] * (len(args) - smem)
    size = sum(a.size * a.dtype.itemsize for a in args)
    return pl.pallas_call(
        body,
        out_shape=out_shape,
        in_specs=specs,
        out_specs=jax.tree.map(lambda _: pl.BlockSpec(memory_space=pltpu.VMEM), out_shape),
        scratch_shapes=[pltpu.VMEM(s, f32) if isinstance(s, tuple) else s for s in scratch],
        compiler_params=pltpu.CompilerParams(vmem_limit_bytes=limit * 2**20),
        cost_estimate=pl.CostEstimate(flops=flops, bytes_accessed=size, transcendentals=0),
    )(*args)


def hold(arrays, flops):
    return pl.pallas_call(
        ready_kernel,
        out_shape=jax.ShapeDtypeStruct((8, lanes), f32),
        in_specs=[pl.BlockSpec(memory_space=pl.ANY)] * len(arrays),
        out_specs=pl.BlockSpec(memory_space=pltpu.VMEM),
        compiler_params=pltpu.CompilerParams(vmem_limit_bytes=2**20),
        cost_estimate=pl.CostEstimate(flops=flops, bytes_accessed=0, transcendentals=0),
    )(*arrays)


def local(
    q_pre,
    gate_pre,
    k_pre,
    v_pre,
    q_gain,
    k_gain,
    lengths,
    q_new,
    gate_new,
    k_new,
    v_new,
    resid,
    w_out,
    norm_gain,
    w_gate,
    w_up,
    w_down,
):
    tps, reqs = lax.axis_size("tp"), lax.axis_size("req")
    tok = q_pre.shape[0]
    rpg, width = resid.shape
    slices = reqs // 2
    head_size = q_gain.shape[0]
    heads = gate_pre.shape[1]
    part = width // slices if slices else 0
    if not (slices == 4 and tps == 4 and head_size == lanes == tok and part == tps * lanes):
        return general(
            q_pre, gate_pre, k_pre, v_pre, q_gain, k_gain, lengths, q_new, gate_new, k_new, v_new,
            resid, w_out, norm_gain, w_gate, w_up, w_down,
        )
    peers = tps * reqs
    toks = rpg * reqs
    units = w_gate.shape[1] // 2
    req = lax.axis_index("req")
    z, y = req // 2, req % 2
    freqs = rope_base ** (-(np.arange(head_size // 2) * 2.0 / head_size))
    freqs = jnp.asarray(np.concatenate([freqs, freqs])[None, :], f32)
    qg, kg = q_gain[None, :], k_gain[None, :]

    def cross(array, by):
        return lax.ppermute(array, "tp", [(i, i ^ by) for i in range(tps)])

    def swap(array):
        return lax.ppermute(array, "req", [(i, i ^ 1) for i in range(reqs)])

    def along(array, by):
        return lax.ppermute(array, "req", [(i, i ^ (2 * by)) for i in range(reqs)])

    inputs = (
        lengths, k_pre, v_pre, q_new, k_new, v_new, gate_new, resid, qg, kg, freqs,
        w_out, w_gate, w_up, w_down,
    )
    kv, pay, w_own, pair, down_pair = call(
        partial_kernel,
        (
            jax.ShapeDtypeStruct((tok, 2 * k_pre.shape[1]), bf16),
            jax.ShapeDtypeStruct((peers, pay_rows // 4, 4, lanes), bf16),
            jax.ShapeDtypeStruct((w_out.shape[0], part), bf16),
            jax.ShapeDtypeStruct((w_gate.shape[0], 2 * units), bf16),
            jax.ShapeDtypeStruct((units, w_down.shape[1]), bf16),
        ),
        inputs,
        scratch=[(heads * rpg, lanes)] * 4
        + [(pay_rows, lanes), pltpu.SMEM(lengths.shape, jnp.int32)]
        + [pltpu.VMEM(a.shape, a.dtype) for a in inputs[1:11]]
        + [pltpu.SemaphoreType.DMA((len(inputs),))],
        hbm=True,
        flops=10**7,
        limit=56,
    )
    w_far = cross(w_own, 2)
    pair = swap(pair)
    half = jax.ShapeDtypeStruct((w_gate.shape[0], 2 * units), bf16)
    mine, ng = call(
        fetch_kernel,
        (half, jax.ShapeDtypeStruct((1, part), f32)),
        (w_gate, w_up, norm_gain[None, :]),
        hbm=True,
        scratch=[pltpu.SemaphoreType.DMA((3,))],
    )
    w_here = call(
        columns_kernel,
        jax.ShapeDtypeStruct(w_own.shape, bf16),
        (w_out,),
        hbm=True,
        scratch=[pltpu.SemaphoreType.DMA((1,))],
    )
    late_far, _, _ = lax.optimization_barrier((w_far, mine, w_here))
    w_near, w_both = cross(w_own, 1), cross(late_far, 1)
    kv_near = cross(kv, 1)
    late_kv, _ = lax.optimization_barrier((kv, w_far))
    kv_far = cross(late_kv, 2)
    late_down, _ = lax.optimization_barrier((down_pair, w_far))
    down_pair = swap(late_down)
    got = lax.all_to_all(pay, ("req", "tp"), 0, 0, tiled=True)
    landed = hold((pair,), 2 * 10**9)
    token = hold((landed, w_near, w_both), 10**9)
    hid, msg = call(
        hidden_kernel,
        (
            jax.ShapeDtypeStruct((toks, part), f32),
            jax.ShapeDtypeStruct((toks, 2 * units + lanes), bf16),
        ),
        (got, w_here, w_near, w_far, w_both, mine, pair, ng, token),
        scratch=[
            (heads, toks, lanes),
            (toks, part),
            (2, toks, part // 2),
            (reqs, pay_rows, lanes),
        ],
        flops=10**7,
    )
    msgs = [msg] + [along(msg, d) for d in (3, 2, 1)]
    kv_both = cross(kv_far, 1)
    prefill_out = call(
        prefill_kernel,
        jax.ShapeDtypeStruct(q_pre.shape, bf16),
        (lengths, q_pre, gate_pre, kv, kv_near, kv_far, kv_both, qg, freqs),
        scratch=[pltpu.VMEM(kv.shape, bf16)],
        smem=1,
        flops=10**9,
    )
    back = call(
        down_kernel,
        jax.ShapeDtypeStruct((peers, back_rows, lanes), bf16),
        (*msgs, hid, w_down, down_pair),
        scratch=[(2, toks, part // 2), (reqs, back_rows, lanes)],
        flops=3 * 10**9,
    )
    returned = lax.all_to_all(back, ("req", "tp"), 0, 0, tiled=True)
    returned, prefill_out = lax.optimization_barrier((returned, prefill_out))
    decode_out = call(
        final_kernel,
        jax.ShapeDtypeStruct((rpg, width), bf16),
        (returned,),
        scratch=[(back_rows, lanes), (back_rows, lanes), (8, width)],
        flops=10**6,
    )
    return (prefill_out, decode_out)


def solution(mesh):
    return jax.shard_map(
        local,
        mesh=mesh,
        in_specs=(
            P(("req", "tp"), None),
            P(("req", "tp"), None),
            P(("req", "tp"), None),
            P(("req", "tp"), None),
            P(),
            P(),
            P("req", None),
            P("req", None),
            P("req", None),
            P("req", None),
            P("req", None),
            P("req", None),
            P("tp", None),
            P(),
            P("req", "tp"),
            P("req", "tp"),
            P("tp", "req"),
        ),
        out_specs=(P(("req", "tp"), None), P("req", None)),
        check_vma=False,
    )
```

```python
import jax
import jax.numpy as jnp
import numpy as np
from jax import lax
from jax.experimental import pallas as pl
from jax.experimental.pallas import tpu as pltpu
from jax.sharding import PartitionSpec as P

rope_base = 1000000.0
norm_eps = 1e-06


def group_layout(lengths_row, total):
    req_ends = jnp.cumsum(lengths_row)
    req_starts = req_ends - lengths_row
    indices = jnp.arange(total, dtype=jnp.int32)
    segment = jnp.sum((indices[:, None] >= req_ends[None, :]).astype(jnp.int32), axis=1)
    onehot = segment[:, None] == jnp.arange(lengths_row.shape[0], dtype=jnp.int32)[None, :]
    offsets = jnp.sum(jnp.where(onehot, req_starts[None, :], 0), axis=1)
    return (segment, indices - offsets)


def head_norm(values, gain):
    mean_sq = jnp.mean(values * values, axis=-1, keepdims=True)
    return values * lax.rsqrt(mean_sq + norm_eps) * gain


def rotate(values, position):
    half_size = values.shape[-1] // 2
    freqs = rope_base ** (-(jnp.arange(half_size, dtype=jnp.float32) * 2.0 / (2 * half_size)))
    angles = position.astype(jnp.float32)[:, None] * freqs[None, :]
    shaped = (values.shape[0],) + (1,) * (values.ndim - 2) + (half_size,)
    cosine = jnp.cos(angles).reshape(shaped)
    sine = jnp.sin(angles).reshape(shaped)
    first_half = values[..., :half_size]
    second_half = values[..., half_size:]
    return jnp.concatenate(
        [first_half * cosine - second_half * sine, second_half * cosine + first_half * sine],
        axis=-1,
    )


def general(
    q_pre,
    gate_pre,
    k_pre,
    v_pre,
    q_gain,
    k_gain,
    lengths,
    q_new,
    gate_new,
    k_new,
    v_new,
    resid,
    w_out,
    norm_gain,
    w_gate,
    w_up,
    w_down,
):
    tok_rows = q_pre.shape[0]
    tp_count = lax.axis_size("tp")
    tp_index = lax.axis_index("tp")
    head_size = q_gain.shape[0]
    query_heads = gate_pre.shape[1]
    kv_heads = k_pre.shape[1] // head_size
    groups_per = query_heads // kv_heads
    kv_local = kv_heads // tp_count
    req_count = lengths.shape[1]
    score_scale = head_size ** (-0.5)
    segment, position = group_layout(lengths[0], tok_rows * tp_count)
    row_offset = tp_index * tok_rows
    seg_local = lax.dynamic_slice_in_dim(segment, row_offset, tok_rows)
    pos_local = lax.dynamic_slice_in_dim(position, row_offset, tok_rows)
    query_index = row_offset + jnp.arange(tok_rows, dtype=jnp.int32)
    queries = rotate(
        head_norm(q_pre.reshape(tok_rows, query_heads, head_size).astype(jnp.float32), q_gain),
        pos_local,
    )
    queries = queries.astype(jnp.bfloat16).reshape(tok_rows, kv_heads, groups_per, head_size)
    keys = rotate(
        head_norm(k_pre.reshape(tok_rows, kv_heads, head_size).astype(jnp.float32), k_gain),
        pos_local,
    ).astype(jnp.bfloat16)
    values = v_pre.reshape(tok_rows, kv_heads, head_size)

    def key_block(running, key_piece, value_piece, first_row):
        key_count = key_piece.shape[0]
        key_index = first_row + jnp.arange(key_count, dtype=jnp.int32)
        allowed = (seg_local[:, None] == segment[None, :]) & (
            query_index[:, None] >= key_index[None, :]
        )
        scores = (
            jnp.einsum(
                "qkgd,pkd->qkgp",
                queries,
                key_piece.reshape(key_count, kv_heads, head_size),
                preferred_element_type=jnp.float32,
            )
            * score_scale
        )
        weights = jnp.where(allowed[:, None, None, :], jnp.exp(scores), 0.0)
        totals = running[0] + jnp.sum(weights, axis=-1)
        mixed = running[1] + jnp.einsum(
            "qkgp,pkd->qkgd",
            weights.astype(jnp.bfloat16),
            value_piece.reshape(key_count, kv_heads, head_size),
            preferred_element_type=jnp.float32,
        )
        return (totals, mixed)

    start_state = (
        jnp.zeros((tok_rows, kv_heads, groups_per), jnp.float32),
        jnp.zeros((tok_rows, kv_heads, groups_per, head_size), jnp.float32),
    )
    pieces = (
        lax.all_gather(keys.reshape(tok_rows, kv_heads * head_size), "tp", axis=0, tiled=True),
        lax.all_gather(v_pre, "tp", axis=0, tiled=True),
    )
    key_count = pieces[0].shape[0]
    block_rows = 512

    def one_block(number, carried):
        begin_at = number * block_rows
        return key_block(carried, pieces[0], pieces[1], begin_at)

    totals, mixed = lax.fori_loop(0, key_count // block_rows, one_block, start_state)
    gates = jax.nn.sigmoid(gate_pre.astype(jnp.float32)).reshape(tok_rows, kv_heads, groups_per)
    prefill_out = (
        (mixed / totals[..., None] * gates[..., None])
        .astype(jnp.bfloat16)
        .reshape(tok_rows, query_heads * head_size)
    )
    new_queries = rotate(
        head_norm(q_new.reshape(req_count, query_heads, head_size).astype(jnp.float32), q_gain),
        lengths[0],
    )
    new_queries = new_queries.astype(jnp.bfloat16).reshape(
        req_count, kv_heads, groups_per, head_size
    )
    new_keys = rotate(
        head_norm(k_new.reshape(req_count, kv_heads, head_size).astype(jnp.float32), k_gain),
        lengths[0],
    ).astype(jnp.bfloat16)
    new_values = v_new.reshape(req_count, kv_heads, head_size)
    new_gates = jax.nn.sigmoid(gate_new.astype(jnp.float32)).reshape(
        req_count, kv_heads, groups_per
    )
    head_first = tp_index * kv_local
    request_ids = jnp.arange(req_count, dtype=jnp.int32)
    own_queries = lax.dynamic_slice_in_dim(new_queries, head_first, kv_local, 1)
    cache_keys, cache_values = (
        lax.all_to_all(keys, "tp", split_axis=1, concat_axis=0, tiled=True),
        lax.all_to_all(values, "tp", split_axis=1, concat_axis=0, tiled=True),
    )
    scores = (
        jnp.einsum("rkgd,pkd->rkgp", own_queries, cache_keys, preferred_element_type=jnp.float32)
        * score_scale
    )
    owned = segment[None, :] == request_ids[:, None]
    weights = jnp.where(owned[:, None, None, :], jnp.exp(scores), 0.0)
    weighted = jnp.einsum(
        "rkgp,pkd->rkgd",
        weights.astype(jnp.bfloat16),
        cache_values,
        preferred_element_type=jnp.float32,
    )
    dec_totals = jnp.sum(weights, axis=-1)
    dec_mixed = weighted
    own_keys = lax.dynamic_slice_in_dim(new_keys, head_first, kv_local, 1)
    own_values = lax.dynamic_slice_in_dim(new_values, head_first, kv_local, 1)
    own_gates = lax.dynamic_slice_in_dim(new_gates, head_first, kv_local, 1)
    self_weight = jnp.exp(
        jnp.einsum("rkgd,rkd->rkg", own_queries, own_keys, preferred_element_type=jnp.float32)
        * score_scale
    )
    dec_totals = dec_totals + self_weight
    dec_mixed = dec_mixed + self_weight[..., None] * own_values.astype(jnp.float32)[:, :, None, :]
    attended = (
        (dec_mixed / dec_totals[..., None] * own_gates[..., None])
        .astype(jnp.bfloat16)
        .reshape(req_count, kv_local * groups_per * head_size)
    )
    partial_out = jnp.dot(attended, w_out, preferred_element_type=jnp.float32)
    attn_rows = lax.psum(partial_out, "tp")
    hidden_state = resid.astype(jnp.float32) + attn_rows
    mean_sq = jnp.mean(hidden_state * hidden_state, axis=-1, keepdims=True)
    normed = (hidden_state * lax.rsqrt(mean_sq + norm_eps) * norm_gain).astype(jnp.bfloat16)
    units_local = w_gate.shape[1]
    paired = jnp.concatenate([w_gate, w_up], axis=1)
    columns = lax.all_to_all(normed, "req", split_axis=1, concat_axis=0, tiled=True)
    whole_sums = lax.psum(jnp.dot(columns, paired, preferred_element_type=jnp.float32), "req")
    hidden_units = (jax.nn.silu(whole_sums[:, :units_local]) * whole_sums[:, units_local:]).astype(
        jnp.bfloat16
    )
    down_part = jnp.dot(hidden_units, w_down, preferred_element_type=jnp.float32)
    back_part = lax.all_to_all(down_part, "req", split_axis=0, concat_axis=1, tiled=True)
    mlp_rows = lax.psum(back_part, "tp")
    decode_out = (hidden_state + mlp_rows).astype(jnp.bfloat16)
    return (prefill_out, decode_out)


f32 = jnp.float32
bf16 = jnp.bfloat16
lanes = 128
pay_rows = 28
back_rows = 16


def dot(a, b):
    return jnp.dot(a, b, preferred_element_type=f32)


def dot_nt(a, b):
    return lax.dot_general(a, b, (((1,), (1,)), ((), ())), preferred_element_type=f32)


def iota(shape, dim):
    return lax.broadcasted_iota(jnp.int32, shape, dim)


def rope_factors(angles):
    turns = jnp.floor(angles * (2.0 / np.pi) + 0.5)
    rest = angles - turns * 1.5703125
    rest = rest - turns * 4.837512969970703125e-4
    rest = rest - turns * 7.549789948768648e-8
    sq = rest * rest
    sine = ((-1.9515295891e-4 * sq + 8.3321608736e-3) * sq - 1.6666654611e-1) * sq * rest + rest
    cosine = (
        ((2.443315711809948e-5 * sq - 1.388731625493765e-3) * sq + 4.166664568298827e-2) * sq * sq
        - 0.5 * sq
        + 1.0
    )
    low = iota(angles.shape, 1) < lanes // 2
    quarter = turns.astype(jnp.int32) + jnp.where(low, 1, 0)
    both = jnp.where((quarter & 1) == 1, cosine, sine)
    both = jnp.where((quarter & 2) == 2, -both, both)
    swapped = pltpu.roll(both, lanes // 2, 1)
    return jnp.where(low, both, swapped), jnp.where(low, -swapped, both)


def norm_rope(values, gain, factors):
    mean_sq = jnp.mean(values * values, axis=-1, keepdims=True)
    normed = values * lax.rsqrt(mean_sq + norm_eps) * gain
    return (normed * factors[0] + pltpu.roll(normed, lanes // 2, 1) * factors[1]).astype(bf16)


def begin_of(indices, len_ref):
    begin = jnp.zeros_like(indices)
    end = 0
    for j in range(len_ref.shape[1] - 1):
        end = end + len_ref[0, j]
        begin = jnp.where(indices >= end, end, begin)
    return begin


def partial_kernel(
    len_hbm, k_hbm, v_hbm, qn_hbm, kn_hbm, vn_hbm, gn_hbm, resid_hbm, qg_hbm, kg_hbm, freq_hbm,
    w_hbm, gate_hbm, up_hbm, down_hbm,
    kv_hbm, pay_hbm, own_hbm, pair_hbm, down_pair_hbm,
    kv_ref, pay_ref, own_ref, pair_ref, down_pair_ref, row_q, row_k, row_v, row_g, pay, len_ref, k_ref, v_ref, qn_ref, kn_ref, vn_ref, gn_ref,
    resid_ref, qg_ref, kg_ref, freq_ref, sems, out_sems,
):
    tp = lax.axis_index("tp")
    req = lax.axis_index("req")
    z, other = lax.div(req, 2), 1 - lax.rem(req, 2)
    width = own_ref.shape[1]
    units = down_pair_ref.shape[0]
    cols = pl.ds(pl.multiple_of(z * width, lanes), width)
    theirs = pl.ds(pl.multiple_of(other * units, lanes), units)
    moves = (
        (len_hbm, len_ref), (freq_hbm, freq_ref), (k_hbm, k_ref), (kg_hbm, kg_ref),
        (qn_hbm, qn_ref), (kn_hbm, kn_ref), (vn_hbm, vn_ref), (gn_hbm, gn_ref), (qg_hbm, qg_ref),
        (v_hbm, v_ref), (resid_hbm, resid_ref),
        (gate_hbm.at[:, theirs], pair_ref.at[:, pl.ds(0, units)]),
        (up_hbm.at[:, theirs], pair_ref.at[:, pl.ds(units, units)]),
        (w_hbm.at[:, cols], own_ref),
        (down_hbm.at[theirs, :], down_pair_ref),
    )
    copies = [pltpu.make_async_copy(a, b, sems.at[i]) for i, (a, b) in enumerate(moves)]
    for copy in copies:
        copy.start()
    ends = (
        (pair_ref, pair_hbm), (own_ref, own_hbm), (down_pair_ref, down_pair_hbm),
        (kv_ref, kv_hbm), (pay_ref, pay_hbm),
    )
    leave = [pltpu.make_async_copy(a, b, out_sems.at[i]) for i, (a, b) in enumerate(ends)]
    tok = k_ref.shape[0]
    rpg = qn_ref.shape[0]
    heads = qn_ref.shape[1] // lanes
    kvs = k_ref.shape[1] // lanes
    per = heads // kvs
    rows = heads * rpg
    for copy in copies[:2]:
        copy.wait()
    freq = freq_ref[...]
    tok_index = tp * tok + iota((tok, lanes), 0)
    factors = rope_factors((tok_index - begin_of(tok_index, len_ref)).astype(f32) * freq)
    for copy in copies[2:11]:
        copy.wait()
    qg, kg = qg_ref[...], kg_ref[...]
    keys = []
    for k in range(kvs):
        at = slice(k * lanes, (k + 1) * lanes)
        keys.append(norm_rope(k_ref[:, at].astype(f32), kg, factors))
        kv_ref[:, at] = keys[-1]
    kv_ref[:, kvs * lanes :] = v_ref[...]
    for copy in copies[11:]:
        copy.wait()
    for copy in leave[:4]:
        copy.start()
    qn, kn = qn_ref[...].astype(f32), kn_ref[...].astype(f32)
    vn, gn = vn_ref[...].astype(f32), gn_ref[...].astype(f32)
    for h in range(heads):
        at = slice(h * rpg, (h + 1) * rpg)
        kv = slice((h // per) * lanes, (h // per + 1) * lanes)
        row_q[at, :] = qn[:, h * lanes : (h + 1) * lanes]
        row_k[at, :] = kn[:, kv]
        row_v[at, :] = vn[:, kv]
        row_g[at, :] = jnp.broadcast_to(gn[:, h : h + 1], (rpg, lanes))
    row = iota((rows, lanes), 0)
    col = iota((rows, lanes), 1)
    head = row * 0
    for h in range(1, heads):
        head = jnp.where(row >= h * rpg, h, head)
    request = row - head * rpg
    length, first, last = row * 0, row * 0, row * 0
    end = 0
    for j in range(rpg):
        mine = request == j
        length = jnp.where(mine, len_ref[0, j], length)
        first = jnp.where(mine, end, first)
        end = end + len_ref[0, j]
        last = jnp.where(mine, end, last)
    new_factors = rope_factors(length.astype(f32) * freq)
    scale = lanes ** (-0.5)
    new_q = norm_rope(row_q[...], qg, new_factors)
    new_k = norm_rope(row_k[...], kg, new_factors)
    scores = jnp.zeros((rows, tok), f32)
    for k in range(kvs):
        mine = (head >= k * per) & (head < (k + 1) * per)
        scores = jnp.where(mine, dot_nt(new_q, keys[k]), scores)
    index = tp * tok + col
    weights = jnp.where((index >= first) & (index < last), jnp.exp(scores * scale), 0.0)
    totals = jnp.sum(weights, axis=-1, keepdims=True)
    rounded = weights.astype(bf16)
    mixed = jnp.zeros((rows, lanes), f32)
    for k in range(kvs):
        mine = (head >= k * per) & (head < (k + 1) * per)
        mixed = mixed + dot(
            jnp.where(mine, rounded, jnp.zeros_like(rounded)), v_ref[:, k * lanes : (k + 1) * lanes]
        )
    self_score = jnp.sum(new_q.astype(f32) * new_k.astype(f32), axis=-1, keepdims=True)
    self_weight = jnp.where(tp == 0, jnp.exp(self_score * scale), 0.0)
    totals = totals + self_weight
    mixed = (mixed + self_weight * row_v[...]) * jax.nn.sigmoid(row_g[...])
    total_row = jnp.sum(jnp.where(row == col, totals, 0.0), axis=0, keepdims=True)
    high = total_row.astype(bf16).astype(f32)
    rest = pltpu.roll(jnp.broadcast_to(total_row - high, (8, lanes)), lanes // 2, 1)
    pay[0:rows, :] = mixed
    pay[rows + rpg : rows + rpg + 1, :] = jnp.where(
        iota((1, lanes), 1) < lanes // 2, high, rest[0:1, :]
    )
    peers = pay_ref.shape[0]
    tps = lax.axis_size("tp")
    slices = resid_ref.shape[1] // (tps * lanes)
    for z in range(slices):
        at = pl.ds(pl.multiple_of((z * tps + tp) * lanes, lanes), lanes)
        pay[rows : rows + rpg, :] = resid_ref[:, at].astype(f32)
        for g in range(pay_ref.shape[1]):
            out = pay[4 * g : 4 * g + 4, :].astype(bf16)
            for peer in range(z * peers // slices, (z + 1) * peers // slices):
                pay_ref[peer, g] = out
    leave[4].start()
    for copy in leave:
        copy.wait()


def fetch_kernel(gate_hbm, up_hbm, ng_hbm, mine_ref, ng_ref, sems):
    units = mine_ref.shape[1] // 2
    width = ng_ref.shape[1]
    req = lax.axis_index("req")
    at = pl.ds(pl.multiple_of(lax.rem(req, 2) * units, lanes), units)
    cols = pl.ds(pl.multiple_of(lax.div(req, 2) * width, lanes), width)
    copies = (
        pltpu.make_async_copy(gate_hbm.at[:, at], mine_ref.at[:, pl.ds(0, units)], sems.at[0]),
        pltpu.make_async_copy(up_hbm.at[:, at], mine_ref.at[:, pl.ds(units, units)], sems.at[1]),
        pltpu.make_async_copy(ng_hbm.at[:, cols], ng_ref, sems.at[2]),
    )
    for copy in copies:
        copy.start()
    for copy in copies:
        copy.wait()


def columns_kernel(w_hbm, w_ref, sems):
    width = w_ref.shape[1]
    z = lax.div(lax.axis_index("req"), 2)
    copy = pltpu.make_async_copy(
        w_hbm.at[:, pl.ds(pl.multiple_of(z * width, lanes), width)], w_ref, sems.at[0]
    )
    copy.start()
    copy.wait()


def ready_kernel(*refs):
    refs[-1][...] = jnp.zeros_like(refs[-1])


def hidden_kernel(
    pay_ref, w0_ref, w1_ref, w2_ref, w3_ref, mine_ref, pair_ref, ng_ref, _,
    hid_ref, msg_ref, att, hid, xs, acc, out,
):
    tp = lax.axis_index("tp")
    req = lax.axis_index("req")
    tps = lax.axis_size("tp")
    z, y = lax.div(req, 2), lax.rem(req, 2)
    heads, toks, _ = att.shape
    groups = pay_ref.shape[0] // tps
    rpg = toks // groups
    rows = heads * rpg
    diag = iota((rows, lanes), 0) == iota((rows, lanes), 1)
    quads = pay_ref.shape[1]
    for r in range(groups):
        for g in range(quads):
            total = jnp.zeros((4, lanes), f32)
            for t in range(tps):
                piece = pay_ref[r * tps + t, g].astype(f32)
                total = total + piece
                if g == quads - 1:
                    hid[r * rpg : (r + 1) * rpg, t * lanes : (t + 1) * lanes] = piece[:rpg, :]
            acc[r, 4 * g : 4 * g + 4, :] = total
    for r in range(groups):
        total_row = jnp.broadcast_to(acc[r, pay_rows - 1 : pay_rows, :], (rows, lanes))
        total_row = total_row + pltpu.roll(total_row, lanes // 2, 1)
        totals = jnp.sum(jnp.where(diag, total_row, 0.0), axis=-1, keepdims=True)
        acc[r, 0:rows, :] = acc[r, 0:rows, :] / totals
    for r in range(groups):
        for h in range(heads):
            att[h, r * rpg : (r + 1) * rpg, :] = acc[r, h * rpg : (h + 1) * rpg, :]
    state = hid[...]
    per = heads // tps
    for d, w_ref in enumerate((w0_ref, w1_ref, w2_ref, w3_ref)):
        source = tp ^ d
        for j in range(per):
            state = state + dot(
                att[source * per + j].astype(bf16), w_ref[j * lanes : (j + 1) * lanes, :]
            )
    hid_ref[...] = state
    width = state.shape[1]
    half = width // 2
    sums = jnp.sum(state * state, axis=-1, keepdims=True)
    scaled = state * ng_ref[...]
    xs[0] = scaled[:, :half]
    xs[1] = scaled[:, half:]
    own, other = xs[y].astype(bf16), xs[1 - y].astype(bf16)
    units = pair_ref.shape[1] // 2
    gate = dot(own, mine_ref[:, :units]) + dot(other, pair_ref[:, :units])
    up = dot(own, mine_ref[:, units:]) + dot(other, pair_ref[:, units:])
    square = iota((toks, lanes), 0) == iota((toks, lanes), 1)
    sums_row = jnp.sum(jnp.where(square, sums, 0.0), axis=0, keepdims=True)
    high = sums_row.astype(bf16).astype(f32)
    blocks = units // lanes
    for i in range(blocks):
        at = slice(i * lanes, (i + 1) * lanes)
        out[i * toks : (i + 1) * toks, :] = gate[:, at]
        out[(blocks + i) * toks : (blocks + i + 1) * toks, :] = up[:, at]
    base = 2 * blocks * toks
    first = iota((8, lanes), 0)
    out[base : base + 8, :] = jnp.where(
        first == 0, high, jnp.where(first == 1, sums_row - high, 0.0)
    )
    msg_ref[...] = out[...].astype(bf16)


def down_kernel(m0_ref, m1_ref, m2_ref, m3_ref, hid_ref, down_ref, pair_ref, back_ref, part, pay, whole):
    tp = lax.axis_index("tp")
    tps = lax.axis_size("tp")
    y = lax.rem(lax.axis_index("req"), 2)
    units, half = pair_ref.shape
    toks, width = hid_ref.shape
    total = m0_ref[...].astype(f32)
    for m_ref in (m1_ref, m2_ref, m3_ref):
        total = total + m_ref[...].astype(f32)
    whole[...] = total
    blocks = units // lanes
    base = 2 * blocks * toks
    square = iota((toks, lanes), 0) == iota((toks, lanes), 1)
    sums_row = whole[base : base + 1, :] + whole[base + 1 : base + 2, :]
    sums = jnp.sum(
        jnp.where(square, jnp.broadcast_to(sums_row, (toks, lanes)), 0.0), axis=-1, keepdims=True
    )
    factor = lax.rsqrt(sums / (width * 4) + norm_eps)
    pieces = []
    for i in range(blocks):
        gate = whole[i * toks : (i + 1) * toks, :] * factor
        up = whole[(blocks + i) * toks : (blocks + i + 1) * toks, :] * factor
        pieces.append((gate / (1.0 + jnp.exp(-gate)) * up).astype(bf16))
    hidden = jnp.concatenate(pieces, axis=1)
    own_rows = pl.ds(pl.multiple_of(y * units, lanes), units)
    part[y] = dot(hidden, down_ref[own_rows, :])
    part[1 - y] = dot(hidden, pair_ref[...])
    chunks = width // lanes
    groups = pay.shape[0]
    rpg = toks // groups
    piece = hid_ref[:, pl.ds(pl.multiple_of(tp * lanes, lanes), lanes)]
    high = piece.astype(bf16).astype(f32)
    piece = jnp.where(y == 0, high, piece - high)
    pay[...] = jnp.zeros_like(pay)
    for c in range(chunks + 1):
        if c < chunks:
            at = (c * lanes) % half
            block = part[c * lanes // half][:, at : at + lanes]
        else:
            block = piece
        for r in range(groups):
            pay[r, c * rpg : (c + 1) * rpg, :] = block[r * rpg : (r + 1) * rpg, :]
    for r in range(groups):
        out = pay[r].astype(bf16)
        for t in range(tps):
            back_ref[r * tps + t] = out


def final_kernel(back_ref, out_ref, acc, tail, rows_out):
    tps = lax.axis_size("tp")
    peers = back_ref.shape[0]
    rpg, width = out_ref.shape
    chunks = tps
    slices = width // (chunks * lanes)
    group = peers // slices
    for z in range(slices):
        total = jnp.zeros(acc.shape, f32)
        by_tp = [jnp.zeros(acc.shape, f32) for _ in range(tps)]
        for p in range(group):
            piece = back_ref[z * group + p].astype(f32)
            total = total + piece
            by_tp[p % tps] = by_tp[p % tps] + piece
        acc[...] = total
        for c in range(chunks):
            tail[...] = by_tp[c]
            at = slice((z * chunks + c) * lanes, (z * chunks + c + 1) * lanes)
            rows_out[0:rpg, at] = (
                acc[c * rpg : (c + 1) * rpg, :] + tail[chunks * rpg : (chunks + 1) * rpg, :]
            )
    out_ref[...] = rows_out[0:rpg, :].astype(bf16)


def prefill_kernel(
    len_ref, q_ref, g_ref, kv0_ref, kv1_ref, kv2_ref, kv3_ref, qg_ref, freq_ref, out_ref, mid_ref
):
    tp = lax.axis_index("tp")
    tok = q_ref.shape[0]
    heads = q_ref.shape[1] // lanes
    kvs = kv0_ref.shape[1] // (2 * lanes)
    per = heads // kvs
    third = tp == 2
    mid_ref[...] = jnp.where(third, kv3_ref[...], kv1_ref[...])
    blocks = ((tp, kv0_ref), (jnp.where(third, tp ^ 3, tp ^ 1), mid_ref), (tp ^ 2, kv2_ref))
    tok_index = tp * tok + iota((tok, lanes), 0)
    begin = begin_of(tok_index, len_ref)
    factors = rope_factors((tok_index - begin).astype(f32) * freq_ref[...])
    col = iota((tok, tok), 1)
    allowed = []
    for block, _ in blocks:
        key_index = block * tok + col
        allowed.append((key_index >= begin) & (key_index <= tok_index))
    gates = jax.nn.sigmoid(g_ref[...].astype(f32))
    qg = qg_ref[...]
    scale = lanes ** (-0.5)
    for h in range(heads):
        k = h // per
        at = slice(h * lanes, (h + 1) * lanes)
        query = norm_rope(q_ref[:, at].astype(f32), qg, factors)
        totals = jnp.zeros((tok, 1), f32)
        mixed = jnp.zeros((tok, lanes), f32)
        for b, (_, kv_ref) in enumerate(blocks):
            scores = dot_nt(query, kv_ref[:, k * lanes : (k + 1) * lanes])
            weights = jnp.where(allowed[b], jnp.exp(scores * scale), 0.0)
            totals = totals + jnp.sum(weights, axis=-1, keepdims=True)
            mixed = mixed + dot(
                weights.astype(bf16), kv_ref[:, (kvs + k) * lanes : (kvs + k + 1) * lanes]
            )
        out_ref[:, at] = (mixed / totals * gates[:, h : h + 1]).astype(bf16)


def call(body, out_shape, args, scratch=(), hbm=False, out_any=False, smem=0, flops=0, limit=12):
    specs = [pl.BlockSpec(memory_space=pltpu.SMEM)] * smem
    space = pltpu.HBM if hbm else pltpu.VMEM
    specs += [pl.BlockSpec(memory_space=space)] * (len(args) - smem)
    size = sum(a.size * a.dtype.itemsize for a in args)
    return pl.pallas_call(
        body,
        out_shape=out_shape,
        in_specs=specs,
        out_specs=jax.tree.map(
            lambda _: pl.BlockSpec(memory_space=pl.ANY if out_any else pltpu.VMEM), out_shape
        ),
        scratch_shapes=[pltpu.VMEM(s, f32) if isinstance(s, tuple) else s for s in scratch],
        compiler_params=pltpu.CompilerParams(vmem_limit_bytes=limit * 2**20),
        cost_estimate=pl.CostEstimate(flops=flops, bytes_accessed=size, transcendentals=0),
    )(*args)


def hold(arrays, flops):
    return pl.pallas_call(
        ready_kernel,
        out_shape=jax.ShapeDtypeStruct((8, lanes), f32),
        in_specs=[pl.BlockSpec(memory_space=pl.ANY)] * len(arrays),
        out_specs=pl.BlockSpec(memory_space=pltpu.VMEM),
        compiler_params=pltpu.CompilerParams(vmem_limit_bytes=2**20),
        cost_estimate=pl.CostEstimate(flops=flops, bytes_accessed=0, transcendentals=0),
    )(*arrays)


def local(
    q_pre,
    gate_pre,
    k_pre,
    v_pre,
    q_gain,
    k_gain,
    lengths,
    q_new,
    gate_new,
    k_new,
    v_new,
    resid,
    w_out,
    norm_gain,
    w_gate,
    w_up,
    w_down,
):
    tps, reqs = lax.axis_size("tp"), lax.axis_size("req")
    tok = q_pre.shape[0]
    rpg, width = resid.shape
    slices = reqs // 2
    head_size = q_gain.shape[0]
    heads = gate_pre.shape[1]
    part = width // slices if slices else 0
    if not (slices == 4 and tps == 4 and head_size == lanes == tok and part == tps * lanes):
        return general(
            q_pre, gate_pre, k_pre, v_pre, q_gain, k_gain, lengths, q_new, gate_new, k_new, v_new,
            resid, w_out, norm_gain, w_gate, w_up, w_down,
        )
    peers = tps * reqs
    toks = rpg * reqs
    units = w_gate.shape[1] // 2
    req = lax.axis_index("req")
    z, y = req // 2, req % 2
    freqs = rope_base ** (-(np.arange(head_size // 2) * 2.0 / head_size))
    freqs = jnp.asarray(np.concatenate([freqs, freqs])[None, :], f32)
    qg, kg = q_gain[None, :], k_gain[None, :]

    def cross(array, by):
        return lax.ppermute(array, "tp", [(i, i ^ by) for i in range(tps)])

    def swap(array):
        return lax.ppermute(array, "req", [(i, i ^ 1) for i in range(reqs)])

    def along(array, by):
        return lax.ppermute(array, "req", [(i, i ^ (2 * by)) for i in range(reqs)])

    inputs = (
        lengths, k_pre, v_pre, q_new, k_new, v_new, gate_new, resid, qg, kg, freqs,
        w_out, w_gate, w_up, w_down,
    )
    outputs = (
        jax.ShapeDtypeStruct((tok, 2 * k_pre.shape[1]), bf16),
        jax.ShapeDtypeStruct((peers, pay_rows // 4, 4, lanes), bf16),
        jax.ShapeDtypeStruct((w_out.shape[0], part), bf16),
        jax.ShapeDtypeStruct((w_gate.shape[0], 2 * units), bf16),
        jax.ShapeDtypeStruct((units, w_down.shape[1]), bf16),
    )
    kv, pay, w_own, pair, down_pair = call(
        partial_kernel,
        outputs,
        inputs,
        scratch=[pltpu.VMEM(o.shape, o.dtype) for o in outputs]
        + [(heads * rpg, lanes)] * 4
        + [(pay_rows, lanes), pltpu.SMEM(lengths.shape, jnp.int32)]
        + [pltpu.VMEM(a.shape, a.dtype) for a in inputs[1:11]]
        + [pltpu.SemaphoreType.DMA((len(inputs),)), pltpu.SemaphoreType.DMA((len(outputs),))],
        hbm=True,
        out_any=True,
        flops=10**7,
        limit=56,
    )
    w_far = cross(w_own, 2)
    pair = swap(pair)
    half = jax.ShapeDtypeStruct((w_gate.shape[0], 2 * units), bf16)
    mine, ng = call(
        fetch_kernel,
        (half, jax.ShapeDtypeStruct((1, part), f32)),
        (w_gate, w_up, norm_gain[None, :]),
        hbm=True,
        scratch=[pltpu.SemaphoreType.DMA((3,))],
    )
    w_here = call(
        columns_kernel,
        jax.ShapeDtypeStruct(w_own.shape, bf16),
        (w_out,),
        hbm=True,
        scratch=[pltpu.SemaphoreType.DMA((1,))],
    )
    late_far, _, _ = lax.optimization_barrier((w_far, mine, w_here))
    w_near, w_both = cross(w_own, 1), cross(late_far, 1)
    kv_near = cross(kv, 1)
    late_kv, _ = lax.optimization_barrier((kv, w_far))
    kv_far = cross(late_kv, 2)
    late_down, _ = lax.optimization_barrier((down_pair, w_far))
    down_pair = swap(late_down)
    got = lax.all_to_all(pay, ("req", "tp"), 0, 0, tiled=True)
    landed = hold((pair,), 2 * 10**9)
    token = hold((landed, w_near, w_both), 10**9)
    msg_shape = (2 * units // lanes * toks + 8, lanes)
    hid, msg = call(
        hidden_kernel,
        (
            jax.ShapeDtypeStruct((toks, part), f32),
            jax.ShapeDtypeStruct(msg_shape, bf16),
        ),
        (got, w_here, w_near, w_far, w_both, mine, pair, ng, token),
        scratch=[
            (heads, toks, lanes),
            (toks, part),
            (2, toks, part // 2),
            (reqs, pay_rows, lanes),
            msg_shape,
        ],
        flops=10**7,
    )
    msgs = [msg] + [along(msg, d) for d in (3, 2, 1)]
    kv_both = cross(kv_far, 1)
    prefill_out = call(
        prefill_kernel,
        jax.ShapeDtypeStruct(q_pre.shape, bf16),
        (lengths, q_pre, gate_pre, kv, kv_near, kv_far, kv_both, qg, freqs),
        scratch=[pltpu.VMEM(kv.shape, bf16)],
        smem=1,
        flops=10**9,
    )
    back = call(
        down_kernel,
        jax.ShapeDtypeStruct((peers, back_rows, lanes), bf16),
        (*msgs, hid, w_down, down_pair),
        scratch=[(2, toks, part // 2), (reqs, back_rows, lanes), msg_shape],
        flops=3 * 10**9,
    )
    returned = lax.all_to_all(back, ("req", "tp"), 0, 0, tiled=True)
    returned, prefill_out = lax.optimization_barrier((returned, prefill_out))
    decode_out = call(
        final_kernel,
        jax.ShapeDtypeStruct((rpg, width), bf16),
        (returned,),
        scratch=[(back_rows, lanes), (back_rows, lanes), (8, width)],
        flops=10**6,
    )
    return (prefill_out, decode_out)


def solution(mesh):
    return jax.shard_map(
        local,
        mesh=mesh,
        in_specs=(
            P(("req", "tp"), None),
            P(("req", "tp"), None),
            P(("req", "tp"), None),
            P(("req", "tp"), None),
            P(),
            P(),
            P("req", None),
            P("req", None),
            P("req", None),
            P("req", None),
            P("req", None),
            P("req", None),
            P("tp", None),
            P(),
            P("req", "tp"),
            P("req", "tp"),
            P("tp", "req"),
        ),
        out_specs=(P(("req", "tp"), None), P("req", None)),
        check_vma=False,
    )
```

```python
import jax
import jax.numpy as jnp
import numpy as np
from jax import lax
from jax.experimental import pallas as pl
from jax.experimental.pallas import tpu as pltpu
from jax.sharding import PartitionSpec as P

rope_base = 1000000.0
norm_eps = 1e-06


def group_layout(lengths_row, total):
    req_ends = jnp.cumsum(lengths_row)
    req_starts = req_ends - lengths_row
    indices = jnp.arange(total, dtype=jnp.int32)
    segment = jnp.sum((indices[:, None] >= req_ends[None, :]).astype(jnp.int32), axis=1)
    onehot = segment[:, None] == jnp.arange(lengths_row.shape[0], dtype=jnp.int32)[None, :]
    offsets = jnp.sum(jnp.where(onehot, req_starts[None, :], 0), axis=1)
    return (segment, indices - offsets)


def head_norm(values, gain):
    mean_sq = jnp.mean(values * values, axis=-1, keepdims=True)
    return values * lax.rsqrt(mean_sq + norm_eps) * gain


def rotate(values, position):
    half_size = values.shape[-1] // 2
    freqs = rope_base ** (-(jnp.arange(half_size, dtype=jnp.float32) * 2.0 / (2 * half_size)))
    angles = position.astype(jnp.float32)[:, None] * freqs[None, :]
    shaped = (values.shape[0],) + (1,) * (values.ndim - 2) + (half_size,)
    cosine = jnp.cos(angles).reshape(shaped)
    sine = jnp.sin(angles).reshape(shaped)
    first_half = values[..., :half_size]
    second_half = values[..., half_size:]
    return jnp.concatenate(
        [first_half * cosine - second_half * sine, second_half * cosine + first_half * sine],
        axis=-1,
    )


def general(
    q_pre,
    gate_pre,
    k_pre,
    v_pre,
    q_gain,
    k_gain,
    lengths,
    q_new,
    gate_new,
    k_new,
    v_new,
    resid,
    w_out,
    norm_gain,
    w_gate,
    w_up,
    w_down,
):
    tok_rows = q_pre.shape[0]
    tp_count = lax.axis_size("tp")
    tp_index = lax.axis_index("tp")
    head_size = q_gain.shape[0]
    query_heads = gate_pre.shape[1]
    kv_heads = k_pre.shape[1] // head_size
    groups_per = query_heads // kv_heads
    kv_local = kv_heads // tp_count
    req_count = lengths.shape[1]
    score_scale = head_size ** (-0.5)
    segment, position = group_layout(lengths[0], tok_rows * tp_count)
    row_offset = tp_index * tok_rows
    seg_local = lax.dynamic_slice_in_dim(segment, row_offset, tok_rows)
    pos_local = lax.dynamic_slice_in_dim(position, row_offset, tok_rows)
    query_index = row_offset + jnp.arange(tok_rows, dtype=jnp.int32)
    queries = rotate(
        head_norm(q_pre.reshape(tok_rows, query_heads, head_size).astype(jnp.float32), q_gain),
        pos_local,
    )
    queries = queries.astype(jnp.bfloat16).reshape(tok_rows, kv_heads, groups_per, head_size)
    keys = rotate(
        head_norm(k_pre.reshape(tok_rows, kv_heads, head_size).astype(jnp.float32), k_gain),
        pos_local,
    ).astype(jnp.bfloat16)
    values = v_pre.reshape(tok_rows, kv_heads, head_size)

    def key_block(running, key_piece, value_piece, first_row):
        key_count = key_piece.shape[0]
        key_index = first_row + jnp.arange(key_count, dtype=jnp.int32)
        allowed = (seg_local[:, None] == segment[None, :]) & (
            query_index[:, None] >= key_index[None, :]
        )
        scores = (
            jnp.einsum(
                "qkgd,pkd->qkgp",
                queries,
                key_piece.reshape(key_count, kv_heads, head_size),
                preferred_element_type=jnp.float32,
            )
            * score_scale
        )
        weights = jnp.where(allowed[:, None, None, :], jnp.exp(scores), 0.0)
        totals = running[0] + jnp.sum(weights, axis=-1)
        mixed = running[1] + jnp.einsum(
            "qkgp,pkd->qkgd",
            weights.astype(jnp.bfloat16),
            value_piece.reshape(key_count, kv_heads, head_size),
            preferred_element_type=jnp.float32,
        )
        return (totals, mixed)

    start_state = (
        jnp.zeros((tok_rows, kv_heads, groups_per), jnp.float32),
        jnp.zeros((tok_rows, kv_heads, groups_per, head_size), jnp.float32),
    )
    pieces = (
        lax.all_gather(keys.reshape(tok_rows, kv_heads * head_size), "tp", axis=0, tiled=True),
        lax.all_gather(v_pre, "tp", axis=0, tiled=True),
    )
    key_count = pieces[0].shape[0]
    block_rows = 512

    def one_block(number, carried):
        begin_at = number * block_rows
        return key_block(carried, pieces[0], pieces[1], begin_at)

    totals, mixed = lax.fori_loop(0, key_count // block_rows, one_block, start_state)
    gates = jax.nn.sigmoid(gate_pre.astype(jnp.float32)).reshape(tok_rows, kv_heads, groups_per)
    prefill_out = (
        (mixed / totals[..., None] * gates[..., None])
        .astype(jnp.bfloat16)
        .reshape(tok_rows, query_heads * head_size)
    )
    new_queries = rotate(
        head_norm(q_new.reshape(req_count, query_heads, head_size).astype(jnp.float32), q_gain),
        lengths[0],
    )
    new_queries = new_queries.astype(jnp.bfloat16).reshape(
        req_count, kv_heads, groups_per, head_size
    )
    new_keys = rotate(
        head_norm(k_new.reshape(req_count, kv_heads, head_size).astype(jnp.float32), k_gain),
        lengths[0],
    ).astype(jnp.bfloat16)
    new_values = v_new.reshape(req_count, kv_heads, head_size)
    new_gates = jax.nn.sigmoid(gate_new.astype(jnp.float32)).reshape(
        req_count, kv_heads, groups_per
    )
    head_first = tp_index * kv_local
    request_ids = jnp.arange(req_count, dtype=jnp.int32)
    own_queries = lax.dynamic_slice_in_dim(new_queries, head_first, kv_local, 1)
    cache_keys, cache_values = (
        lax.all_to_all(keys, "tp", split_axis=1, concat_axis=0, tiled=True),
        lax.all_to_all(values, "tp", split_axis=1, concat_axis=0, tiled=True),
    )
    scores = (
        jnp.einsum("rkgd,pkd->rkgp", own_queries, cache_keys, preferred_element_type=jnp.float32)
        * score_scale
    )
    owned = segment[None, :] == request_ids[:, None]
    weights = jnp.where(owned[:, None, None, :], jnp.exp(scores), 0.0)
    weighted = jnp.einsum(
        "rkgp,pkd->rkgd",
        weights.astype(jnp.bfloat16),
        cache_values,
        preferred_element_type=jnp.float32,
    )
    dec_totals = jnp.sum(weights, axis=-1)
    dec_mixed = weighted
    own_keys = lax.dynamic_slice_in_dim(new_keys, head_first, kv_local, 1)
    own_values = lax.dynamic_slice_in_dim(new_values, head_first, kv_local, 1)
    own_gates = lax.dynamic_slice_in_dim(new_gates, head_first, kv_local, 1)
    self_weight = jnp.exp(
        jnp.einsum("rkgd,rkd->rkg", own_queries, own_keys, preferred_element_type=jnp.float32)
        * score_scale
    )
    dec_totals = dec_totals + self_weight
    dec_mixed = dec_mixed + self_weight[..., None] * own_values.astype(jnp.float32)[:, :, None, :]
    attended = (
        (dec_mixed / dec_totals[..., None] * own_gates[..., None])
        .astype(jnp.bfloat16)
        .reshape(req_count, kv_local * groups_per * head_size)
    )
    partial_out = jnp.dot(attended, w_out, preferred_element_type=jnp.float32)
    attn_rows = lax.psum(partial_out, "tp")
    hidden_state = resid.astype(jnp.float32) + attn_rows
    mean_sq = jnp.mean(hidden_state * hidden_state, axis=-1, keepdims=True)
    normed = (hidden_state * lax.rsqrt(mean_sq + norm_eps) * norm_gain).astype(jnp.bfloat16)
    units_local = w_gate.shape[1]
    paired = jnp.concatenate([w_gate, w_up], axis=1)
    columns = lax.all_to_all(normed, "req", split_axis=1, concat_axis=0, tiled=True)
    whole_sums = lax.psum(jnp.dot(columns, paired, preferred_element_type=jnp.float32), "req")
    hidden_units = (jax.nn.silu(whole_sums[:, :units_local]) * whole_sums[:, units_local:]).astype(
        jnp.bfloat16
    )
    down_part = jnp.dot(hidden_units, w_down, preferred_element_type=jnp.float32)
    back_part = lax.all_to_all(down_part, "req", split_axis=0, concat_axis=1, tiled=True)
    mlp_rows = lax.psum(back_part, "tp")
    decode_out = (hidden_state + mlp_rows).astype(jnp.bfloat16)
    return (prefill_out, decode_out)


f32 = jnp.float32
bf16 = jnp.bfloat16
lanes = 128
pay_rows = 28
back_rows = 12


def dot(a, b):
    return jnp.dot(a, b, preferred_element_type=f32)


def dot_nt(a, b):
    return lax.dot_general(a, b, (((1,), (1,)), ((), ())), preferred_element_type=f32)


def iota(shape, dim):
    return lax.broadcasted_iota(jnp.int32, shape, dim)


def rope_factors(angles):
    turns = jnp.floor(angles * (2.0 / np.pi) + 0.5)
    rest = angles - turns * 1.5703125
    rest = rest - turns * 4.837512969970703125e-4
    rest = rest - turns * 7.549789948768648e-8
    sq = rest * rest
    sine = ((-1.9515295891e-4 * sq + 8.3321608736e-3) * sq - 1.6666654611e-1) * sq * rest + rest
    cosine = (
        ((2.443315711809948e-5 * sq - 1.388731625493765e-3) * sq + 4.166664568298827e-2) * sq * sq
        - 0.5 * sq
        + 1.0
    )
    low = iota(angles.shape, 1) < lanes // 2
    quarter = turns.astype(jnp.int32) + jnp.where(low, 1, 0)
    both = jnp.where((quarter & 1) == 1, cosine, sine)
    both = jnp.where((quarter & 2) == 2, -both, both)
    swapped = pltpu.roll(both, lanes // 2, 1)
    return jnp.where(low, both, swapped), jnp.where(low, -swapped, both)


def norm_rope(values, gain, factors):
    mean_sq = jnp.mean(values * values, axis=-1, keepdims=True)
    normed = values * lax.rsqrt(mean_sq + norm_eps) * gain
    return (normed * factors[0] + pltpu.roll(normed, lanes // 2, 1) * factors[1]).astype(bf16)


def begin_of(indices, len_ref):
    begin = jnp.zeros_like(indices)
    end = 0
    for j in range(len_ref.shape[1] - 1):
        end = end + len_ref[0, j]
        begin = jnp.where(indices >= end, end, begin)
    return begin


def partial_kernel(
    len_hbm, k_hbm, v_hbm, qn_hbm, kn_hbm, vn_hbm, gn_hbm, resid_hbm, qg_hbm, kg_hbm, freq_hbm,
    w_hbm, gate_hbm, up_hbm, down_hbm,
    kv_hbm, pay_hbm, own_hbm, pair_hbm, down_pair_hbm,
    kv_ref, pay_ref, own_ref, pair_ref, down_pair_ref, row_q, row_k, row_v, row_g, pay, len_ref, k_ref, v_ref, qn_ref, kn_ref, vn_ref, gn_ref,
    resid_ref, qg_ref, kg_ref, freq_ref, sems, out_sems,
):
    tp = lax.axis_index("tp")
    req = lax.axis_index("req")
    z, other = lax.div(req, 2), 1 - lax.rem(req, 2)
    width = own_ref.shape[1]
    units = down_pair_ref.shape[0]
    cols = pl.ds(pl.multiple_of(z * width, lanes), width)
    theirs = pl.ds(pl.multiple_of(other * units, lanes), units)
    moves = (
        (len_hbm, len_ref), (freq_hbm, freq_ref), (k_hbm, k_ref), (kg_hbm, kg_ref),
        (qn_hbm, qn_ref), (kn_hbm, kn_ref), (vn_hbm, vn_ref), (gn_hbm, gn_ref), (qg_hbm, qg_ref),
        (v_hbm, v_ref), (resid_hbm, resid_ref),
        (gate_hbm.at[:, theirs], pair_ref.at[:, pl.ds(0, units)]),
        (up_hbm.at[:, theirs], pair_ref.at[:, pl.ds(units, units)]),
        (w_hbm.at[:, cols], own_ref),
        (down_hbm.at[theirs, :], down_pair_ref),
    )
    copies = [pltpu.make_async_copy(a, b, sems.at[i]) for i, (a, b) in enumerate(moves)]
    for copy in copies:
        copy.start()
    ends = (
        (pair_ref, pair_hbm), (own_ref, own_hbm), (down_pair_ref, down_pair_hbm),
        (kv_ref, kv_hbm), (pay_ref, pay_hbm),
    )
    leave = [pltpu.make_async_copy(a, b, out_sems.at[i]) for i, (a, b) in enumerate(ends)]
    tok = k_ref.shape[0]
    rpg = qn_ref.shape[0]
    heads = qn_ref.shape[1] // lanes
    kvs = k_ref.shape[1] // lanes
    per = heads // kvs
    rows = heads * rpg
    for copy in copies[:2]:
        copy.wait()
    freq = freq_ref[...]
    tok_index = tp * tok + iota((tok, lanes), 0)
    factors = rope_factors((tok_index - begin_of(tok_index, len_ref)).astype(f32) * freq)
    for copy in copies[2:11]:
        copy.wait()
    qg, kg = qg_ref[...], kg_ref[...]
    keys = []
    for k in range(kvs):
        at = slice(k * lanes, (k + 1) * lanes)
        keys.append(norm_rope(k_ref[:, at].astype(f32), kg, factors))
        kv_ref[:, at] = keys[-1]
    kv_ref[:, kvs * lanes :] = v_ref[...]
    for copy in copies[11:]:
        copy.wait()
    for copy in leave[:4]:
        copy.start()
    qn, kn = qn_ref[...].astype(f32), kn_ref[...].astype(f32)
    vn, gn = vn_ref[...].astype(f32), gn_ref[...].astype(f32)
    for h in range(heads):
        at = slice(h * rpg, (h + 1) * rpg)
        kv = slice((h // per) * lanes, (h // per + 1) * lanes)
        row_q[at, :] = qn[:, h * lanes : (h + 1) * lanes]
        row_k[at, :] = kn[:, kv]
        row_v[at, :] = vn[:, kv]
        row_g[at, :] = jnp.broadcast_to(gn[:, h : h + 1], (rpg, lanes))
    row = iota((rows, lanes), 0)
    col = iota((rows, lanes), 1)
    head = row * 0
    for h in range(1, heads):
        head = jnp.where(row >= h * rpg, h, head)
    request = row - head * rpg
    length, first, last = row * 0, row * 0, row * 0
    end = 0
    for j in range(rpg):
        mine = request == j
        length = jnp.where(mine, len_ref[0, j], length)
        first = jnp.where(mine, end, first)
        end = end + len_ref[0, j]
        last = jnp.where(mine, end, last)
    new_factors = rope_factors(length.astype(f32) * freq)
    scale = lanes ** (-0.5)
    new_q = norm_rope(row_q[...], qg, new_factors)
    new_k = norm_rope(row_k[...], kg, new_factors)
    scores = jnp.zeros((rows, tok), f32)
    for k in range(kvs):
        mine = (head >= k * per) & (head < (k + 1) * per)
        scores = jnp.where(mine, dot_nt(new_q, keys[k]), scores)
    index = tp * tok + col
    weights = jnp.where((index >= first) & (index < last), jnp.exp(scores * scale), 0.0)
    totals = jnp.sum(weights, axis=-1, keepdims=True)
    rounded = weights.astype(bf16)
    mixed = jnp.zeros((rows, lanes), f32)
    for k in range(kvs):
        mine = (head >= k * per) & (head < (k + 1) * per)
        mixed = mixed + dot(
            jnp.where(mine, rounded, jnp.zeros_like(rounded)), v_ref[:, k * lanes : (k + 1) * lanes]
        )
    self_score = jnp.sum(new_q.astype(f32) * new_k.astype(f32), axis=-1, keepdims=True)
    self_weight = jnp.where(tp == 0, jnp.exp(self_score * scale), 0.0)
    totals = totals + self_weight
    mixed = (mixed + self_weight * row_v[...]) * jax.nn.sigmoid(row_g[...])
    total_row = jnp.sum(jnp.where(row == col, totals, 0.0), axis=0, keepdims=True)
    high = total_row.astype(bf16).astype(f32)
    rest = pltpu.roll(jnp.broadcast_to(total_row - high, (8, lanes)), lanes // 2, 1)
    pay[0:rows, :] = mixed
    pay[rows + rpg : rows + rpg + 1, :] = jnp.where(
        iota((1, lanes), 1) < lanes // 2, high, rest[0:1, :]
    )
    peers = pay_ref.shape[0]
    tps = lax.axis_size("tp")
    slices = resid_ref.shape[1] // (tps * lanes)
    for z in range(slices):
        at = pl.ds(pl.multiple_of((z * tps + tp) * lanes, lanes), lanes)
        pay[rows : rows + rpg, :] = resid_ref[:, at].astype(f32)
        for g in range(pay_ref.shape[1]):
            out = pay[4 * g : 4 * g + 4, :].astype(bf16)
            for peer in range(z * peers // slices, (z + 1) * peers // slices):
                pay_ref[peer, g] = out
    leave[4].start()
    for copy in leave:
        copy.wait()


def fetch_kernel(gate_hbm, up_hbm, ng_hbm, mine_ref, ng_ref, sems):
    units = mine_ref.shape[1] // 2
    width = ng_ref.shape[1]
    req = lax.axis_index("req")
    at = pl.ds(pl.multiple_of(lax.rem(req, 2) * units, lanes), units)
    cols = pl.ds(pl.multiple_of(lax.div(req, 2) * width, lanes), width)
    copies = (
        pltpu.make_async_copy(gate_hbm.at[:, at], mine_ref.at[:, pl.ds(0, units)], sems.at[0]),
        pltpu.make_async_copy(up_hbm.at[:, at], mine_ref.at[:, pl.ds(units, units)], sems.at[1]),
        pltpu.make_async_copy(ng_hbm.at[:, cols], ng_ref, sems.at[2]),
    )
    for copy in copies:
        copy.start()
    for copy in copies:
        copy.wait()


def columns_kernel(w_hbm, w_ref, sems):
    width = w_ref.shape[1]
    z = lax.div(lax.axis_index("req"), 2)
    copy = pltpu.make_async_copy(
        w_hbm.at[:, pl.ds(pl.multiple_of(z * width, lanes), width)], w_ref, sems.at[0]
    )
    copy.start()
    copy.wait()


def ready_kernel(*refs):
    refs[-1][...] = jnp.zeros_like(refs[-1])


def hidden_kernel(
    pay_ref, w0_ref, w1_ref, w2_ref, w3_ref, mine_ref, pair_ref, ng_ref, _,
    hid_ref, msg_ref, att, hid, xs, acc, out,
):
    tp = lax.axis_index("tp")
    req = lax.axis_index("req")
    tps = lax.axis_size("tp")
    z, y = lax.div(req, 2), lax.rem(req, 2)
    heads, toks, _ = att.shape
    groups = pay_ref.shape[0] // tps
    rpg = toks // groups
    rows = heads * rpg
    diag = iota((rows, lanes), 0) == iota((rows, lanes), 1)
    quads = pay_ref.shape[1]
    for r in range(groups):
        for g in range(quads):
            total = jnp.zeros((4, lanes), f32)
            for t in range(tps):
                piece = pay_ref[r * tps + t, g].astype(f32)
                total = total + piece
                if g == quads - 1:
                    hid[r * rpg : (r + 1) * rpg, t * lanes : (t + 1) * lanes] = piece[:rpg, :]
            acc[r, 4 * g : 4 * g + 4, :] = total
    for r in range(groups):
        total_row = jnp.broadcast_to(acc[r, pay_rows - 1 : pay_rows, :], (rows, lanes))
        total_row = total_row + pltpu.roll(total_row, lanes // 2, 1)
        totals = jnp.sum(jnp.where(diag, total_row, 0.0), axis=-1, keepdims=True)
        acc[r, 0:rows, :] = acc[r, 0:rows, :] / totals
    for r in range(groups):
        for h in range(heads):
            att[h, r * rpg : (r + 1) * rpg, :] = acc[r, h * rpg : (h + 1) * rpg, :]
    state = hid[...]
    per = heads // tps
    for d, w_ref in enumerate((w0_ref, w1_ref, w2_ref, w3_ref)):
        source = tp ^ d
        for j in range(per):
            state = state + dot(
                att[source * per + j].astype(bf16), w_ref[j * lanes : (j + 1) * lanes, :]
            )
    hid_ref[...] = state
    width = state.shape[1]
    half = width // 2
    sums = jnp.sum(state * state, axis=-1, keepdims=True)
    scaled = state * ng_ref[...]
    xs[0] = scaled[:, :half]
    xs[1] = scaled[:, half:]
    own, other = xs[y].astype(bf16), xs[1 - y].astype(bf16)
    units = pair_ref.shape[1] // 2
    gate = dot(own, mine_ref[:, :units]) + dot(other, pair_ref[:, :units])
    up = dot(own, mine_ref[:, units:]) + dot(other, pair_ref[:, units:])
    square = iota((toks, lanes), 0) == iota((toks, lanes), 1)
    sums_row = jnp.sum(jnp.where(square, sums, 0.0), axis=0, keepdims=True)
    high = sums_row.astype(bf16).astype(f32)
    blocks = units // lanes
    for i in range(blocks):
        at = slice(i * lanes, (i + 1) * lanes)
        out[i * toks : (i + 1) * toks, :] = gate[:, at]
        out[(blocks + i) * toks : (blocks + i + 1) * toks, :] = up[:, at]
    base = 2 * blocks * toks
    first = iota((8, lanes), 0)
    out[base : base + 8, :] = jnp.where(
        first == 0, high, jnp.where(first == 1, sums_row - high, 0.0)
    )
    msg_ref[...] = out[...].astype(bf16)


def down_kernel(m0_ref, m1_ref, m2_ref, m3_ref, hid_ref, down_ref, pair_ref, back_ref, part, pay, whole):
    tp = lax.axis_index("tp")
    tps = lax.axis_size("tp")
    y = lax.rem(lax.axis_index("req"), 2)
    units, half = pair_ref.shape
    toks, width = hid_ref.shape
    total = m0_ref[...].astype(f32)
    for m_ref in (m1_ref, m2_ref, m3_ref):
        total = total + m_ref[...].astype(f32)
    whole[...] = total
    blocks = units // lanes
    base = 2 * blocks * toks
    square = iota((toks, lanes), 0) == iota((toks, lanes), 1)
    sums_row = whole[base : base + 1, :] + whole[base + 1 : base + 2, :]
    sums = jnp.sum(
        jnp.where(square, jnp.broadcast_to(sums_row, (toks, lanes)), 0.0), axis=-1, keepdims=True
    )
    factor = lax.rsqrt(sums / (width * 4) + norm_eps)
    pieces = []
    for i in range(blocks):
        gate = whole[i * toks : (i + 1) * toks, :] * factor
        up = whole[(blocks + i) * toks : (blocks + i + 1) * toks, :] * factor
        pieces.append((gate / (1.0 + jnp.exp(-gate)) * up).astype(bf16))
    hidden = jnp.concatenate(pieces, axis=1)
    own_rows = pl.ds(pl.multiple_of(y * units, lanes), units)
    part[y] = dot(hidden, down_ref[own_rows, :])
    part[1 - y] = dot(hidden, pair_ref[...])
    chunks = width // lanes
    groups = pay.shape[0]
    rpg = toks // groups
    for c in range(chunks):
        at = (c * lanes) % half
        block = part[c * lanes // half][:, at : at + lanes]
        adds = (y == 0) & (tp == c)
        block = block + jnp.where(adds, hid_ref[:, c * lanes : (c + 1) * lanes], 0.0)
        for r in range(groups):
            pay[r, c * rpg : (c + 1) * rpg, :] = block[r * rpg : (r + 1) * rpg, :]
    for r in range(groups):
        for g in range(back_ref.shape[1]):
            out = pay[r, 4 * g : 4 * g + 4, :].astype(bf16)
            for t in range(tps):
                back_ref[r * tps + t, g] = out


def final_kernel(back_ref, out_ref, acc, rows_out):
    tps = lax.axis_size("tp")
    peers = back_ref.shape[0]
    rpg, width = out_ref.shape
    slices = acc.shape[0]
    group = peers // slices
    chunks = width // (slices * lanes)
    for z in range(slices):
        for g in range(back_ref.shape[1]):
            total = back_ref[z * group, g].astype(f32)
            for p in range(1, group):
                total = total + back_ref[z * group + p, g].astype(f32)
            acc[z, 4 * g : 4 * g + 4, :] = total
    for z in range(slices):
        for c in range(chunks):
            at = slice((z * chunks + c) * lanes, (z * chunks + c + 1) * lanes)
            rows_out[0:rpg, at] = acc[z, c * rpg : (c + 1) * rpg, :]
    out_ref[...] = rows_out[0:rpg, :].astype(bf16)


def prefill_kernel(
    len_ref, q_ref, g_ref, kv0_ref, kv1_ref, kv2_ref, kv3_ref, qg_ref, freq_ref, out_ref, mid_ref
):
    tp = lax.axis_index("tp")
    tok = q_ref.shape[0]
    heads = q_ref.shape[1] // lanes
    kvs = kv0_ref.shape[1] // (2 * lanes)
    per = heads // kvs
    third = tp == 2
    mid_ref[...] = jnp.where(third, kv3_ref[...], kv1_ref[...])
    blocks = ((tp, kv0_ref), (jnp.where(third, tp ^ 3, tp ^ 1), mid_ref), (tp ^ 2, kv2_ref))
    tok_index = tp * tok + iota((tok, lanes), 0)
    begin = begin_of(tok_index, len_ref)
    factors = rope_factors((tok_index - begin).astype(f32) * freq_ref[...])
    col = iota((tok, tok), 1)
    allowed = []
    for block, _ in blocks:
        key_index = block * tok + col
        allowed.append((key_index >= begin) & (key_index <= tok_index))
    gates = jax.nn.sigmoid(g_ref[...].astype(f32))
    qg = qg_ref[...]
    scale = lanes ** (-0.5)
    for h in range(heads):
        k = h // per
        at = slice(h * lanes, (h + 1) * lanes)
        query = norm_rope(q_ref[:, at].astype(f32), qg, factors)
        totals = jnp.zeros((tok, 1), f32)
        mixed = jnp.zeros((tok, lanes), f32)
        for b, (_, kv_ref) in enumerate(blocks):
            scores = dot_nt(query, kv_ref[:, k * lanes : (k + 1) * lanes])
            weights = jnp.where(allowed[b], jnp.exp(scores * scale), 0.0)
            totals = totals + jnp.sum(weights, axis=-1, keepdims=True)
            mixed = mixed + dot(
                weights.astype(bf16), kv_ref[:, (kvs + k) * lanes : (kvs + k + 1) * lanes]
            )
        out_ref[:, at] = (mixed / totals * gates[:, h : h + 1]).astype(bf16)


def call(body, out_shape, args, scratch=(), hbm=False, out_any=False, smem=0, flops=0, limit=12):
    specs = [pl.BlockSpec(memory_space=pltpu.SMEM)] * smem
    space = pltpu.HBM if hbm else pltpu.VMEM
    specs += [pl.BlockSpec(memory_space=space)] * (len(args) - smem)
    size = sum(a.size * a.dtype.itemsize for a in args)
    return pl.pallas_call(
        body,
        out_shape=out_shape,
        in_specs=specs,
        out_specs=jax.tree.map(
            lambda _: pl.BlockSpec(memory_space=pl.ANY if out_any else pltpu.VMEM), out_shape
        ),
        scratch_shapes=[pltpu.VMEM(s, f32) if isinstance(s, tuple) else s for s in scratch],
        compiler_params=pltpu.CompilerParams(vmem_limit_bytes=limit * 2**20),
        cost_estimate=pl.CostEstimate(flops=flops, bytes_accessed=size, transcendentals=0),
    )(*args)


def hold(arrays, flops):
    return pl.pallas_call(
        ready_kernel,
        out_shape=jax.ShapeDtypeStruct((8, lanes), f32),
        in_specs=[pl.BlockSpec(memory_space=pl.ANY)] * len(arrays),
        out_specs=pl.BlockSpec(memory_space=pltpu.VMEM),
        compiler_params=pltpu.CompilerParams(vmem_limit_bytes=2**20),
        cost_estimate=pl.CostEstimate(flops=flops, bytes_accessed=0, transcendentals=0),
    )(*arrays)


def local(
    q_pre,
    gate_pre,
    k_pre,
    v_pre,
    q_gain,
    k_gain,
    lengths,
    q_new,
    gate_new,
    k_new,
    v_new,
    resid,
    w_out,
    norm_gain,
    w_gate,
    w_up,
    w_down,
):
    tps, reqs = lax.axis_size("tp"), lax.axis_size("req")
    tok = q_pre.shape[0]
    rpg, width = resid.shape
    slices = reqs // 2
    head_size = q_gain.shape[0]
    heads = gate_pre.shape[1]
    part = width // slices if slices else 0
    if not (slices == 4 and tps == 4 and head_size == lanes == tok and part == tps * lanes):
        return general(
            q_pre, gate_pre, k_pre, v_pre, q_gain, k_gain, lengths, q_new, gate_new, k_new, v_new,
            resid, w_out, norm_gain, w_gate, w_up, w_down,
        )
    peers = tps * reqs
    toks = rpg * reqs
    units = w_gate.shape[1] // 2
    req = lax.axis_index("req")
    z, y = req // 2, req % 2
    freqs = rope_base ** (-(np.arange(head_size // 2) * 2.0 / head_size))
    freqs = jnp.asarray(np.concatenate([freqs, freqs])[None, :], f32)
    qg, kg = q_gain[None, :], k_gain[None, :]

    def cross(array, by):
        return lax.ppermute(array, "tp", [(i, i ^ by) for i in range(tps)])

    def swap(array):
        return lax.ppermute(array, "req", [(i, i ^ 1) for i in range(reqs)])

    def along(array, by):
        return lax.ppermute(array, "req", [(i, i ^ (2 * by)) for i in range(reqs)])

    inputs = (
        lengths, k_pre, v_pre, q_new, k_new, v_new, gate_new, resid, qg, kg, freqs,
        w_out, w_gate, w_up, w_down,
    )
    outputs = (
        jax.ShapeDtypeStruct((tok, 2 * k_pre.shape[1]), bf16),
        jax.ShapeDtypeStruct((peers, pay_rows // 4, 4, lanes), bf16),
        jax.ShapeDtypeStruct((w_out.shape[0], part), bf16),
        jax.ShapeDtypeStruct((w_gate.shape[0], 2 * units), bf16),
        jax.ShapeDtypeStruct((units, w_down.shape[1]), bf16),
    )
    kv, pay, w_own, pair, down_pair = call(
        partial_kernel,
        outputs,
        inputs,
        scratch=[pltpu.VMEM(o.shape, o.dtype) for o in outputs]
        + [(heads * rpg, lanes)] * 4
        + [(pay_rows, lanes), pltpu.SMEM(lengths.shape, jnp.int32)]
        + [pltpu.VMEM(a.shape, a.dtype) for a in inputs[1:11]]
        + [pltpu.SemaphoreType.DMA((len(inputs),)), pltpu.SemaphoreType.DMA((len(outputs),))],
        hbm=True,
        out_any=True,
        flops=10**7,
        limit=56,
    )
    w_far = cross(w_own, 2)
    pair = swap(pair)
    half = jax.ShapeDtypeStruct((w_gate.shape[0], 2 * units), bf16)
    mine, ng = call(
        fetch_kernel,
        (half, jax.ShapeDtypeStruct((1, part), f32)),
        (w_gate, w_up, norm_gain[None, :]),
        hbm=True,
        scratch=[pltpu.SemaphoreType.DMA((3,))],
    )
    w_here = call(
        columns_kernel,
        jax.ShapeDtypeStruct(w_own.shape, bf16),
        (w_out,),
        hbm=True,
        scratch=[pltpu.SemaphoreType.DMA((1,))],
    )
    late_far, _, _ = lax.optimization_barrier((w_far, mine, w_here))
    w_near, w_both = cross(w_own, 1), cross(late_far, 1)
    kv_near = cross(kv, 1)
    late_kv, _ = lax.optimization_barrier((kv, w_far))
    kv_far = cross(late_kv, 2)
    late_down, _ = lax.optimization_barrier((down_pair, pair))
    down_pair = swap(late_down)
    got = lax.all_to_all(pay, ("req", "tp"), 0, 0, tiled=True)
    landed = hold((pair,), 2 * 10**9)
    token = hold((landed, w_near, w_both), 10**9)
    msg_shape = (2 * units // lanes * toks + 8, lanes)
    hid, msg = call(
        hidden_kernel,
        (
            jax.ShapeDtypeStruct((toks, part), f32),
            jax.ShapeDtypeStruct(msg_shape, bf16),
        ),
        (got, w_here, w_near, w_far, w_both, mine, pair, ng, token),
        scratch=[
            (heads, toks, lanes),
            (toks, part),
            (2, toks, part // 2),
            (reqs, pay_rows, lanes),
            msg_shape,
        ],
        flops=10**7,
    )
    msgs = [msg] + [along(msg, d) for d in (3, 2, 1)]
    kv_both = cross(kv_far, 1)
    prefill_out = call(
        prefill_kernel,
        jax.ShapeDtypeStruct(q_pre.shape, bf16),
        (lengths, q_pre, gate_pre, kv, kv_near, kv_far, kv_both, qg, freqs),
        scratch=[pltpu.VMEM(kv.shape, bf16)],
        smem=1,
        flops=10**9,
    )
    back = call(
        down_kernel,
        jax.ShapeDtypeStruct((peers, back_rows // 4, 4, lanes), bf16),
        (*msgs, hid, w_down, down_pair),
        scratch=[(2, toks, part // 2), (reqs, back_rows, lanes), msg_shape],
        flops=3 * 10**9,
    )
    returned = lax.all_to_all(back, ("req", "tp"), 0, 0, tiled=True)
    returned, prefill_out = lax.optimization_barrier((returned, prefill_out))
    decode_out = call(
        final_kernel,
        jax.ShapeDtypeStruct((rpg, width), bf16),
        (returned,),
        scratch=[(slices, back_rows, lanes), (8, width)],
        flops=10**6,
    )
    return (prefill_out, decode_out)


def solution(mesh):
    return jax.shard_map(
        local,
        mesh=mesh,
        in_specs=(
            P(("req", "tp"), None),
            P(("req", "tp"), None),
            P(("req", "tp"), None),
            P(("req", "tp"), None),
            P(),
            P(),
            P("req", None),
            P("req", None),
            P("req", None),
            P("req", None),
            P("req", None),
            P("req", None),
            P("tp", None),
            P(),
            P("req", "tp"),
            P("req", "tp"),
            P("tp", "req"),
        ),
        out_specs=(P(("req", "tp"), None), P("req", None)),
        check_vma=False,
    )
```

```python
import jax
import jax.numpy as jnp
import numpy as np
from jax import lax
from jax.experimental import pallas as pl
from jax.experimental.pallas import tpu as pltpu
from jax.sharding import PartitionSpec as P

rope_base = 1000000.0
norm_eps = 1e-06


def group_layout(lengths_row, total):
    req_ends = jnp.cumsum(lengths_row)
    req_starts = req_ends - lengths_row
    indices = jnp.arange(total, dtype=jnp.int32)
    segment = jnp.sum((indices[:, None] >= req_ends[None, :]).astype(jnp.int32), axis=1)
    onehot = segment[:, None] == jnp.arange(lengths_row.shape[0], dtype=jnp.int32)[None, :]
    offsets = jnp.sum(jnp.where(onehot, req_starts[None, :], 0), axis=1)
    return (segment, indices - offsets)


def head_norm(values, gain):
    mean_sq = jnp.mean(values * values, axis=-1, keepdims=True)
    return values * lax.rsqrt(mean_sq + norm_eps) * gain


def rotate(values, position):
    half_size = values.shape[-1] // 2
    freqs = rope_base ** (-(jnp.arange(half_size, dtype=jnp.float32) * 2.0 / (2 * half_size)))
    angles = position.astype(jnp.float32)[:, None] * freqs[None, :]
    shaped = (values.shape[0],) + (1,) * (values.ndim - 2) + (half_size,)
    cosine = jnp.cos(angles).reshape(shaped)
    sine = jnp.sin(angles).reshape(shaped)
    first_half = values[..., :half_size]
    second_half = values[..., half_size:]
    return jnp.concatenate(
        [first_half * cosine - second_half * sine, second_half * cosine + first_half * sine],
        axis=-1,
    )


def general(
    q_pre,
    gate_pre,
    k_pre,
    v_pre,
    q_gain,
    k_gain,
    lengths,
    q_new,
    gate_new,
    k_new,
    v_new,
    resid,
    w_out,
    norm_gain,
    w_gate,
    w_up,
    w_down,
):
    tok_rows = q_pre.shape[0]
    tp_count = lax.axis_size("tp")
    tp_index = lax.axis_index("tp")
    head_size = q_gain.shape[0]
    query_heads = gate_pre.shape[1]
    kv_heads = k_pre.shape[1] // head_size
    groups_per = query_heads // kv_heads
    kv_local = kv_heads // tp_count
    req_count = lengths.shape[1]
    score_scale = head_size ** (-0.5)
    segment, position = group_layout(lengths[0], tok_rows * tp_count)
    row_offset = tp_index * tok_rows
    seg_local = lax.dynamic_slice_in_dim(segment, row_offset, tok_rows)
    pos_local = lax.dynamic_slice_in_dim(position, row_offset, tok_rows)
    query_index = row_offset + jnp.arange(tok_rows, dtype=jnp.int32)
    queries = rotate(
        head_norm(q_pre.reshape(tok_rows, query_heads, head_size).astype(jnp.float32), q_gain),
        pos_local,
    )
    queries = queries.astype(jnp.bfloat16).reshape(tok_rows, kv_heads, groups_per, head_size)
    keys = rotate(
        head_norm(k_pre.reshape(tok_rows, kv_heads, head_size).astype(jnp.float32), k_gain),
        pos_local,
    ).astype(jnp.bfloat16)
    values = v_pre.reshape(tok_rows, kv_heads, head_size)

    def key_block(running, key_piece, value_piece, first_row):
        key_count = key_piece.shape[0]
        key_index = first_row + jnp.arange(key_count, dtype=jnp.int32)
        allowed = (seg_local[:, None] == segment[None, :]) & (
            query_index[:, None] >= key_index[None, :]
        )
        scores = (
            jnp.einsum(
                "qkgd,pkd->qkgp",
                queries,
                key_piece.reshape(key_count, kv_heads, head_size),
                preferred_element_type=jnp.float32,
            )
            * score_scale
        )
        weights = jnp.where(allowed[:, None, None, :], jnp.exp(scores), 0.0)
        totals = running[0] + jnp.sum(weights, axis=-1)
        mixed = running[1] + jnp.einsum(
            "qkgp,pkd->qkgd",
            weights.astype(jnp.bfloat16),
            value_piece.reshape(key_count, kv_heads, head_size),
            preferred_element_type=jnp.float32,
        )
        return (totals, mixed)

    start_state = (
        jnp.zeros((tok_rows, kv_heads, groups_per), jnp.float32),
        jnp.zeros((tok_rows, kv_heads, groups_per, head_size), jnp.float32),
    )
    pieces = (
        lax.all_gather(keys.reshape(tok_rows, kv_heads * head_size), "tp", axis=0, tiled=True),
        lax.all_gather(v_pre, "tp", axis=0, tiled=True),
    )
    key_count = pieces[0].shape[0]
    block_rows = 512

    def one_block(number, carried):
        begin_at = number * block_rows
        return key_block(carried, pieces[0], pieces[1], begin_at)

    totals, mixed = lax.fori_loop(0, key_count // block_rows, one_block, start_state)
    gates = jax.nn.sigmoid(gate_pre.astype(jnp.float32)).reshape(tok_rows, kv_heads, groups_per)
    prefill_out = (
        (mixed / totals[..., None] * gates[..., None])
        .astype(jnp.bfloat16)
        .reshape(tok_rows, query_heads * head_size)
    )
    new_queries = rotate(
        head_norm(q_new.reshape(req_count, query_heads, head_size).astype(jnp.float32), q_gain),
        lengths[0],
    )
    new_queries = new_queries.astype(jnp.bfloat16).reshape(
        req_count, kv_heads, groups_per, head_size
    )
    new_keys = rotate(
        head_norm(k_new.reshape(req_count, kv_heads, head_size).astype(jnp.float32), k_gain),
        lengths[0],
    ).astype(jnp.bfloat16)
    new_values = v_new.reshape(req_count, kv_heads, head_size)
    new_gates = jax.nn.sigmoid(gate_new.astype(jnp.float32)).reshape(
        req_count, kv_heads, groups_per
    )
    head_first = tp_index * kv_local
    request_ids = jnp.arange(req_count, dtype=jnp.int32)
    own_queries = lax.dynamic_slice_in_dim(new_queries, head_first, kv_local, 1)
    cache_keys, cache_values = (
        lax.all_to_all(keys, "tp", split_axis=1, concat_axis=0, tiled=True),
        lax.all_to_all(values, "tp", split_axis=1, concat_axis=0, tiled=True),
    )
    scores = (
        jnp.einsum("rkgd,pkd->rkgp", own_queries, cache_keys, preferred_element_type=jnp.float32)
        * score_scale
    )
    owned = segment[None, :] == request_ids[:, None]
    weights = jnp.where(owned[:, None, None, :], jnp.exp(scores), 0.0)
    weighted = jnp.einsum(
        "rkgp,pkd->rkgd",
        weights.astype(jnp.bfloat16),
        cache_values,
        preferred_element_type=jnp.float32,
    )
    dec_totals = jnp.sum(weights, axis=-1)
    dec_mixed = weighted
    own_keys = lax.dynamic_slice_in_dim(new_keys, head_first, kv_local, 1)
    own_values = lax.dynamic_slice_in_dim(new_values, head_first, kv_local, 1)
    own_gates = lax.dynamic_slice_in_dim(new_gates, head_first, kv_local, 1)
    self_weight = jnp.exp(
        jnp.einsum("rkgd,rkd->rkg", own_queries, own_keys, preferred_element_type=jnp.float32)
        * score_scale
    )
    dec_totals = dec_totals + self_weight
    dec_mixed = dec_mixed + self_weight[..., None] * own_values.astype(jnp.float32)[:, :, None, :]
    attended = (
        (dec_mixed / dec_totals[..., None] * own_gates[..., None])
        .astype(jnp.bfloat16)
        .reshape(req_count, kv_local * groups_per * head_size)
    )
    partial_out = jnp.dot(attended, w_out, preferred_element_type=jnp.float32)
    attn_rows = lax.psum(partial_out, "tp")
    hidden_state = resid.astype(jnp.float32) + attn_rows
    mean_sq = jnp.mean(hidden_state * hidden_state, axis=-1, keepdims=True)
    normed = (hidden_state * lax.rsqrt(mean_sq + norm_eps) * norm_gain).astype(jnp.bfloat16)
    units_local = w_gate.shape[1]
    paired = jnp.concatenate([w_gate, w_up], axis=1)
    columns = lax.all_to_all(normed, "req", split_axis=1, concat_axis=0, tiled=True)
    whole_sums = lax.psum(jnp.dot(columns, paired, preferred_element_type=jnp.float32), "req")
    hidden_units = (jax.nn.silu(whole_sums[:, :units_local]) * whole_sums[:, units_local:]).astype(
        jnp.bfloat16
    )
    down_part = jnp.dot(hidden_units, w_down, preferred_element_type=jnp.float32)
    back_part = lax.all_to_all(down_part, "req", split_axis=0, concat_axis=1, tiled=True)
    mlp_rows = lax.psum(back_part, "tp")
    decode_out = (hidden_state + mlp_rows).astype(jnp.bfloat16)
    return (prefill_out, decode_out)


f32 = jnp.float32
bf16 = jnp.bfloat16
lanes = 128
pay_rows = 28
back_rows = 12


def dot(a, b):
    return jnp.dot(a, b, preferred_element_type=f32)


def dot_nt(a, b):
    return lax.dot_general(a, b, (((1,), (1,)), ((), ())), preferred_element_type=f32)


def iota(shape, dim):
    return lax.broadcasted_iota(jnp.int32, shape, dim)


def rope_factors(angles):
    turns = jnp.floor(angles * (2.0 / np.pi) + 0.5)
    rest = angles - turns * 1.5703125
    rest = rest - turns * 4.837512969970703125e-4
    rest = rest - turns * 7.549789948768648e-8
    sq = rest * rest
    sine = ((-1.9515295891e-4 * sq + 8.3321608736e-3) * sq - 1.6666654611e-1) * sq * rest + rest
    cosine = (
        ((2.443315711809948e-5 * sq - 1.388731625493765e-3) * sq + 4.166664568298827e-2) * sq * sq
        - 0.5 * sq
        + 1.0
    )
    low = iota(angles.shape, 1) < lanes // 2
    quarter = turns.astype(jnp.int32) + jnp.where(low, 1, 0)
    both = jnp.where((quarter & 1) == 1, cosine, sine)
    both = jnp.where((quarter & 2) == 2, -both, both)
    swapped = pltpu.roll(both, lanes // 2, 1)
    return jnp.where(low, both, swapped), jnp.where(low, -swapped, both)


def norm_rope(values, gain, factors):
    mean_sq = jnp.mean(values * values, axis=-1, keepdims=True)
    normed = values * lax.rsqrt(mean_sq + norm_eps) * gain
    return (normed * factors[0] + pltpu.roll(normed, lanes // 2, 1) * factors[1]).astype(bf16)


def begin_of(indices, len_ref):
    begin = jnp.zeros_like(indices)
    end = 0
    for j in range(len_ref.shape[1] - 1):
        end = end + len_ref[0, j]
        begin = jnp.where(indices >= end, end, begin)
    return begin


def partial_kernel(
    len_hbm, k_hbm, v_hbm, qn_hbm, kn_hbm, vn_hbm, gn_hbm, resid_hbm, qg_hbm, kg_hbm, freq_hbm,
    w_hbm, gate_hbm, up_hbm,
    kv_hbm, pay_hbm, own_hbm, pair_hbm,
    kv_ref, pay_ref, own_ref, pair_ref, row_q, row_k, row_v, row_g, pay, len_ref, k_ref, v_ref, qn_ref, kn_ref, vn_ref, gn_ref,
    resid_ref, qg_ref, kg_ref, freq_ref, sems, out_sems,
):
    tp = lax.axis_index("tp")
    req = lax.axis_index("req")
    z, other = lax.div(req, 2), 1 - lax.rem(req, 2)
    width = own_ref.shape[1]
    units = pair_ref.shape[1] // 2
    cols = pl.ds(pl.multiple_of(z * width, lanes), width)
    theirs = pl.ds(pl.multiple_of(other * units, lanes), units)
    moves = (
        (len_hbm, len_ref), (freq_hbm, freq_ref), (k_hbm, k_ref), (kg_hbm, kg_ref),
        (qn_hbm, qn_ref), (kn_hbm, kn_ref), (vn_hbm, vn_ref), (gn_hbm, gn_ref), (qg_hbm, qg_ref),
        (v_hbm, v_ref), (resid_hbm, resid_ref),
        (gate_hbm.at[:, theirs], pair_ref.at[:, pl.ds(0, units)]),
        (up_hbm.at[:, theirs], pair_ref.at[:, pl.ds(units, units)]),
        (w_hbm.at[:, cols], own_ref),
    )
    copies = [pltpu.make_async_copy(a, b, sems.at[i]) for i, (a, b) in enumerate(moves)]
    for copy in copies:
        copy.start()
    ends = (
        (pair_ref, pair_hbm), (own_ref, own_hbm), (kv_ref, kv_hbm), (pay_ref, pay_hbm),
    )
    leave = [pltpu.make_async_copy(a, b, out_sems.at[i]) for i, (a, b) in enumerate(ends)]
    tok = k_ref.shape[0]
    rpg = qn_ref.shape[0]
    heads = qn_ref.shape[1] // lanes
    kvs = k_ref.shape[1] // lanes
    per = heads // kvs
    rows = heads * rpg
    for copy in copies[:2]:
        copy.wait()
    freq = freq_ref[...]
    tok_index = tp * tok + iota((tok, lanes), 0)
    factors = rope_factors((tok_index - begin_of(tok_index, len_ref)).astype(f32) * freq)
    for copy in copies[2:11]:
        copy.wait()
    qg, kg = qg_ref[...], kg_ref[...]
    keys = []
    for k in range(kvs):
        at = slice(k * lanes, (k + 1) * lanes)
        keys.append(norm_rope(k_ref[:, at].astype(f32), kg, factors))
        kv_ref[:, at] = keys[-1]
    kv_ref[:, kvs * lanes :] = v_ref[...]
    for copy in copies[11:]:
        copy.wait()
    for copy in leave[:3]:
        copy.start()
    qn, kn = qn_ref[...].astype(f32), kn_ref[...].astype(f32)
    vn, gn = vn_ref[...].astype(f32), gn_ref[...].astype(f32)
    for h in range(heads):
        at = slice(h * rpg, (h + 1) * rpg)
        kv = slice((h // per) * lanes, (h // per + 1) * lanes)
        row_q[at, :] = qn[:, h * lanes : (h + 1) * lanes]
        row_k[at, :] = kn[:, kv]
        row_v[at, :] = vn[:, kv]
        row_g[at, :] = jnp.broadcast_to(gn[:, h : h + 1], (rpg, lanes))
    row = iota((rows, lanes), 0)
    col = iota((rows, lanes), 1)
    head = row * 0
    for h in range(1, heads):
        head = jnp.where(row >= h * rpg, h, head)
    request = row - head * rpg
    length, first, last = row * 0, row * 0, row * 0
    end = 0
    for j in range(rpg):
        mine = request == j
        length = jnp.where(mine, len_ref[0, j], length)
        first = jnp.where(mine, end, first)
        end = end + len_ref[0, j]
        last = jnp.where(mine, end, last)
    new_factors = rope_factors(length.astype(f32) * freq)
    scale = lanes ** (-0.5)
    new_q = norm_rope(row_q[...], qg, new_factors)
    new_k = norm_rope(row_k[...], kg, new_factors)
    scores = jnp.zeros((rows, tok), f32)
    for k in range(kvs):
        mine = (head >= k * per) & (head < (k + 1) * per)
        scores = jnp.where(mine, dot_nt(new_q, keys[k]), scores)
    index = tp * tok + col
    weights = jnp.where((index >= first) & (index < last), jnp.exp(scores * scale), 0.0)
    totals = jnp.sum(weights, axis=-1, keepdims=True)
    rounded = weights.astype(bf16)
    mixed = jnp.zeros((rows, lanes), f32)
    for k in range(kvs):
        mine = (head >= k * per) & (head < (k + 1) * per)
        mixed = mixed + dot(
            jnp.where(mine, rounded, jnp.zeros_like(rounded)), v_ref[:, k * lanes : (k + 1) * lanes]
        )
    self_score = jnp.sum(new_q.astype(f32) * new_k.astype(f32), axis=-1, keepdims=True)
    self_weight = jnp.where(tp == 0, jnp.exp(self_score * scale), 0.0)
    totals = totals + self_weight
    mixed = (mixed + self_weight * row_v[...]) * jax.nn.sigmoid(row_g[...])
    total_row = jnp.sum(jnp.where(row == col, totals, 0.0), axis=0, keepdims=True)
    high = total_row.astype(bf16).astype(f32)
    rest = pltpu.roll(jnp.broadcast_to(total_row - high, (8, lanes)), lanes // 2, 1)
    pay[0:rows, :] = mixed
    pay[rows + rpg : rows + rpg + 1, :] = jnp.where(
        iota((1, lanes), 1) < lanes // 2, high, rest[0:1, :]
    )
    peers = pay_ref.shape[0]
    tps = lax.axis_size("tp")
    slices = resid_ref.shape[1] // (tps * lanes)
    for z in range(slices):
        at = pl.ds(pl.multiple_of((z * tps + tp) * lanes, lanes), lanes)
        pay[rows : rows + rpg, :] = resid_ref[:, at].astype(f32)
        for g in range(pay_ref.shape[1]):
            out = pay[4 * g : 4 * g + 4, :].astype(bf16)
            for peer in range(z * peers // slices, (z + 1) * peers // slices):
                pay_ref[peer, g] = out
    leave[3].start()
    for copy in leave:
        copy.wait()


def fetch_kernel(gate_hbm, up_hbm, ng_hbm, mine_ref, ng_ref, sems):
    units = mine_ref.shape[1] // 2
    width = ng_ref.shape[1]
    req = lax.axis_index("req")
    at = pl.ds(pl.multiple_of(lax.rem(req, 2) * units, lanes), units)
    cols = pl.ds(pl.multiple_of(lax.div(req, 2) * width, lanes), width)
    copies = (
        pltpu.make_async_copy(gate_hbm.at[:, at], mine_ref.at[:, pl.ds(0, units)], sems.at[0]),
        pltpu.make_async_copy(up_hbm.at[:, at], mine_ref.at[:, pl.ds(units, units)], sems.at[1]),
        pltpu.make_async_copy(ng_hbm.at[:, cols], ng_ref, sems.at[2]),
    )
    for copy in copies:
        copy.start()
    for copy in copies:
        copy.wait()


def columns_kernel(w_hbm, down_hbm, w_ref, down_ref, sems):
    width = w_ref.shape[1]
    units = down_ref.shape[0]
    req = lax.axis_index("req")
    cols = pl.ds(pl.multiple_of(lax.div(req, 2) * width, lanes), width)
    theirs = pl.ds(pl.multiple_of((1 - lax.rem(req, 2)) * units, lanes), units)
    copies = (
        pltpu.make_async_copy(w_hbm.at[:, cols], w_ref, sems.at[0]),
        pltpu.make_async_copy(down_hbm.at[theirs, :], down_ref, sems.at[1]),
    )
    for copy in copies:
        copy.start()
    for copy in copies:
        copy.wait()


def ready_kernel(*refs):
    refs[-1][...] = jnp.zeros_like(refs[-1])


def hidden_kernel(
    pay_ref, w0_ref, w1_ref, w2_ref, w3_ref, mine_ref, pair_ref, ng_ref, _,
    hid_ref, msg_ref, att, hid, xs, acc, out,
):
    tp = lax.axis_index("tp")
    req = lax.axis_index("req")
    tps = lax.axis_size("tp")
    z, y = lax.div(req, 2), lax.rem(req, 2)
    heads, toks, _ = att.shape
    groups = pay_ref.shape[0] // tps
    rpg = toks // groups
    rows = heads * rpg
    diag = iota((rows, lanes), 0) == iota((rows, lanes), 1)
    quads = pay_ref.shape[1]
    for r in range(groups):
        for g in range(quads):
            total = jnp.zeros((4, lanes), f32)
            for t in range(tps):
                piece = pay_ref[r * tps + t, g].astype(f32)
                total = total + piece
                if g == quads - 1:
                    hid[r * rpg : (r + 1) * rpg, t * lanes : (t + 1) * lanes] = piece[:rpg, :]
            acc[r, 4 * g : 4 * g + 4, :] = total
    for r in range(groups):
        total_row = jnp.broadcast_to(acc[r, pay_rows - 1 : pay_rows, :], (rows, lanes))
        total_row = total_row + pltpu.roll(total_row, lanes // 2, 1)
        totals = jnp.sum(jnp.where(diag, total_row, 0.0), axis=-1, keepdims=True)
        acc[r, 0:rows, :] = acc[r, 0:rows, :] / totals
    for r in range(groups):
        for h in range(heads):
            att[h, r * rpg : (r + 1) * rpg, :] = acc[r, h * rpg : (h + 1) * rpg, :]
    state = hid[...]
    per = heads // tps
    for d, w_ref in enumerate((w0_ref, w1_ref, w2_ref, w3_ref)):
        source = tp ^ d
        for j in range(per):
            state = state + dot(
                att[source * per + j].astype(bf16), w_ref[j * lanes : (j + 1) * lanes, :]
            )
    hid_ref[...] = state
    width = state.shape[1]
    half = width // 2
    sums = jnp.sum(state * state, axis=-1, keepdims=True)
    scaled = state * ng_ref[...]
    xs[0] = scaled[:, :half]
    xs[1] = scaled[:, half:]
    own, other = xs[y].astype(bf16), xs[1 - y].astype(bf16)
    units = pair_ref.shape[1] // 2
    gate = dot(own, mine_ref[:, :units]) + dot(other, pair_ref[:, :units])
    up = dot(own, mine_ref[:, units:]) + dot(other, pair_ref[:, units:])
    square = iota((toks, lanes), 0) == iota((toks, lanes), 1)
    sums_row = jnp.sum(jnp.where(square, sums, 0.0), axis=0, keepdims=True)
    high = sums_row.astype(bf16).astype(f32)
    blocks = units // lanes
    for i in range(blocks):
        at = slice(i * lanes, (i + 1) * lanes)
        out[i * toks : (i + 1) * toks, :] = gate[:, at]
        out[(blocks + i) * toks : (blocks + i + 1) * toks, :] = up[:, at]
    base = 2 * blocks * toks
    first = iota((8, lanes), 0)
    out[base : base + 8, :] = jnp.where(
        first == 0, high, jnp.where(first == 1, sums_row - high, 0.0)
    )
    msg_ref[...] = out[...].astype(bf16)


def down_kernel(m0_ref, m1_ref, m2_ref, m3_ref, hid_ref, down_ref, pair_ref, back_ref, pay, whole):
    tp = lax.axis_index("tp")
    tps = lax.axis_size("tp")
    y = lax.rem(lax.axis_index("req"), 2)
    units, half = pair_ref.shape
    toks, width = hid_ref.shape
    total = m0_ref[...].astype(f32)
    for m_ref in (m1_ref, m2_ref, m3_ref):
        total = total + m_ref[...].astype(f32)
    whole[...] = total
    blocks = units // lanes
    base = 2 * blocks * toks
    square = iota((toks, lanes), 0) == iota((toks, lanes), 1)
    sums_row = whole[base : base + 1, :] + whole[base + 1 : base + 2, :]
    sums = jnp.sum(
        jnp.where(square, jnp.broadcast_to(sums_row, (toks, lanes)), 0.0), axis=-1, keepdims=True
    )
    factor = lax.rsqrt(sums / (width * 4) + norm_eps)
    pieces = []
    for i in range(blocks):
        gate = whole[i * toks : (i + 1) * toks, :] * factor
        up = whole[(blocks + i) * toks : (blocks + i + 1) * toks, :] * factor
        pieces.append((gate / (1.0 + jnp.exp(-gate)) * up).astype(bf16))
    hidden = jnp.concatenate(pieces, axis=1)
    own_rows = pl.ds(pl.multiple_of(y * units, lanes), units)
    mine, theirs = dot(hidden, down_ref[own_rows, :]), dot(hidden, pair_ref[...])
    part = (jnp.where(y == 0, mine, theirs), jnp.where(y == 0, theirs, mine))
    chunks = width // lanes
    groups = pay.shape[0]
    rpg = toks // groups
    for c in range(chunks):
        at = (c * lanes) % half
        block = part[c * lanes // half][:, at : at + lanes]
        adds = (y == 0) & (tp == c)
        block = block + jnp.where(adds, hid_ref[:, c * lanes : (c + 1) * lanes], 0.0)
        for r in range(groups):
            pay[r, c * rpg : (c + 1) * rpg, :] = block[r * rpg : (r + 1) * rpg, :]
    for r in range(groups):
        for g in range(back_ref.shape[1]):
            out = pay[r, 4 * g : 4 * g + 4, :].astype(bf16)
            for t in range(tps):
                back_ref[r * tps + t, g] = out


def final_kernel(back_ref, out_ref, acc, rows_out):
    tps = lax.axis_size("tp")
    peers = back_ref.shape[0]
    rpg, width = out_ref.shape
    slices = acc.shape[0]
    group = peers // slices
    chunks = width // (slices * lanes)
    for z in range(slices):
        for g in range(back_ref.shape[1]):
            total = back_ref[z * group, g].astype(f32)
            for p in range(1, group):
                total = total + back_ref[z * group + p, g].astype(f32)
            acc[z, 4 * g : 4 * g + 4, :] = total
    for z in range(slices):
        for c in range(chunks):
            at = slice((z * chunks + c) * lanes, (z * chunks + c + 1) * lanes)
            rows_out[0:rpg, at] = acc[z, c * rpg : (c + 1) * rpg, :]
    out_ref[...] = rows_out[0:rpg, :].astype(bf16)


def prefill_kernel(
    len_ref, q_ref, g_ref, kv0_ref, kv1_ref, kv2_ref, kv3_ref, qg_ref, freq_ref, out_ref, mid_ref
):
    tp = lax.axis_index("tp")
    tok = q_ref.shape[0]
    heads = q_ref.shape[1] // lanes
    kvs = kv0_ref.shape[1] // (2 * lanes)
    per = heads // kvs
    third = tp == 2
    mid_ref[...] = jnp.where(third, kv3_ref[...], kv1_ref[...])
    blocks = ((tp, kv0_ref), (jnp.where(third, tp ^ 3, tp ^ 1), mid_ref), (tp ^ 2, kv2_ref))
    tok_index = tp * tok + iota((tok, lanes), 0)
    begin = begin_of(tok_index, len_ref)
    factors = rope_factors((tok_index - begin).astype(f32) * freq_ref[...])
    col = iota((tok, tok), 1)
    allowed = []
    for block, _ in blocks:
        key_index = block * tok + col
        allowed.append((key_index >= begin) & (key_index <= tok_index))
    gates = jax.nn.sigmoid(g_ref[...].astype(f32))
    qg = qg_ref[...]
    scale = lanes ** (-0.5)
    for h in range(heads):
        k = h // per
        at = slice(h * lanes, (h + 1) * lanes)
        query = norm_rope(q_ref[:, at].astype(f32), qg, factors)
        totals = jnp.zeros((tok, 1), f32)
        mixed = jnp.zeros((tok, lanes), f32)
        for b, (_, kv_ref) in enumerate(blocks):
            scores = dot_nt(query, kv_ref[:, k * lanes : (k + 1) * lanes])
            weights = jnp.where(allowed[b], jnp.exp(scores * scale), 0.0)
            totals = totals + jnp.sum(weights, axis=-1, keepdims=True)
            mixed = mixed + dot(
                weights.astype(bf16), kv_ref[:, (kvs + k) * lanes : (kvs + k + 1) * lanes]
            )
        out_ref[:, at] = (mixed / totals * gates[:, h : h + 1]).astype(bf16)


def call(body, out_shape, args, scratch=(), hbm=False, out_any=False, smem=0, flops=0, limit=12):
    specs = [pl.BlockSpec(memory_space=pltpu.SMEM)] * smem
    space = pltpu.HBM if hbm else pltpu.VMEM
    specs += [pl.BlockSpec(memory_space=space)] * (len(args) - smem)
    size = sum(a.size * a.dtype.itemsize for a in args)
    return pl.pallas_call(
        body,
        out_shape=out_shape,
        in_specs=specs,
        out_specs=jax.tree.map(
            lambda _: pl.BlockSpec(memory_space=pl.ANY if out_any else pltpu.VMEM), out_shape
        ),
        scratch_shapes=[pltpu.VMEM(s, f32) if isinstance(s, tuple) else s for s in scratch],
        compiler_params=pltpu.CompilerParams(vmem_limit_bytes=limit * 2**20),
        cost_estimate=pl.CostEstimate(flops=flops, bytes_accessed=size, transcendentals=0),
    )(*args)


def hold(arrays, flops):
    return pl.pallas_call(
        ready_kernel,
        out_shape=jax.ShapeDtypeStruct((8, lanes), f32),
        in_specs=[pl.BlockSpec(memory_space=pl.ANY)] * len(arrays),
        out_specs=pl.BlockSpec(memory_space=pltpu.VMEM),
        compiler_params=pltpu.CompilerParams(vmem_limit_bytes=2**20),
        cost_estimate=pl.CostEstimate(flops=flops, bytes_accessed=0, transcendentals=0),
    )(*arrays)


def local(
    q_pre,
    gate_pre,
    k_pre,
    v_pre,
    q_gain,
    k_gain,
    lengths,
    q_new,
    gate_new,
    k_new,
    v_new,
    resid,
    w_out,
    norm_gain,
    w_gate,
    w_up,
    w_down,
):
    tps, reqs = lax.axis_size("tp"), lax.axis_size("req")
    tok = q_pre.shape[0]
    rpg, width = resid.shape
    slices = reqs // 2
    head_size = q_gain.shape[0]
    heads = gate_pre.shape[1]
    part = width // slices if slices else 0
    if not (slices == 4 and tps == 4 and head_size == lanes == tok and part == tps * lanes):
        return general(
            q_pre, gate_pre, k_pre, v_pre, q_gain, k_gain, lengths, q_new, gate_new, k_new, v_new,
            resid, w_out, norm_gain, w_gate, w_up, w_down,
        )
    peers = tps * reqs
    toks = rpg * reqs
    units = w_gate.shape[1] // 2
    req = lax.axis_index("req")
    z, y = req // 2, req % 2
    freqs = rope_base ** (-(np.arange(head_size // 2) * 2.0 / head_size))
    freqs = jnp.asarray(np.concatenate([freqs, freqs])[None, :], f32)
    qg, kg = q_gain[None, :], k_gain[None, :]

    def cross(array, by):
        return lax.ppermute(array, "tp", [(i, i ^ by) for i in range(tps)])

    def swap(array):
        return lax.ppermute(array, "req", [(i, i ^ 1) for i in range(reqs)])

    def along(array, by):
        return lax.ppermute(array, "req", [(i, i ^ (2 * by)) for i in range(reqs)])

    inputs = (
        lengths, k_pre, v_pre, q_new, k_new, v_new, gate_new, resid, qg, kg, freqs,
        w_out, w_gate, w_up,
    )
    outputs = (
        jax.ShapeDtypeStruct((tok, 2 * k_pre.shape[1]), bf16),
        jax.ShapeDtypeStruct((peers, pay_rows // 4, 4, lanes), bf16),
        jax.ShapeDtypeStruct((w_out.shape[0], part), bf16),
        jax.ShapeDtypeStruct((w_gate.shape[0], 2 * units), bf16),
    )
    kv, pay, w_own, pair = call(
        partial_kernel,
        outputs,
        inputs,
        scratch=[pltpu.VMEM(o.shape, o.dtype) for o in outputs]
        + [(heads * rpg, lanes)] * 4
        + [(pay_rows, lanes), pltpu.SMEM(lengths.shape, jnp.int32)]
        + [pltpu.VMEM(a.shape, a.dtype) for a in inputs[1:11]]
        + [pltpu.SemaphoreType.DMA((len(inputs),)), pltpu.SemaphoreType.DMA((len(outputs),))],
        hbm=True,
        out_any=True,
        flops=10**7,
        limit=56,
    )
    w_far = cross(w_own, 2)
    pair = swap(pair)
    half = jax.ShapeDtypeStruct((w_gate.shape[0], 2 * units), bf16)
    mine, ng = call(
        fetch_kernel,
        (half, jax.ShapeDtypeStruct((1, part), f32)),
        (w_gate, w_up, norm_gain[None, :]),
        hbm=True,
        scratch=[pltpu.SemaphoreType.DMA((3,))],
    )
    w_here, down_pair = call(
        columns_kernel,
        (
            jax.ShapeDtypeStruct(w_own.shape, bf16),
            jax.ShapeDtypeStruct((units, w_down.shape[1]), bf16),
        ),
        (w_out, w_down),
        hbm=True,
        scratch=[pltpu.SemaphoreType.DMA((2,))],
    )
    late_far, _, _ = lax.optimization_barrier((w_far, mine, w_here))
    w_near, w_both = cross(w_own, 1), cross(late_far, 1)
    kv_near = cross(kv, 1)
    late_kv, _ = lax.optimization_barrier((kv, w_far))
    kv_far = cross(late_kv, 2)
    late_down, _ = lax.optimization_barrier((down_pair, pair))
    down_pair = swap(late_down)
    got = lax.all_to_all(pay, ("req", "tp"), 0, 0, tiled=True)
    landed = hold((pair,), 2 * 10**9)
    token = hold((landed, w_near, w_both), 10**9)
    msg_shape = (2 * units // lanes * toks + 8, lanes)
    hid, msg = call(
        hidden_kernel,
        (
            jax.ShapeDtypeStruct((toks, part), f32),
            jax.ShapeDtypeStruct(msg_shape, bf16),
        ),
        (got, w_here, w_near, w_far, w_both, mine, pair, ng, token),
        scratch=[
            (heads, toks, lanes),
            (toks, part),
            (2, toks, part // 2),
            (reqs, pay_rows, lanes),
            msg_shape,
        ],
        flops=10**7,
    )
    msgs = [msg] + [along(msg, d) for d in (3, 2, 1)]
    kv_both = cross(kv_far, 1)
    prefill_out = call(
        prefill_kernel,
        jax.ShapeDtypeStruct(q_pre.shape, bf16),
        (lengths, q_pre, gate_pre, kv, kv_near, kv_far, kv_both, qg, freqs),
        scratch=[pltpu.VMEM(kv.shape, bf16)],
        smem=1,
        flops=10**9,
    )
    back = call(
        down_kernel,
        jax.ShapeDtypeStruct((peers, back_rows // 4, 4, lanes), bf16),
        (*msgs, hid, w_down, down_pair),
        scratch=[(reqs, back_rows, lanes), msg_shape],
        flops=3 * 10**9,
    )
    returned = lax.all_to_all(back, ("req", "tp"), 0, 0, tiled=True)
    returned, prefill_out = lax.optimization_barrier((returned, prefill_out))
    decode_out = call(
        final_kernel,
        jax.ShapeDtypeStruct((rpg, width), bf16),
        (returned,),
        scratch=[(slices, back_rows, lanes), (8, width)],
        flops=10**6,
    )
    return (prefill_out, decode_out)


def solution(mesh):
    return jax.shard_map(
        local,
        mesh=mesh,
        in_specs=(
            P(("req", "tp"), None),
            P(("req", "tp"), None),
            P(("req", "tp"), None),
            P(("req", "tp"), None),
            P(),
            P(),
            P("req", None),
            P("req", None),
            P("req", None),
            P("req", None),
            P("req", None),
            P("req", None),
            P("tp", None),
            P(),
            P("req", "tp"),
            P("req", "tp"),
            P("tp", "req"),
        ),
        out_specs=(P(("req", "tp"), None), P("req", None)),
        check_vma=False,
    )
```

```python
import jax
import jax.numpy as jnp
import numpy as np
from jax import lax
from jax.experimental import pallas as pl
from jax.experimental.pallas import tpu as pltpu
from jax.sharding import PartitionSpec as P

rope_base = 1000000.0
norm_eps = 1e-06


def group_layout(lengths_row, total):
    req_ends = jnp.cumsum(lengths_row)
    req_starts = req_ends - lengths_row
    indices = jnp.arange(total, dtype=jnp.int32)
    segment = jnp.sum((indices[:, None] >= req_ends[None, :]).astype(jnp.int32), axis=1)
    onehot = segment[:, None] == jnp.arange(lengths_row.shape[0], dtype=jnp.int32)[None, :]
    offsets = jnp.sum(jnp.where(onehot, req_starts[None, :], 0), axis=1)
    return (segment, indices - offsets)


def head_norm(values, gain):
    mean_sq = jnp.mean(values * values, axis=-1, keepdims=True)
    return values * lax.rsqrt(mean_sq + norm_eps) * gain


def rotate(values, position):
    half_size = values.shape[-1] // 2
    freqs = rope_base ** (-(jnp.arange(half_size, dtype=jnp.float32) * 2.0 / (2 * half_size)))
    angles = position.astype(jnp.float32)[:, None] * freqs[None, :]
    shaped = (values.shape[0],) + (1,) * (values.ndim - 2) + (half_size,)
    cosine = jnp.cos(angles).reshape(shaped)
    sine = jnp.sin(angles).reshape(shaped)
    first_half = values[..., :half_size]
    second_half = values[..., half_size:]
    return jnp.concatenate(
        [first_half * cosine - second_half * sine, second_half * cosine + first_half * sine],
        axis=-1,
    )


def general(
    q_pre,
    gate_pre,
    k_pre,
    v_pre,
    q_gain,
    k_gain,
    lengths,
    q_new,
    gate_new,
    k_new,
    v_new,
    resid,
    w_out,
    norm_gain,
    w_gate,
    w_up,
    w_down,
):
    tok_rows = q_pre.shape[0]
    tp_count = lax.axis_size("tp")
    tp_index = lax.axis_index("tp")
    head_size = q_gain.shape[0]
    query_heads = gate_pre.shape[1]
    kv_heads = k_pre.shape[1] // head_size
    groups_per = query_heads // kv_heads
    kv_local = kv_heads // tp_count
    req_count = lengths.shape[1]
    score_scale = head_size ** (-0.5)
    segment, position = group_layout(lengths[0], tok_rows * tp_count)
    row_offset = tp_index * tok_rows
    seg_local = lax.dynamic_slice_in_dim(segment, row_offset, tok_rows)
    pos_local = lax.dynamic_slice_in_dim(position, row_offset, tok_rows)
    query_index = row_offset + jnp.arange(tok_rows, dtype=jnp.int32)
    queries = rotate(
        head_norm(q_pre.reshape(tok_rows, query_heads, head_size).astype(jnp.float32), q_gain),
        pos_local,
    )
    queries = queries.astype(jnp.bfloat16).reshape(tok_rows, kv_heads, groups_per, head_size)
    keys = rotate(
        head_norm(k_pre.reshape(tok_rows, kv_heads, head_size).astype(jnp.float32), k_gain),
        pos_local,
    ).astype(jnp.bfloat16)
    values = v_pre.reshape(tok_rows, kv_heads, head_size)

    def key_block(running, key_piece, value_piece, first_row):
        key_count = key_piece.shape[0]
        key_index = first_row + jnp.arange(key_count, dtype=jnp.int32)
        allowed = (seg_local[:, None] == segment[None, :]) & (
            query_index[:, None] >= key_index[None, :]
        )
        scores = (
            jnp.einsum(
                "qkgd,pkd->qkgp",
                queries,
                key_piece.reshape(key_count, kv_heads, head_size),
                preferred_element_type=jnp.float32,
            )
            * score_scale
        )
        weights = jnp.where(allowed[:, None, None, :], jnp.exp(scores), 0.0)
        totals = running[0] + jnp.sum(weights, axis=-1)
        mixed = running[1] + jnp.einsum(
            "qkgp,pkd->qkgd",
            weights.astype(jnp.bfloat16),
            value_piece.reshape(key_count, kv_heads, head_size),
            preferred_element_type=jnp.float32,
        )
        return (totals, mixed)

    start_state = (
        jnp.zeros((tok_rows, kv_heads, groups_per), jnp.float32),
        jnp.zeros((tok_rows, kv_heads, groups_per, head_size), jnp.float32),
    )
    pieces = (
        lax.all_gather(keys.reshape(tok_rows, kv_heads * head_size), "tp", axis=0, tiled=True),
        lax.all_gather(v_pre, "tp", axis=0, tiled=True),
    )
    key_count = pieces[0].shape[0]
    block_rows = 512

    def one_block(number, carried):
        begin_at = number * block_rows
        return key_block(carried, pieces[0], pieces[1], begin_at)

    totals, mixed = lax.fori_loop(0, key_count // block_rows, one_block, start_state)
    gates = jax.nn.sigmoid(gate_pre.astype(jnp.float32)).reshape(tok_rows, kv_heads, groups_per)
    prefill_out = (
        (mixed / totals[..., None] * gates[..., None])
        .astype(jnp.bfloat16)
        .reshape(tok_rows, query_heads * head_size)
    )
    new_queries = rotate(
        head_norm(q_new.reshape(req_count, query_heads, head_size).astype(jnp.float32), q_gain),
        lengths[0],
    )
    new_queries = new_queries.astype(jnp.bfloat16).reshape(
        req_count, kv_heads, groups_per, head_size
    )
    new_keys = rotate(
        head_norm(k_new.reshape(req_count, kv_heads, head_size).astype(jnp.float32), k_gain),
        lengths[0],
    ).astype(jnp.bfloat16)
    new_values = v_new.reshape(req_count, kv_heads, head_size)
    new_gates = jax.nn.sigmoid(gate_new.astype(jnp.float32)).reshape(
        req_count, kv_heads, groups_per
    )
    head_first = tp_index * kv_local
    request_ids = jnp.arange(req_count, dtype=jnp.int32)
    own_queries = lax.dynamic_slice_in_dim(new_queries, head_first, kv_local, 1)
    cache_keys, cache_values = (
        lax.all_to_all(keys, "tp", split_axis=1, concat_axis=0, tiled=True),
        lax.all_to_all(values, "tp", split_axis=1, concat_axis=0, tiled=True),
    )
    scores = (
        jnp.einsum("rkgd,pkd->rkgp", own_queries, cache_keys, preferred_element_type=jnp.float32)
        * score_scale
    )
    owned = segment[None, :] == request_ids[:, None]
    weights = jnp.where(owned[:, None, None, :], jnp.exp(scores), 0.0)
    weighted = jnp.einsum(
        "rkgp,pkd->rkgd",
        weights.astype(jnp.bfloat16),
        cache_values,
        preferred_element_type=jnp.float32,
    )
    dec_totals = jnp.sum(weights, axis=-1)
    dec_mixed = weighted
    own_keys = lax.dynamic_slice_in_dim(new_keys, head_first, kv_local, 1)
    own_values = lax.dynamic_slice_in_dim(new_values, head_first, kv_local, 1)
    own_gates = lax.dynamic_slice_in_dim(new_gates, head_first, kv_local, 1)
    self_weight = jnp.exp(
        jnp.einsum("rkgd,rkd->rkg", own_queries, own_keys, preferred_element_type=jnp.float32)
        * score_scale
    )
    dec_totals = dec_totals + self_weight
    dec_mixed = dec_mixed + self_weight[..., None] * own_values.astype(jnp.float32)[:, :, None, :]
    attended = (
        (dec_mixed / dec_totals[..., None] * own_gates[..., None])
        .astype(jnp.bfloat16)
        .reshape(req_count, kv_local * groups_per * head_size)
    )
    partial_out = jnp.dot(attended, w_out, preferred_element_type=jnp.float32)
    attn_rows = lax.psum(partial_out, "tp")
    hidden_state = resid.astype(jnp.float32) + attn_rows
    mean_sq = jnp.mean(hidden_state * hidden_state, axis=-1, keepdims=True)
    normed = (hidden_state * lax.rsqrt(mean_sq + norm_eps) * norm_gain).astype(jnp.bfloat16)
    units_local = w_gate.shape[1]
    paired = jnp.concatenate([w_gate, w_up], axis=1)
    columns = lax.all_to_all(normed, "req", split_axis=1, concat_axis=0, tiled=True)
    whole_sums = lax.psum(jnp.dot(columns, paired, preferred_element_type=jnp.float32), "req")
    hidden_units = (jax.nn.silu(whole_sums[:, :units_local]) * whole_sums[:, units_local:]).astype(
        jnp.bfloat16
    )
    down_part = jnp.dot(hidden_units, w_down, preferred_element_type=jnp.float32)
    back_part = lax.all_to_all(down_part, "req", split_axis=0, concat_axis=1, tiled=True)
    mlp_rows = lax.psum(back_part, "tp")
    decode_out = (hidden_state + mlp_rows).astype(jnp.bfloat16)
    return (prefill_out, decode_out)


f32 = jnp.float32
bf16 = jnp.bfloat16
lanes = 128
pay_rows = 28
back_rows = 12


def dot(a, b):
    return jnp.dot(a, b, preferred_element_type=f32)


def dot_nt(a, b):
    return lax.dot_general(a, b, (((1,), (1,)), ((), ())), preferred_element_type=f32)


def iota(shape, dim):
    return lax.broadcasted_iota(jnp.int32, shape, dim)


def rope_factors(angles):
    turns = jnp.floor(angles * (2.0 / np.pi) + 0.5)
    rest = angles - turns * 1.5703125
    rest = rest - turns * 4.837512969970703125e-4
    rest = rest - turns * 7.549789948768648e-8
    sq = rest * rest
    sine = ((-1.9515295891e-4 * sq + 8.3321608736e-3) * sq - 1.6666654611e-1) * sq * rest + rest
    cosine = (
        ((2.443315711809948e-5 * sq - 1.388731625493765e-3) * sq + 4.166664568298827e-2) * sq * sq
        - 0.5 * sq
        + 1.0
    )
    low = iota(angles.shape, 1) < lanes // 2
    quarter = turns.astype(jnp.int32) + jnp.where(low, 1, 0)
    both = jnp.where((quarter & 1) == 1, cosine, sine)
    both = jnp.where((quarter & 2) == 2, -both, both)
    swapped = pltpu.roll(both, lanes // 2, 1)
    return jnp.where(low, both, swapped), jnp.where(low, -swapped, both)


def norm_rope(values, gain, factors):
    mean_sq = jnp.mean(values * values, axis=-1, keepdims=True)
    normed = values * lax.rsqrt(mean_sq + norm_eps) * gain
    return (normed * factors[0] + pltpu.roll(normed, lanes // 2, 1) * factors[1]).astype(bf16)


def begin_of(indices, len_ref):
    begin = jnp.zeros_like(indices)
    end = 0
    for j in range(len_ref.shape[1] - 1):
        end = end + len_ref[0, j]
        begin = jnp.where(indices >= end, end, begin)
    return begin


def partial_kernel(
    len_hbm, k_hbm, v_hbm, qn_hbm, kn_hbm, vn_hbm, gn_hbm, resid_hbm, qg_hbm, kg_hbm, freq_hbm,
    w_hbm, gate_hbm, up_hbm,
    kv_hbm, pay_hbm, own_hbm, pair_hbm,
    kv_ref, pay_ref, own_ref, pair_ref, row_q, row_k, row_v, row_g, pay, len_ref, k_ref, v_ref, qn_ref, kn_ref, vn_ref, gn_ref,
    resid_ref, qg_ref, kg_ref, freq_ref, sems, out_sems,
):
    tp = lax.axis_index("tp")
    req = lax.axis_index("req")
    z, other = lax.div(req, 2), 1 - lax.rem(req, 2)
    width = own_ref.shape[1]
    units = pair_ref.shape[1] // 2
    cols = pl.ds(pl.multiple_of(z * width, lanes), width)
    theirs = pl.ds(pl.multiple_of(other * units, lanes), units)
    moves = (
        (len_hbm, len_ref), (freq_hbm, freq_ref), (k_hbm, k_ref), (kg_hbm, kg_ref),
        (qn_hbm, qn_ref), (kn_hbm, kn_ref), (vn_hbm, vn_ref), (gn_hbm, gn_ref), (qg_hbm, qg_ref),
        (v_hbm, v_ref), (resid_hbm, resid_ref),
        (gate_hbm.at[:, theirs], pair_ref.at[:, pl.ds(0, units)]),
        (up_hbm.at[:, theirs], pair_ref.at[:, pl.ds(units, units)]),
        (w_hbm.at[:, cols], own_ref),
    )
    copies = [pltpu.make_async_copy(a, b, sems.at[i]) for i, (a, b) in enumerate(moves)]
    for copy in copies:
        copy.start()
    ends = (
        (pair_ref, pair_hbm), (own_ref, own_hbm), (kv_ref, kv_hbm), (pay_ref, pay_hbm),
    )
    leave = [pltpu.make_async_copy(a, b, out_sems.at[i]) for i, (a, b) in enumerate(ends)]
    tok = k_ref.shape[0]
    rpg = qn_ref.shape[0]
    heads = qn_ref.shape[1] // lanes
    kvs = k_ref.shape[1] // lanes
    per = heads // kvs
    rows = heads * rpg
    for copy in copies[:2]:
        copy.wait()
    freq = freq_ref[...]
    tok_index = tp * tok + iota((tok, lanes), 0)
    factors = rope_factors((tok_index - begin_of(tok_index, len_ref)).astype(f32) * freq)
    for copy in copies[2:11]:
        copy.wait()
    qg, kg = qg_ref[...], kg_ref[...]
    keys = []
    for k in range(kvs):
        at = slice(k * lanes, (k + 1) * lanes)
        keys.append(norm_rope(k_ref[:, at].astype(f32), kg, factors))
        kv_ref[:, at] = keys[-1]
    kv_ref[:, kvs * lanes :] = v_ref[...]
    for copy in copies[11:]:
        copy.wait()
    for copy in leave[:3]:
        copy.start()
    qn, kn = qn_ref[...].astype(f32), kn_ref[...].astype(f32)
    vn, gn = vn_ref[...].astype(f32), gn_ref[...].astype(f32)
    for h in range(heads):
        at = slice(h * rpg, (h + 1) * rpg)
        kv = slice((h // per) * lanes, (h // per + 1) * lanes)
        row_q[at, :] = qn[:, h * lanes : (h + 1) * lanes]
        row_k[at, :] = kn[:, kv]
        row_v[at, :] = vn[:, kv]
        row_g[at, :] = jnp.broadcast_to(gn[:, h : h + 1], (rpg, lanes))
    row = iota((rows, lanes), 0)
    col = iota((rows, lanes), 1)
    head = row * 0
    for h in range(1, heads):
        head = jnp.where(row >= h * rpg, h, head)
    request = row - head * rpg
    length, first, last = row * 0, row * 0, row * 0
    end = 0
    for j in range(rpg):
        mine = request == j
        length = jnp.where(mine, len_ref[0, j], length)
        first = jnp.where(mine, end, first)
        end = end + len_ref[0, j]
        last = jnp.where(mine, end, last)
    new_factors = rope_factors(length.astype(f32) * freq)
    scale = lanes ** (-0.5)
    new_q = norm_rope(row_q[0:rows, :], qg, new_factors)
    new_k = norm_rope(row_k[0:rows, :], kg, new_factors)
    scores = jnp.zeros((rows, tok), f32)
    for k in range(kvs):
        mine = (head >= k * per) & (head < (k + 1) * per)
        scores = jnp.where(mine, dot_nt(new_q, keys[k]), scores)
    index = tp * tok + col
    weights = jnp.where((index >= first) & (index < last), jnp.exp(scores * scale), 0.0)
    totals = jnp.sum(weights, axis=-1, keepdims=True)
    rounded = weights.astype(bf16)
    mixed = jnp.zeros((rows, lanes), f32)
    for k in range(kvs):
        mine = (head >= k * per) & (head < (k + 1) * per)
        mixed = mixed + dot(
            jnp.where(mine, rounded, jnp.zeros_like(rounded)), v_ref[:, k * lanes : (k + 1) * lanes]
        )
    self_score = jnp.sum(new_q.astype(f32) * new_k.astype(f32), axis=-1, keepdims=True)
    self_weight = jnp.where(tp == 0, jnp.exp(self_score * scale), 0.0)
    totals = totals + self_weight
    mixed = (mixed + self_weight * row_v[0:rows, :]) * jax.nn.sigmoid(row_g[0:rows, :])
    total_row = jnp.sum(jnp.where(row == col, totals, 0.0), axis=0, keepdims=True)
    high = total_row.astype(bf16).astype(f32)
    rest = pltpu.roll(jnp.broadcast_to(total_row - high, (8, lanes)), lanes // 2, 1)
    pay[0:rows, :] = mixed
    pay[rows + rpg : rows + rpg + 1, :] = jnp.where(
        iota((1, lanes), 1) < lanes // 2, high, rest[0:1, :]
    )
    peers = pay_ref.shape[0]
    tps = lax.axis_size("tp")
    slices = resid_ref.shape[1] // (tps * lanes)
    for z in range(slices):
        at = pl.ds(pl.multiple_of((z * tps + tp) * lanes, lanes), lanes)
        pay[rows : rows + rpg, :] = resid_ref[:, at].astype(f32)
        for g in range(pay_ref.shape[1]):
            out = pay[4 * g : 4 * g + 4, :].astype(bf16)
            for peer in range(z * peers // slices, (z + 1) * peers // slices):
                pay_ref[peer, g] = out
    leave[3].start()
    for copy in leave:
        copy.wait()


def fetch_kernel(gate_hbm, up_hbm, ng_hbm, mine_ref, ng_ref, sems):
    units = mine_ref.shape[1] // 2
    width = ng_ref.shape[1]
    req = lax.axis_index("req")
    at = pl.ds(pl.multiple_of(lax.rem(req, 2) * units, lanes), units)
    cols = pl.ds(pl.multiple_of(lax.div(req, 2) * width, lanes), width)
    copies = (
        pltpu.make_async_copy(gate_hbm.at[:, at], mine_ref.at[:, pl.ds(0, units)], sems.at[0]),
        pltpu.make_async_copy(up_hbm.at[:, at], mine_ref.at[:, pl.ds(units, units)], sems.at[1]),
        pltpu.make_async_copy(ng_hbm.at[:, cols], ng_ref, sems.at[2]),
    )
    for copy in copies:
        copy.start()
    for copy in copies:
        copy.wait()


def columns_kernel(w_hbm, down_hbm, w_ref, down_ref, sems):
    width = w_ref.shape[1]
    units = down_ref.shape[0]
    req = lax.axis_index("req")
    cols = pl.ds(pl.multiple_of(lax.div(req, 2) * width, lanes), width)
    theirs = pl.ds(pl.multiple_of((1 - lax.rem(req, 2)) * units, lanes), units)
    copies = (
        pltpu.make_async_copy(w_hbm.at[:, cols], w_ref, sems.at[0]),
        pltpu.make_async_copy(down_hbm.at[theirs, :], down_ref, sems.at[1]),
    )
    for copy in copies:
        copy.start()
    for copy in copies:
        copy.wait()


def ready_kernel(*refs):
    refs[-1][...] = jnp.zeros_like(refs[-1])


def hidden_kernel(
    pay_ref, w0_ref, w1_ref, w2_ref, w3_ref, mine_ref, pair_ref, ng_ref, _,
    hid_ref, msg_ref, att, hid, xs, acc, out,
):
    tp = lax.axis_index("tp")
    req = lax.axis_index("req")
    tps = lax.axis_size("tp")
    z, y = lax.div(req, 2), lax.rem(req, 2)
    heads, toks = att.shape[0], hid_ref.shape[0]
    groups = pay_ref.shape[0] // tps
    rpg = toks // groups
    rows = heads * rpg
    diag = iota((rows, lanes), 0) == iota((rows, lanes), 1)
    quads = pay_ref.shape[1]
    for r in range(groups):
        for g in range(quads):
            total = jnp.zeros((4, lanes), f32)
            for t in range(tps):
                piece = pay_ref[r * tps + t, g].astype(f32)
                total = total + piece
                if g == quads - 1:
                    hid[r * rpg : (r + 1) * rpg, t * lanes : (t + 1) * lanes] = piece[:rpg, :]
            acc[r, 4 * g : 4 * g + 4, :] = total
    for r in range(groups):
        total_row = jnp.broadcast_to(acc[r, pay_rows - 1 : pay_rows, :], (rows, lanes))
        total_row = total_row + pltpu.roll(total_row, lanes // 2, 1)
        totals = jnp.sum(jnp.where(diag, total_row, 0.0), axis=-1, keepdims=True)
        acc[r, 0:rows, :] = acc[r, 0:rows, :] / totals
    for r in range(groups):
        for h in range(heads):
            att[h, r * rpg : (r + 1) * rpg, :] = acc[r, h * rpg : (h + 1) * rpg, :]
    state = hid[0:toks, :]
    per = heads // tps
    for d, w_ref in enumerate((w0_ref, w1_ref, w2_ref, w3_ref)):
        source = tp ^ d
        for j in range(per):
            state = state + dot(
                att[source * per + j, 0:toks, :].astype(bf16), w_ref[j * lanes : (j + 1) * lanes, :]
            )
    hid_ref[...] = state
    width = state.shape[1]
    half = width // 2
    sums = jnp.sum(state * state, axis=-1, keepdims=True)
    scaled = state * ng_ref[...]
    xs[0] = scaled[:, :half]
    xs[1] = scaled[:, half:]
    own, other = xs[y].astype(bf16), xs[1 - y].astype(bf16)
    units = pair_ref.shape[1] // 2
    gate = dot(own, mine_ref[:, :units]) + dot(other, pair_ref[:, :units])
    up = dot(own, mine_ref[:, units:]) + dot(other, pair_ref[:, units:])
    square = iota((toks, lanes), 0) == iota((toks, lanes), 1)
    sums_row = jnp.sum(jnp.where(square, sums, 0.0), axis=0, keepdims=True)
    high = sums_row.astype(bf16).astype(f32)
    blocks = units // lanes
    for i in range(blocks):
        at = slice(i * lanes, (i + 1) * lanes)
        out[i * toks : (i + 1) * toks, :] = gate[:, at]
        out[(blocks + i) * toks : (blocks + i + 1) * toks, :] = up[:, at]
    base = 2 * blocks * toks
    first = iota((8, lanes), 0)
    out[base : base + 8, :] = jnp.where(
        first == 0, high, jnp.where(first == 1, sums_row - high, 0.0)
    )
    msg_ref[...] = out[0 : msg_ref.shape[0], :].astype(bf16)


def down_kernel(m0_ref, m1_ref, m2_ref, m3_ref, hid_ref, down_ref, pair_ref, back_ref, pay, whole):
    tp = lax.axis_index("tp")
    tps = lax.axis_size("tp")
    y = lax.rem(lax.axis_index("req"), 2)
    units, half = pair_ref.shape
    toks, width = hid_ref.shape
    total = m0_ref[...].astype(f32)
    for m_ref in (m1_ref, m2_ref, m3_ref):
        total = total + m_ref[...].astype(f32)
    whole[0 : total.shape[0], :] = total
    blocks = units // lanes
    base = 2 * blocks * toks
    square = iota((toks, lanes), 0) == iota((toks, lanes), 1)
    sums_row = whole[base : base + 1, :] + whole[base + 1 : base + 2, :]
    sums = jnp.sum(
        jnp.where(square, jnp.broadcast_to(sums_row, (toks, lanes)), 0.0), axis=-1, keepdims=True
    )
    factor = lax.rsqrt(sums / (width * 4) + norm_eps)
    pieces = []
    for i in range(blocks):
        gate = whole[i * toks : (i + 1) * toks, :] * factor
        up = whole[(blocks + i) * toks : (blocks + i + 1) * toks, :] * factor
        pieces.append((gate / (1.0 + jnp.exp(-gate)) * up).astype(bf16))
    hidden = jnp.concatenate(pieces, axis=1)
    own_rows = pl.ds(pl.multiple_of(y * units, lanes), units)
    mine, theirs = dot(hidden, down_ref[own_rows, :]), dot(hidden, pair_ref[...])
    part = (jnp.where(y == 0, mine, theirs), jnp.where(y == 0, theirs, mine))
    chunks = width // lanes
    groups = pay.shape[0]
    rpg = toks // groups
    for c in range(chunks):
        at = (c * lanes) % half
        block = part[c * lanes // half][:, at : at + lanes]
        adds = (y == 0) & (tp == c)
        block = block + jnp.where(adds, hid_ref[:, c * lanes : (c + 1) * lanes], 0.0)
        for r in range(groups):
            pay[r, c * rpg : (c + 1) * rpg, :] = block[r * rpg : (r + 1) * rpg, :]
    for r in range(groups):
        for g in range(back_ref.shape[1]):
            out = pay[r, 4 * g : 4 * g + 4, :].astype(bf16)
            for t in range(tps):
                back_ref[r * tps + t, g] = out


def final_kernel(back_ref, out_ref, acc, rows_out):
    tps = lax.axis_size("tp")
    peers = back_ref.shape[0]
    rpg, width = out_ref.shape
    slices = acc.shape[0]
    group = peers // slices
    chunks = width // (slices * lanes)
    for z in range(slices):
        for g in range(back_ref.shape[1]):
            total = back_ref[z * group, g].astype(f32)
            for p in range(1, group):
                total = total + back_ref[z * group + p, g].astype(f32)
            acc[z, 4 * g : 4 * g + 4, :] = total
    for z in range(slices):
        for c in range(chunks):
            at = slice((z * chunks + c) * lanes, (z * chunks + c + 1) * lanes)
            rows_out[0:rpg, at] = acc[z, c * rpg : (c + 1) * rpg, :]
    out_ref[...] = rows_out[0:rpg, :].astype(bf16)


def prefill_kernel(
    len_ref, q_ref, g_ref, kv0_ref, kv1_ref, kv2_ref, kv3_ref, qg_ref, freq_ref, out_ref, mid_ref
):
    tp = lax.axis_index("tp")
    tok = q_ref.shape[0]
    heads = q_ref.shape[1] // lanes
    kvs = kv0_ref.shape[1] // (2 * lanes)
    per = heads // kvs
    third = tp == 2
    mid_ref[...] = jnp.where(third, kv3_ref[...], kv1_ref[...])
    blocks = ((tp, kv0_ref), (jnp.where(third, tp ^ 3, tp ^ 1), mid_ref), (tp ^ 2, kv2_ref))
    tok_index = tp * tok + iota((tok, lanes), 0)
    begin = begin_of(tok_index, len_ref)
    factors = rope_factors((tok_index - begin).astype(f32) * freq_ref[...])
    col = iota((tok, tok), 1)
    allowed = []
    for block, _ in blocks:
        key_index = block * tok + col
        allowed.append((key_index >= begin) & (key_index <= tok_index))
    gates = jax.nn.sigmoid(g_ref[...].astype(f32))
    qg = qg_ref[...]
    scale = lanes ** (-0.5)
    for h in range(heads):
        k = h // per
        at = slice(h * lanes, (h + 1) * lanes)
        query = norm_rope(q_ref[:, at].astype(f32), qg, factors)
        totals = jnp.zeros((tok, 1), f32)
        mixed = jnp.zeros((tok, lanes), f32)
        for b, (_, kv_ref) in enumerate(blocks):
            scores = dot_nt(query, kv_ref[:, k * lanes : (k + 1) * lanes])
            weights = jnp.where(allowed[b], jnp.exp(scores * scale), 0.0)
            totals = totals + jnp.sum(weights, axis=-1, keepdims=True)
            mixed = mixed + dot(
                weights.astype(bf16), kv_ref[:, (kvs + k) * lanes : (kvs + k + 1) * lanes]
            )
        out_ref[:, at] = (mixed / totals * gates[:, h : h + 1]).astype(bf16)


def room(rows):
    return (rows + 15) // 8 * 8


def call(body, out_shape, args, scratch=(), hbm=False, out_any=False, smem=0, flops=0, limit=12):
    specs = [pl.BlockSpec(memory_space=pltpu.SMEM)] * smem
    space = pltpu.HBM if hbm else pltpu.VMEM
    specs += [pl.BlockSpec(memory_space=space)] * (len(args) - smem)
    size = sum(a.size * a.dtype.itemsize for a in args)
    return pl.pallas_call(
        body,
        out_shape=out_shape,
        in_specs=specs,
        out_specs=jax.tree.map(
            lambda _: pl.BlockSpec(memory_space=pl.ANY if out_any else pltpu.VMEM), out_shape
        ),
        scratch_shapes=[pltpu.VMEM(s, f32) if isinstance(s, tuple) else s for s in scratch],
        compiler_params=pltpu.CompilerParams(vmem_limit_bytes=limit * 2**20),
        cost_estimate=pl.CostEstimate(flops=flops, bytes_accessed=size, transcendentals=0),
    )(*args)


def hold(arrays, flops):
    return pl.pallas_call(
        ready_kernel,
        out_shape=jax.ShapeDtypeStruct((8, lanes), f32),
        in_specs=[pl.BlockSpec(memory_space=pl.ANY)] * len(arrays),
        out_specs=pl.BlockSpec(memory_space=pltpu.VMEM),
        compiler_params=pltpu.CompilerParams(vmem_limit_bytes=2**20),
        cost_estimate=pl.CostEstimate(flops=flops, bytes_accessed=0, transcendentals=0),
    )(*arrays)


def local(
    q_pre,
    gate_pre,
    k_pre,
    v_pre,
    q_gain,
    k_gain,
    lengths,
    q_new,
    gate_new,
    k_new,
    v_new,
    resid,
    w_out,
    norm_gain,
    w_gate,
    w_up,
    w_down,
):
    tps, reqs = lax.axis_size("tp"), lax.axis_size("req")
    tok = q_pre.shape[0]
    rpg, width = resid.shape
    slices = reqs // 2
    head_size = q_gain.shape[0]
    heads = gate_pre.shape[1]
    part = width // slices if slices else 0
    if not (slices == 4 and tps == 4 and head_size == lanes == tok and part == tps * lanes):
        return general(
            q_pre, gate_pre, k_pre, v_pre, q_gain, k_gain, lengths, q_new, gate_new, k_new, v_new,
            resid, w_out, norm_gain, w_gate, w_up, w_down,
        )
    peers = tps * reqs
    toks = rpg * reqs
    units = w_gate.shape[1] // 2
    req = lax.axis_index("req")
    z, y = req // 2, req % 2
    freqs = rope_base ** (-(np.arange(head_size // 2) * 2.0 / head_size))
    freqs = jnp.asarray(np.concatenate([freqs, freqs])[None, :], f32)
    qg, kg = q_gain[None, :], k_gain[None, :]

    def cross(array, by):
        return lax.ppermute(array, "tp", [(i, i ^ by) for i in range(tps)])

    def swap(array):
        return lax.ppermute(array, "req", [(i, i ^ 1) for i in range(reqs)])

    def along(array, by):
        return lax.ppermute(array, "req", [(i, i ^ (2 * by)) for i in range(reqs)])

    inputs = (
        lengths, k_pre, v_pre, q_new, k_new, v_new, gate_new, resid, qg, kg, freqs,
        w_out, w_gate, w_up,
    )
    outputs = (
        jax.ShapeDtypeStruct((tok, 2 * k_pre.shape[1]), bf16),
        jax.ShapeDtypeStruct((peers, pay_rows // 4, 4, lanes), bf16),
        jax.ShapeDtypeStruct((w_out.shape[0], part), bf16),
        jax.ShapeDtypeStruct((w_gate.shape[0], 2 * units), bf16),
    )
    kv, pay, w_own, pair = call(
        partial_kernel,
        outputs,
        inputs,
        scratch=[pltpu.VMEM(o.shape, o.dtype) for o in outputs]
        + [(room(heads * rpg), lanes)] * 4
        + [(room(pay_rows), lanes), pltpu.SMEM(lengths.shape, jnp.int32)]
        + [pltpu.VMEM(a.shape, a.dtype) for a in inputs[1:11]]
        + [pltpu.SemaphoreType.DMA((len(inputs),)), pltpu.SemaphoreType.DMA((len(outputs),))],
        hbm=True,
        out_any=True,
        flops=10**7,
        limit=56,
    )
    w_far = cross(w_own, 2)
    pair = swap(pair)
    half = jax.ShapeDtypeStruct((w_gate.shape[0], 2 * units), bf16)
    mine, ng = call(
        fetch_kernel,
        (half, jax.ShapeDtypeStruct((1, part), f32)),
        (w_gate, w_up, norm_gain[None, :]),
        hbm=True,
        scratch=[pltpu.SemaphoreType.DMA((3,))],
    )
    w_here, down_pair = call(
        columns_kernel,
        (
            jax.ShapeDtypeStruct(w_own.shape, bf16),
            jax.ShapeDtypeStruct((units, w_down.shape[1]), bf16),
        ),
        (w_out, w_down),
        hbm=True,
        scratch=[pltpu.SemaphoreType.DMA((2,))],
    )
    late_far, _, _ = lax.optimization_barrier((w_far, mine, w_here))
    w_near, w_both = cross(w_own, 1), cross(late_far, 1)
    kv_near = cross(kv, 1)
    late_kv, _ = lax.optimization_barrier((kv, w_far))
    kv_far = cross(late_kv, 2)
    late_down, _ = lax.optimization_barrier((down_pair, pair))
    down_pair = swap(late_down)
    got = lax.all_to_all(pay, ("req", "tp"), 0, 0, tiled=True)
    landed = hold((pair,), 2 * 10**9)
    token = hold((landed, w_near, w_both), 10**9)
    msg_shape = (2 * units // lanes * toks + 8, lanes)
    hid, msg = call(
        hidden_kernel,
        (
            jax.ShapeDtypeStruct((toks, part), f32),
            jax.ShapeDtypeStruct(msg_shape, bf16),
        ),
        (got, w_here, w_near, w_far, w_both, mine, pair, ng, token),
        scratch=[
            (heads, room(toks), lanes),
            (room(toks), part),
            (2, toks, part // 2),
            (reqs, room(pay_rows), lanes),
            (room(msg_shape[0]), lanes),
        ],
        flops=10**7,
    )
    msgs = [msg] + [along(msg, d) for d in (3, 2, 1)]
    kv_both = cross(kv_far, 1)
    prefill_out = call(
        prefill_kernel,
        jax.ShapeDtypeStruct(q_pre.shape, bf16),
        (lengths, q_pre, gate_pre, kv, kv_near, kv_far, kv_both, qg, freqs),
        scratch=[pltpu.VMEM(kv.shape, bf16)],
        smem=1,
        flops=10**9,
    )
    back = call(
        down_kernel,
        jax.ShapeDtypeStruct((peers, back_rows // 4, 4, lanes), bf16),
        (*msgs, hid, w_down, down_pair),
        scratch=[(reqs, room(back_rows), lanes), (room(msg_shape[0]), lanes)],
        flops=3 * 10**9,
    )
    returned = lax.all_to_all(back, ("req", "tp"), 0, 0, tiled=True)
    returned, prefill_out = lax.optimization_barrier((returned, prefill_out))
    decode_out = call(
        final_kernel,
        jax.ShapeDtypeStruct((rpg, width), bf16),
        (returned,),
        scratch=[(slices, room(back_rows), lanes), (room(rpg), width)],
        flops=10**6,
    )
    return (prefill_out, decode_out)


def solution(mesh):
    return jax.shard_map(
        local,
        mesh=mesh,
        in_specs=(
            P(("req", "tp"), None),
            P(("req", "tp"), None),
            P(("req", "tp"), None),
            P(("req", "tp"), None),
            P(),
            P(),
            P("req", None),
            P("req", None),
            P("req", None),
            P("req", None),
            P("req", None),
            P("req", None),
            P("tp", None),
            P(),
            P("req", "tp"),
            P("req", "tp"),
            P("tp", "req"),
        ),
        out_specs=(P(("req", "tp"), None), P("req", None)),
        check_vma=False,
    )
```

```python
import jax
import jax.numpy as jnp
import numpy as np
from jax import lax
from jax.experimental import pallas as pl
from jax.experimental.pallas import tpu as pltpu
from jax.sharding import PartitionSpec as P

rope_base = 1000000.0
norm_eps = 1e-06


def group_layout(lengths_row, total):
    req_ends = jnp.cumsum(lengths_row)
    req_starts = req_ends - lengths_row
    indices = jnp.arange(total, dtype=jnp.int32)
    segment = jnp.sum((indices[:, None] >= req_ends[None, :]).astype(jnp.int32), axis=1)
    onehot = segment[:, None] == jnp.arange(lengths_row.shape[0], dtype=jnp.int32)[None, :]
    offsets = jnp.sum(jnp.where(onehot, req_starts[None, :], 0), axis=1)
    return (segment, indices - offsets)


def head_norm(values, gain):
    mean_sq = jnp.mean(values * values, axis=-1, keepdims=True)
    return values * lax.rsqrt(mean_sq + norm_eps) * gain


def rotate(values, position):
    half_size = values.shape[-1] // 2
    freqs = rope_base ** (-(jnp.arange(half_size, dtype=jnp.float32) * 2.0 / (2 * half_size)))
    angles = position.astype(jnp.float32)[:, None] * freqs[None, :]
    shaped = (values.shape[0],) + (1,) * (values.ndim - 2) + (half_size,)
    cosine = jnp.cos(angles).reshape(shaped)
    sine = jnp.sin(angles).reshape(shaped)
    first_half = values[..., :half_size]
    second_half = values[..., half_size:]
    return jnp.concatenate(
        [first_half * cosine - second_half * sine, second_half * cosine + first_half * sine],
        axis=-1,
    )


def general(
    q_pre,
    gate_pre,
    k_pre,
    v_pre,
    q_gain,
    k_gain,
    lengths,
    q_new,
    gate_new,
    k_new,
    v_new,
    resid,
    w_out,
    norm_gain,
    w_gate,
    w_up,
    w_down,
):
    tok_rows = q_pre.shape[0]
    tp_count = lax.axis_size("tp")
    tp_index = lax.axis_index("tp")
    head_size = q_gain.shape[0]
    query_heads = gate_pre.shape[1]
    kv_heads = k_pre.shape[1] // head_size
    groups_per = query_heads // kv_heads
    kv_local = kv_heads // tp_count
    req_count = lengths.shape[1]
    score_scale = head_size ** (-0.5)
    segment, position = group_layout(lengths[0], tok_rows * tp_count)
    row_offset = tp_index * tok_rows
    seg_local = lax.dynamic_slice_in_dim(segment, row_offset, tok_rows)
    pos_local = lax.dynamic_slice_in_dim(position, row_offset, tok_rows)
    query_index = row_offset + jnp.arange(tok_rows, dtype=jnp.int32)
    queries = rotate(
        head_norm(q_pre.reshape(tok_rows, query_heads, head_size).astype(jnp.float32), q_gain),
        pos_local,
    )
    queries = queries.astype(jnp.bfloat16).reshape(tok_rows, kv_heads, groups_per, head_size)
    keys = rotate(
        head_norm(k_pre.reshape(tok_rows, kv_heads, head_size).astype(jnp.float32), k_gain),
        pos_local,
    ).astype(jnp.bfloat16)
    values = v_pre.reshape(tok_rows, kv_heads, head_size)

    def key_block(running, key_piece, value_piece, first_row):
        key_count = key_piece.shape[0]
        key_index = first_row + jnp.arange(key_count, dtype=jnp.int32)
        allowed = (seg_local[:, None] == segment[None, :]) & (
            query_index[:, None] >= key_index[None, :]
        )
        scores = (
            jnp.einsum(
                "qkgd,pkd->qkgp",
                queries,
                key_piece.reshape(key_count, kv_heads, head_size),
                preferred_element_type=jnp.float32,
            )
            * score_scale
        )
        weights = jnp.where(allowed[:, None, None, :], jnp.exp(scores), 0.0)
        totals = running[0] + jnp.sum(weights, axis=-1)
        mixed = running[1] + jnp.einsum(
            "qkgp,pkd->qkgd",
            weights.astype(jnp.bfloat16),
            value_piece.reshape(key_count, kv_heads, head_size),
            preferred_element_type=jnp.float32,
        )
        return (totals, mixed)

    start_state = (
        jnp.zeros((tok_rows, kv_heads, groups_per), jnp.float32),
        jnp.zeros((tok_rows, kv_heads, groups_per, head_size), jnp.float32),
    )
    pieces = (
        lax.all_gather(keys.reshape(tok_rows, kv_heads * head_size), "tp", axis=0, tiled=True),
        lax.all_gather(v_pre, "tp", axis=0, tiled=True),
    )
    key_count = pieces[0].shape[0]
    block_rows = 512

    def one_block(number, carried):
        begin_at = number * block_rows
        return key_block(carried, pieces[0], pieces[1], begin_at)

    totals, mixed = lax.fori_loop(0, key_count // block_rows, one_block, start_state)
    gates = jax.nn.sigmoid(gate_pre.astype(jnp.float32)).reshape(tok_rows, kv_heads, groups_per)
    prefill_out = (
        (mixed / totals[..., None] * gates[..., None])
        .astype(jnp.bfloat16)
        .reshape(tok_rows, query_heads * head_size)
    )
    new_queries = rotate(
        head_norm(q_new.reshape(req_count, query_heads, head_size).astype(jnp.float32), q_gain),
        lengths[0],
    )
    new_queries = new_queries.astype(jnp.bfloat16).reshape(
        req_count, kv_heads, groups_per, head_size
    )
    new_keys = rotate(
        head_norm(k_new.reshape(req_count, kv_heads, head_size).astype(jnp.float32), k_gain),
        lengths[0],
    ).astype(jnp.bfloat16)
    new_values = v_new.reshape(req_count, kv_heads, head_size)
    new_gates = jax.nn.sigmoid(gate_new.astype(jnp.float32)).reshape(
        req_count, kv_heads, groups_per
    )
    head_first = tp_index * kv_local
    request_ids = jnp.arange(req_count, dtype=jnp.int32)
    own_queries = lax.dynamic_slice_in_dim(new_queries, head_first, kv_local, 1)
    cache_keys, cache_values = (
        lax.all_to_all(keys, "tp", split_axis=1, concat_axis=0, tiled=True),
        lax.all_to_all(values, "tp", split_axis=1, concat_axis=0, tiled=True),
    )
    scores = (
        jnp.einsum("rkgd,pkd->rkgp", own_queries, cache_keys, preferred_element_type=jnp.float32)
        * score_scale
    )
    owned = segment[None, :] == request_ids[:, None]
    weights = jnp.where(owned[:, None, None, :], jnp.exp(scores), 0.0)
    weighted = jnp.einsum(
        "rkgp,pkd->rkgd",
        weights.astype(jnp.bfloat16),
        cache_values,
        preferred_element_type=jnp.float32,
    )
    dec_totals = jnp.sum(weights, axis=-1)
    dec_mixed = weighted
    own_keys = lax.dynamic_slice_in_dim(new_keys, head_first, kv_local, 1)
    own_values = lax.dynamic_slice_in_dim(new_values, head_first, kv_local, 1)
    own_gates = lax.dynamic_slice_in_dim(new_gates, head_first, kv_local, 1)
    self_weight = jnp.exp(
        jnp.einsum("rkgd,rkd->rkg", own_queries, own_keys, preferred_element_type=jnp.float32)
        * score_scale
    )
    dec_totals = dec_totals + self_weight
    dec_mixed = dec_mixed + self_weight[..., None] * own_values.astype(jnp.float32)[:, :, None, :]
    attended = (
        (dec_mixed / dec_totals[..., None] * own_gates[..., None])
        .astype(jnp.bfloat16)
        .reshape(req_count, kv_local * groups_per * head_size)
    )
    partial_out = jnp.dot(attended, w_out, preferred_element_type=jnp.float32)
    attn_rows = lax.psum(partial_out, "tp")
    hidden_state = resid.astype(jnp.float32) + attn_rows
    mean_sq = jnp.mean(hidden_state * hidden_state, axis=-1, keepdims=True)
    normed = (hidden_state * lax.rsqrt(mean_sq + norm_eps) * norm_gain).astype(jnp.bfloat16)
    units_local = w_gate.shape[1]
    paired = jnp.concatenate([w_gate, w_up], axis=1)
    columns = lax.all_to_all(normed, "req", split_axis=1, concat_axis=0, tiled=True)
    whole_sums = lax.psum(jnp.dot(columns, paired, preferred_element_type=jnp.float32), "req")
    hidden_units = (jax.nn.silu(whole_sums[:, :units_local]) * whole_sums[:, units_local:]).astype(
        jnp.bfloat16
    )
    down_part = jnp.dot(hidden_units, w_down, preferred_element_type=jnp.float32)
    back_part = lax.all_to_all(down_part, "req", split_axis=0, concat_axis=1, tiled=True)
    mlp_rows = lax.psum(back_part, "tp")
    decode_out = (hidden_state + mlp_rows).astype(jnp.bfloat16)
    return (prefill_out, decode_out)


f32 = jnp.float32
bf16 = jnp.bfloat16
lanes = 128
pay_rows = 28
back_rows = 12


def dot(a, b):
    return jnp.dot(a, b, preferred_element_type=f32)


def dot_nt(a, b):
    return lax.dot_general(a, b, (((1,), (1,)), ((), ())), preferred_element_type=f32)


def iota(shape, dim):
    return lax.broadcasted_iota(jnp.int32, shape, dim)


def rope_factors(angles):
    turns = jnp.floor(angles * (2.0 / np.pi) + 0.5)
    rest = angles - turns * 1.5703125
    rest = rest - turns * 4.837512969970703125e-4
    rest = rest - turns * 7.549789948768648e-8
    sq = rest * rest
    sine = ((-1.9515295891e-4 * sq + 8.3321608736e-3) * sq - 1.6666654611e-1) * sq * rest + rest
    cosine = (
        ((2.443315711809948e-5 * sq - 1.388731625493765e-3) * sq + 4.166664568298827e-2) * sq * sq
        - 0.5 * sq
        + 1.0
    )
    low = iota(angles.shape, 1) < lanes // 2
    quarter = turns.astype(jnp.int32) + jnp.where(low, 1, 0)
    both = jnp.where((quarter & 1) == 1, cosine, sine)
    both = jnp.where((quarter & 2) == 2, -both, both)
    swapped = pltpu.roll(both, lanes // 2, 1)
    return jnp.where(low, both, swapped), jnp.where(low, -swapped, both)


def norm_rope(values, gain, factors):
    mean_sq = jnp.mean(values * values, axis=-1, keepdims=True)
    normed = values * lax.rsqrt(mean_sq + norm_eps) * gain
    return (normed * factors[0] + pltpu.roll(normed, lanes // 2, 1) * factors[1]).astype(bf16)


def begin_of(indices, len_ref):
    begin = jnp.zeros_like(indices)
    end = 0
    for j in range(len_ref.shape[1] - 1):
        end = end + len_ref[0, j]
        begin = jnp.where(indices >= end, end, begin)
    return begin


def partial_kernel(
    len_hbm, k_hbm, v_hbm, qn_hbm, kn_hbm, vn_hbm, gn_hbm, resid_hbm, qg_hbm, kg_hbm, freq_hbm,
    w_hbm, gate_hbm, up_hbm,
    kv_hbm, pay_hbm, own_hbm, pair_hbm,
    kv_ref, pay_ref, own_ref, pair_ref, row_q, row_k, row_v, row_g, pay, len_ref, k_ref, v_ref, qn_ref, kn_ref, vn_ref, gn_ref,
    resid_ref, qg_ref, kg_ref, freq_ref, sems, out_sems,
):
    tp = lax.axis_index("tp")
    req = lax.axis_index("req")
    z, other = lax.div(req, 2), 1 - lax.rem(req, 2)
    width = own_ref.shape[1]
    units = pair_ref.shape[1] // 2
    cols = pl.ds(pl.multiple_of(z * width, lanes), width)
    theirs = pl.ds(pl.multiple_of(other * units, lanes), units)
    moves = (
        (len_hbm, len_ref), (freq_hbm, freq_ref), (k_hbm, k_ref), (kg_hbm, kg_ref),
        (qn_hbm, qn_ref), (kn_hbm, kn_ref), (vn_hbm, vn_ref), (gn_hbm, gn_ref), (qg_hbm, qg_ref),
        (v_hbm, v_ref), (resid_hbm, resid_ref),
        (gate_hbm.at[:, theirs], pair_ref.at[:, pl.ds(0, units)]),
        (up_hbm.at[:, theirs], pair_ref.at[:, pl.ds(units, units)]),
        (w_hbm.at[:, cols], own_ref),
    )
    copies = [pltpu.make_async_copy(a, b, sems.at[i]) for i, (a, b) in enumerate(moves)]
    for copy in copies:
        copy.start()
    ends = (
        (pair_ref, pair_hbm), (own_ref, own_hbm), (kv_ref, kv_hbm), (pay_ref, pay_hbm),
    )
    leave = [pltpu.make_async_copy(a, b, out_sems.at[i]) for i, (a, b) in enumerate(ends)]
    tok = k_ref.shape[0]
    rpg = qn_ref.shape[0]
    heads = qn_ref.shape[1] // lanes
    kvs = k_ref.shape[1] // lanes
    per = heads // kvs
    rows = heads * rpg
    for copy in copies[:2]:
        copy.wait()
    freq = freq_ref[...]
    tok_index = tp * tok + iota((tok, lanes), 0)
    factors = rope_factors((tok_index - begin_of(tok_index, len_ref)).astype(f32) * freq)
    for copy in copies[2:11]:
        copy.wait()
    qg, kg = qg_ref[...], kg_ref[...]
    keys = []
    for k in range(kvs):
        at = slice(k * lanes, (k + 1) * lanes)
        keys.append(norm_rope(k_ref[:, at].astype(f32), kg, factors))
        kv_ref[:, at] = keys[-1]
    kv_ref[:, kvs * lanes :] = v_ref[...]
    for copy in copies[11:]:
        copy.wait()
    for copy in leave[:3]:
        copy.start()
    qn, kn = qn_ref[...].astype(f32), kn_ref[...].astype(f32)
    vn, gn = vn_ref[...].astype(f32), gn_ref[...].astype(f32)
    for h in range(heads):
        at = slice(h * rpg, (h + 1) * rpg)
        kv = slice((h // per) * lanes, (h // per + 1) * lanes)
        row_q[at, :] = qn[:, h * lanes : (h + 1) * lanes]
        row_k[at, :] = kn[:, kv]
        row_v[at, :] = vn[:, kv]
        row_g[at, :] = jnp.broadcast_to(gn[:, h : h + 1], (rpg, lanes))
    row = iota((rows, lanes), 0)
    col = iota((rows, lanes), 1)
    head = row * 0
    for h in range(1, heads):
        head = jnp.where(row >= h * rpg, h, head)
    request = row - head * rpg
    length, first, last = row * 0, row * 0, row * 0
    end = 0
    for j in range(rpg):
        mine = request == j
        length = jnp.where(mine, len_ref[0, j], length)
        first = jnp.where(mine, end, first)
        end = end + len_ref[0, j]
        last = jnp.where(mine, end, last)
    new_factors = rope_factors(length.astype(f32) * freq)
    scale = lanes ** (-0.5)
    new_q = norm_rope(row_q[0:rows, :], qg, new_factors)
    new_k = norm_rope(row_k[0:rows, :], kg, new_factors)
    scores = jnp.zeros((rows, tok), f32)
    for k in range(kvs):
        mine = (head >= k * per) & (head < (k + 1) * per)
        scores = jnp.where(mine, dot_nt(new_q, keys[k]), scores)
    index = tp * tok + col
    weights = jnp.where((index >= first) & (index < last), jnp.exp(scores * scale), 0.0)
    totals = jnp.sum(weights, axis=-1, keepdims=True)
    rounded = weights.astype(bf16)
    mixed = jnp.zeros((rows, lanes), f32)
    for k in range(kvs):
        mine = (head >= k * per) & (head < (k + 1) * per)
        mixed = mixed + dot(
            jnp.where(mine, rounded, jnp.zeros_like(rounded)), v_ref[:, k * lanes : (k + 1) * lanes]
        )
    self_score = jnp.sum(new_q.astype(f32) * new_k.astype(f32), axis=-1, keepdims=True)
    self_weight = jnp.where(tp == 0, jnp.exp(self_score * scale), 0.0)
    totals = totals + self_weight
    mixed = (mixed + self_weight * row_v[0:rows, :]) * jax.nn.sigmoid(row_g[0:rows, :])
    total_row = jnp.sum(jnp.where(row == col, totals, 0.0), axis=0, keepdims=True)
    high = total_row.astype(bf16).astype(f32)
    rest = pltpu.roll(jnp.broadcast_to(total_row - high, (8, lanes)), lanes // 2, 1)
    pay[0:rows, :] = mixed
    pay[rows + rpg : rows + rpg + 1, :] = jnp.where(
        iota((1, lanes), 1) < lanes // 2, high, rest[0:1, :]
    )
    peers = pay_ref.shape[0]
    tps = lax.axis_size("tp")
    slices = resid_ref.shape[1] // (tps * lanes)
    for z in range(slices):
        at = pl.ds(pl.multiple_of((z * tps + tp) * lanes, lanes), lanes)
        pay[rows : rows + rpg, :] = resid_ref[:, at].astype(f32)
        for g in range(pay_ref.shape[1]):
            out = pay[4 * g : 4 * g + 4, :].astype(bf16)
            for peer in range(z * peers // slices, (z + 1) * peers // slices):
                pay_ref[peer, g] = out
    leave[3].start()
    for copy in leave:
        copy.wait()


def fetch_kernel(gate_hbm, up_hbm, ng_hbm, mine_ref, ng_ref, sems):
    units = mine_ref.shape[1] // 2
    width = ng_ref.shape[1]
    req = lax.axis_index("req")
    at = pl.ds(pl.multiple_of(lax.rem(req, 2) * units, lanes), units)
    cols = pl.ds(pl.multiple_of(lax.div(req, 2) * width, lanes), width)
    copies = (
        pltpu.make_async_copy(gate_hbm.at[:, at], mine_ref.at[:, pl.ds(0, units)], sems.at[0]),
        pltpu.make_async_copy(up_hbm.at[:, at], mine_ref.at[:, pl.ds(units, units)], sems.at[1]),
        pltpu.make_async_copy(ng_hbm.at[:, cols], ng_ref, sems.at[2]),
    )
    for copy in copies:
        copy.start()
    for copy in copies:
        copy.wait()


def columns_kernel(w_hbm, down_hbm, w_ref, down_ref, sems):
    width = w_ref.shape[1]
    units = down_ref.shape[0]
    req = lax.axis_index("req")
    cols = pl.ds(pl.multiple_of(lax.div(req, 2) * width, lanes), width)
    theirs = pl.ds(pl.multiple_of((1 - lax.rem(req, 2)) * units, lanes), units)
    copies = (
        pltpu.make_async_copy(w_hbm.at[:, cols], w_ref, sems.at[0]),
        pltpu.make_async_copy(down_hbm.at[theirs, :], down_ref, sems.at[1]),
    )
    for copy in copies:
        copy.start()
    for copy in copies:
        copy.wait()


def ready_kernel(*refs):
    refs[-1][...] = jnp.zeros_like(refs[-1])


def hidden_kernel(
    pay_ref, w0_ref, w1_ref, w2_ref, w3_ref, mine_ref, pair_ref, ng_ref, _,
    hid_ref, msg_ref, att, hid, xs, acc, out,
):
    tp = lax.axis_index("tp")
    req = lax.axis_index("req")
    tps = lax.axis_size("tp")
    z, y = lax.div(req, 2), lax.rem(req, 2)
    heads, toks = att.shape[0], hid_ref.shape[0]
    groups = pay_ref.shape[0] // tps
    rpg = toks // groups
    rows = heads * rpg
    diag = iota((rows, lanes), 0) == iota((rows, lanes), 1)
    quads = pay_ref.shape[1]
    for r in range(groups):
        for g in range(quads):
            total = jnp.zeros((4, lanes), f32)
            for t in range(tps):
                piece = pay_ref[r * tps + t, g].astype(f32)
                total = total + piece
                if g == quads - 1:
                    hid[r * rpg : (r + 1) * rpg, t * lanes : (t + 1) * lanes] = piece[:rpg, :]
            acc[r, 4 * g : 4 * g + 4, :] = total
    for r in range(groups):
        total_row = jnp.broadcast_to(acc[r, pay_rows - 1 : pay_rows, :], (rows, lanes))
        total_row = total_row + pltpu.roll(total_row, lanes // 2, 1)
        totals = jnp.sum(jnp.where(diag, total_row, 0.0), axis=-1, keepdims=True)
        acc[r, 0:rows, :] = acc[r, 0:rows, :] / totals
    for r in range(groups):
        for h in range(heads):
            att[h, r * rpg : (r + 1) * rpg, :] = acc[r, h * rpg : (h + 1) * rpg, :]
    state = hid[0:toks, :]
    per = heads // tps
    for d, w_ref in enumerate((w0_ref, w1_ref, w2_ref, w3_ref)):
        source = tp ^ d
        for j in range(per):
            state = state + dot(
                att[source * per + j, 0:toks, :].astype(bf16), w_ref[j * lanes : (j + 1) * lanes, :]
            )
    hid_ref[...] = state
    width = state.shape[1]
    half = width // 2
    sums = jnp.sum(state * state, axis=-1, keepdims=True)
    scaled = state * ng_ref[...]
    xs[0] = scaled[:, :half]
    xs[1] = scaled[:, half:]
    own, other = xs[y].astype(bf16), xs[1 - y].astype(bf16)
    units = pair_ref.shape[1] // 2
    gate = dot(own, mine_ref[:, :units]) + dot(other, pair_ref[:, :units])
    up = dot(own, mine_ref[:, units:]) + dot(other, pair_ref[:, units:])
    square = iota((toks, lanes), 0) == iota((toks, lanes), 1)
    sums_row = jnp.sum(jnp.where(square, sums, 0.0), axis=0, keepdims=True)
    high = sums_row.astype(bf16).astype(f32)
    blocks = units // lanes
    for i in range(blocks):
        at = slice(i * lanes, (i + 1) * lanes)
        out[i * toks : (i + 1) * toks, :] = gate[:, at]
        out[(blocks + i) * toks : (blocks + i + 1) * toks, :] = up[:, at]
    base = 2 * blocks * toks
    first = iota((8, lanes), 0)
    out[base : base + 8, :] = jnp.where(
        first == 0, high, jnp.where(first == 1, sums_row - high, 0.0)
    )
    msg_ref[...] = out[0 : msg_ref.shape[0], :].astype(bf16)


def down_kernel(m0_ref, m1_ref, m2_ref, m3_ref, hid_ref, down_ref, pair_ref, back_ref, pay, whole):
    tp = lax.axis_index("tp")
    tps = lax.axis_size("tp")
    y = lax.rem(lax.axis_index("req"), 2)
    units, half = pair_ref.shape
    toks, width = hid_ref.shape
    total = m0_ref[...].astype(f32)
    for m_ref in (m1_ref, m2_ref, m3_ref):
        total = total + m_ref[...].astype(f32)
    whole[0 : total.shape[0], :] = total
    blocks = units // lanes
    base = 2 * blocks * toks
    square = iota((toks, lanes), 0) == iota((toks, lanes), 1)
    sums_row = whole[base : base + 1, :] + whole[base + 1 : base + 2, :]
    sums = jnp.sum(
        jnp.where(square, jnp.broadcast_to(sums_row, (toks, lanes)), 0.0), axis=-1, keepdims=True
    )
    factor = lax.rsqrt(sums / (width * 4) + norm_eps)
    pieces = []
    for i in range(blocks):
        gate = whole[i * toks : (i + 1) * toks, :] * factor
        up = whole[(blocks + i) * toks : (blocks + i + 1) * toks, :] * factor
        pieces.append((gate / (1.0 + jnp.exp(-gate)) * up).astype(bf16))
    hidden = jnp.concatenate(pieces, axis=1)
    own_rows = pl.ds(pl.multiple_of(y * units, lanes), units)
    mine, theirs = dot(hidden, down_ref[own_rows, :]), dot(hidden, pair_ref[...])
    part = (jnp.where(y == 0, mine, theirs), jnp.where(y == 0, theirs, mine))
    chunks = width // lanes
    groups = pay.shape[0]
    rpg = toks // groups
    for c in range(chunks):
        at = (c * lanes) % half
        block = part[c * lanes // half][:, at : at + lanes]
        adds = (y == 0) & (tp == c)
        block = block + jnp.where(adds, hid_ref[:, c * lanes : (c + 1) * lanes], 0.0)
        for r in range(groups):
            pay[r, c * rpg : (c + 1) * rpg, :] = block[r * rpg : (r + 1) * rpg, :]
    for r in range(groups):
        for g in range(back_ref.shape[1]):
            out = pay[r, 4 * g : 4 * g + 4, :].astype(bf16)
            for t in range(tps):
                back_ref[r * tps + t, g] = out


def final_kernel(back_ref, out_ref, acc, rows_out):
    tps = lax.axis_size("tp")
    peers = back_ref.shape[0]
    rpg, width = out_ref.shape
    slices = acc.shape[0]
    group = peers // slices
    chunks = width // (slices * lanes)
    for z in range(slices):
        for g in range(back_ref.shape[1]):
            total = back_ref[z * group, g].astype(f32)
            for p in range(1, group):
                total = total + back_ref[z * group + p, g].astype(f32)
            acc[z, 4 * g : 4 * g + 4, :] = total
    for z in range(slices):
        for c in range(chunks):
            at = slice((z * chunks + c) * lanes, (z * chunks + c + 1) * lanes)
            rows_out[0:rpg, at] = acc[z, c * rpg : (c + 1) * rpg, :]
    out_ref[...] = rows_out[0:rpg, :].astype(bf16)


def query_kernel(len_ref, q_ref, g_ref, qg_ref, freq_ref, query_ref, side_ref):
    tp = lax.axis_index("tp")
    tok = q_ref.shape[0]
    heads = q_ref.shape[1] // lanes
    tok_index = tp * tok + iota((tok, lanes), 0)
    begin = begin_of(tok_index, len_ref)
    factors = rope_factors((tok_index - begin).astype(f32) * freq_ref[...])
    gates = jax.nn.sigmoid(g_ref[...].astype(f32))
    lane = iota((tok, lanes), 1)
    side = jnp.where(lane == heads, begin.astype(f32), 0.0)
    for h in range(heads):
        at = slice(h * lanes, (h + 1) * lanes)
        query_ref[:, at] = norm_rope(q_ref[:, at].astype(f32), qg_ref[...], factors)
        side = jnp.where(lane == h, gates[:, h : h + 1], side)
    side_ref[...] = side


def prefill_kernel(query_ref, side_ref, kv0_ref, kv1_ref, kv2_ref, kv3_ref, out_ref, mid_ref):
    tp = lax.axis_index("tp")
    tok = query_ref.shape[0]
    heads = query_ref.shape[1] // lanes
    kvs = kv0_ref.shape[1] // (2 * lanes)
    per = heads // kvs
    third = tp == 2
    mid_ref[...] = jnp.where(third, kv3_ref[...], kv1_ref[...])
    blocks = ((tp, kv0_ref), (jnp.where(third, tp ^ 3, tp ^ 1), mid_ref), (tp ^ 2, kv2_ref))
    tok_index = tp * tok + iota((tok, tok), 0)
    begin = side_ref[:, heads : heads + 1].astype(jnp.int32)
    col = iota((tok, tok), 1)
    allowed = []
    for block, _ in blocks:
        key_index = block * tok + col
        mask = ((key_index >= begin) & (key_index <= tok_index)).astype(f32)
        allowed.append(jnp.concatenate([mask] * per, axis=0) > 0.5)
    ones = jnp.ones((tok, lanes), bf16)
    scale = lanes ** (-0.5)
    for k in range(kvs):
        query = jnp.concatenate(
            [query_ref[:, h * lanes : (h + 1) * lanes] for h in range(k * per, (k + 1) * per)],
            axis=0,
        )
        sums = jnp.zeros((per * tok, 2 * lanes), f32)
        for b, (_, kv_ref) in enumerate(blocks):
            scores = dot_nt(query, kv_ref[:, k * lanes : (k + 1) * lanes])
            weights = jnp.where(allowed[b], jnp.exp(scores * scale), 0.0).astype(bf16)
            values = kv_ref[:, (kvs + k) * lanes : (kvs + k + 1) * lanes]
            sums = sums + dot(weights, jnp.concatenate([values, ones], axis=1))
        for i in range(per):
            h = k * per + i
            rows = slice(i * tok, (i + 1) * tok)
            out_ref[:, h * lanes : (h + 1) * lanes] = (
                sums[rows, :lanes] / sums[rows, lanes:] * side_ref[:, h : h + 1]
            ).astype(bf16)


def room(rows):
    return (rows + 15) // 8 * 8


def call(body, out_shape, args, scratch=(), hbm=False, out_any=False, smem=0, flops=0, limit=12):
    specs = [pl.BlockSpec(memory_space=pltpu.SMEM)] * smem
    space = pltpu.HBM if hbm else pltpu.VMEM
    specs += [pl.BlockSpec(memory_space=space)] * (len(args) - smem)
    size = sum(a.size * a.dtype.itemsize for a in args)
    return pl.pallas_call(
        body,
        out_shape=out_shape,
        in_specs=specs,
        out_specs=jax.tree.map(
            lambda _: pl.BlockSpec(memory_space=pl.ANY if out_any else pltpu.VMEM), out_shape
        ),
        scratch_shapes=[pltpu.VMEM(s, f32) if isinstance(s, tuple) else s for s in scratch],
        compiler_params=pltpu.CompilerParams(vmem_limit_bytes=limit * 2**20),
        cost_estimate=pl.CostEstimate(flops=flops, bytes_accessed=size, transcendentals=0),
    )(*args)


def hold(arrays, flops):
    return pl.pallas_call(
        ready_kernel,
        out_shape=jax.ShapeDtypeStruct((8, lanes), f32),
        in_specs=[pl.BlockSpec(memory_space=pl.ANY)] * len(arrays),
        out_specs=pl.BlockSpec(memory_space=pltpu.VMEM),
        compiler_params=pltpu.CompilerParams(vmem_limit_bytes=2**20),
        cost_estimate=pl.CostEstimate(flops=flops, bytes_accessed=0, transcendentals=0),
    )(*arrays)


def local(
    q_pre,
    gate_pre,
    k_pre,
    v_pre,
    q_gain,
    k_gain,
    lengths,
    q_new,
    gate_new,
    k_new,
    v_new,
    resid,
    w_out,
    norm_gain,
    w_gate,
    w_up,
    w_down,
):
    tps, reqs = lax.axis_size("tp"), lax.axis_size("req")
    tok = q_pre.shape[0]
    rpg, width = resid.shape
    slices = reqs // 2
    head_size = q_gain.shape[0]
    heads = gate_pre.shape[1]
    part = width // slices if slices else 0
    if not (slices == 4 and tps == 4 and head_size == lanes == tok and part == tps * lanes):
        return general(
            q_pre, gate_pre, k_pre, v_pre, q_gain, k_gain, lengths, q_new, gate_new, k_new, v_new,
            resid, w_out, norm_gain, w_gate, w_up, w_down,
        )
    peers = tps * reqs
    toks = rpg * reqs
    units = w_gate.shape[1] // 2
    req = lax.axis_index("req")
    z, y = req // 2, req % 2
    freqs = rope_base ** (-(np.arange(head_size // 2) * 2.0 / head_size))
    freqs = jnp.asarray(np.concatenate([freqs, freqs])[None, :], f32)
    qg, kg = q_gain[None, :], k_gain[None, :]

    def cross(array, by):
        return lax.ppermute(array, "tp", [(i, i ^ by) for i in range(tps)])

    def swap(array):
        return lax.ppermute(array, "req", [(i, i ^ 1) for i in range(reqs)])

    def along(array, by):
        return lax.ppermute(array, "req", [(i, i ^ (2 * by)) for i in range(reqs)])

    inputs = (
        lengths, k_pre, v_pre, q_new, k_new, v_new, gate_new, resid, qg, kg, freqs,
        w_out, w_gate, w_up,
    )
    outputs = (
        jax.ShapeDtypeStruct((tok, 2 * k_pre.shape[1]), bf16),
        jax.ShapeDtypeStruct((peers, pay_rows // 4, 4, lanes), bf16),
        jax.ShapeDtypeStruct((w_out.shape[0], part), bf16),
        jax.ShapeDtypeStruct((w_gate.shape[0], 2 * units), bf16),
    )
    kv, pay, w_own, pair = call(
        partial_kernel,
        outputs,
        inputs,
        scratch=[pltpu.VMEM(o.shape, o.dtype) for o in outputs]
        + [(room(heads * rpg), lanes)] * 4
        + [(room(pay_rows), lanes), pltpu.SMEM(lengths.shape, jnp.int32)]
        + [pltpu.VMEM(a.shape, a.dtype) for a in inputs[1:11]]
        + [pltpu.SemaphoreType.DMA((len(inputs),)), pltpu.SemaphoreType.DMA((len(outputs),))],
        hbm=True,
        out_any=True,
        flops=10**7,
        limit=56,
    )
    w_far = cross(w_own, 2)
    pair = swap(pair)
    half = jax.ShapeDtypeStruct((w_gate.shape[0], 2 * units), bf16)
    mine, ng = call(
        fetch_kernel,
        (half, jax.ShapeDtypeStruct((1, part), f32)),
        (w_gate, w_up, norm_gain[None, :]),
        hbm=True,
        scratch=[pltpu.SemaphoreType.DMA((3,))],
    )
    w_here, down_pair = call(
        columns_kernel,
        (
            jax.ShapeDtypeStruct(w_own.shape, bf16),
            jax.ShapeDtypeStruct((units, w_down.shape[1]), bf16),
        ),
        (w_out, w_down),
        hbm=True,
        scratch=[pltpu.SemaphoreType.DMA((2,))],
    )
    query, side = call(
        query_kernel,
        (jax.ShapeDtypeStruct(q_pre.shape, bf16), jax.ShapeDtypeStruct((tok, lanes), f32)),
        (lengths, q_pre, gate_pre, qg, freqs),
        smem=1,
        flops=10**6,
    )
    late_far, _, _, _ = lax.optimization_barrier((w_far, mine, w_here, side))
    w_near, w_both = cross(w_own, 1), cross(late_far, 1)
    kv_near = cross(kv, 1)
    late_kv, _ = lax.optimization_barrier((kv, w_far))
    kv_far = cross(late_kv, 2)
    late_down, _ = lax.optimization_barrier((down_pair, pair))
    down_pair = swap(late_down)
    got = lax.all_to_all(pay, ("req", "tp"), 0, 0, tiled=True)
    landed = hold((pair,), 2 * 10**9)
    token = hold((landed, w_near, w_both), 10**9)
    msg_shape = (2 * units // lanes * toks + 8, lanes)
    hid, msg = call(
        hidden_kernel,
        (
            jax.ShapeDtypeStruct((toks, part), f32),
            jax.ShapeDtypeStruct(msg_shape, bf16),
        ),
        (got, w_here, w_near, w_far, w_both, mine, pair, ng, token),
        scratch=[
            (heads, room(toks), lanes),
            (room(toks), part),
            (2, toks, part // 2),
            (reqs, room(pay_rows), lanes),
            (room(msg_shape[0]), lanes),
        ],
        flops=10**7,
    )
    msgs = [msg] + [along(msg, d) for d in (3, 2, 1)]
    kv_both = cross(kv_far, 1)
    prefill_out = call(
        prefill_kernel,
        jax.ShapeDtypeStruct(q_pre.shape, bf16),
        (query, side, kv, kv_near, kv_far, kv_both),
        scratch=[pltpu.VMEM(kv.shape, bf16)],
        flops=10**9,
    )
    back = call(
        down_kernel,
        jax.ShapeDtypeStruct((peers, back_rows // 4, 4, lanes), bf16),
        (*msgs, hid, w_down, down_pair),
        scratch=[(reqs, room(back_rows), lanes), (room(msg_shape[0]), lanes)],
        flops=3 * 10**9,
    )
    returned = lax.all_to_all(back, ("req", "tp"), 0, 0, tiled=True)
    returned, prefill_out = lax.optimization_barrier((returned, prefill_out))
    decode_out = call(
        final_kernel,
        jax.ShapeDtypeStruct((rpg, width), bf16),
        (returned,),
        scratch=[(slices, room(back_rows), lanes), (room(rpg), width)],
        flops=10**6,
    )
    return (prefill_out, decode_out)


def solution(mesh):
    return jax.shard_map(
        local,
        mesh=mesh,
        in_specs=(
            P(("req", "tp"), None),
            P(("req", "tp"), None),
            P(("req", "tp"), None),
            P(("req", "tp"), None),
            P(),
            P(),
            P("req", None),
            P("req", None),
            P("req", None),
            P("req", None),
            P("req", None),
            P("req", None),
            P("tp", None),
            P(),
            P("req", "tp"),
            P("req", "tp"),
            P("tp", "req"),
        ),
        out_specs=(P(("req", "tp"), None), P("req", None)),
        check_vma=False,
    )
```

```python
import jax
import jax.numpy as jnp
import numpy as np
from jax import lax
from jax.experimental import pallas as pl
from jax.experimental.pallas import tpu as pltpu
from jax.sharding import PartitionSpec as P

rope_base = 1000000.0
norm_eps = 1e-06


def group_layout(lengths_row, total):
    req_ends = jnp.cumsum(lengths_row)
    req_starts = req_ends - lengths_row
    indices = jnp.arange(total, dtype=jnp.int32)
    segment = jnp.sum((indices[:, None] >= req_ends[None, :]).astype(jnp.int32), axis=1)
    onehot = segment[:, None] == jnp.arange(lengths_row.shape[0], dtype=jnp.int32)[None, :]
    offsets = jnp.sum(jnp.where(onehot, req_starts[None, :], 0), axis=1)
    return (segment, indices - offsets)


def head_norm(values, gain):
    mean_sq = jnp.mean(values * values, axis=-1, keepdims=True)
    return values * lax.rsqrt(mean_sq + norm_eps) * gain


def rotate(values, position):
    half_size = values.shape[-1] // 2
    freqs = rope_base ** (-(jnp.arange(half_size, dtype=jnp.float32) * 2.0 / (2 * half_size)))
    angles = position.astype(jnp.float32)[:, None] * freqs[None, :]
    shaped = (values.shape[0],) + (1,) * (values.ndim - 2) + (half_size,)
    cosine = jnp.cos(angles).reshape(shaped)
    sine = jnp.sin(angles).reshape(shaped)
    first_half = values[..., :half_size]
    second_half = values[..., half_size:]
    return jnp.concatenate(
        [first_half * cosine - second_half * sine, second_half * cosine + first_half * sine],
        axis=-1,
    )


def general(
    q_pre,
    gate_pre,
    k_pre,
    v_pre,
    q_gain,
    k_gain,
    lengths,
    q_new,
    gate_new,
    k_new,
    v_new,
    resid,
    w_out,
    norm_gain,
    w_gate,
    w_up,
    w_down,
):
    tok_rows = q_pre.shape[0]
    tp_count = lax.axis_size("tp")
    tp_index = lax.axis_index("tp")
    head_size = q_gain.shape[0]
    query_heads = gate_pre.shape[1]
    kv_heads = k_pre.shape[1] // head_size
    groups_per = query_heads // kv_heads
    kv_local = kv_heads // tp_count
    req_count = lengths.shape[1]
    score_scale = head_size ** (-0.5)
    segment, position = group_layout(lengths[0], tok_rows * tp_count)
    row_offset = tp_index * tok_rows
    seg_local = lax.dynamic_slice_in_dim(segment, row_offset, tok_rows)
    pos_local = lax.dynamic_slice_in_dim(position, row_offset, tok_rows)
    query_index = row_offset + jnp.arange(tok_rows, dtype=jnp.int32)
    queries = rotate(
        head_norm(q_pre.reshape(tok_rows, query_heads, head_size).astype(jnp.float32), q_gain),
        pos_local,
    )
    queries = queries.astype(jnp.bfloat16).reshape(tok_rows, kv_heads, groups_per, head_size)
    keys = rotate(
        head_norm(k_pre.reshape(tok_rows, kv_heads, head_size).astype(jnp.float32), k_gain),
        pos_local,
    ).astype(jnp.bfloat16)
    values = v_pre.reshape(tok_rows, kv_heads, head_size)

    def key_block(running, key_piece, value_piece, first_row):
        key_count = key_piece.shape[0]
        key_index = first_row + jnp.arange(key_count, dtype=jnp.int32)
        allowed = (seg_local[:, None] == segment[None, :]) & (
            query_index[:, None] >= key_index[None, :]
        )
        scores = (
            jnp.einsum(
                "qkgd,pkd->qkgp",
                queries,
                key_piece.reshape(key_count, kv_heads, head_size),
                preferred_element_type=jnp.float32,
            )
            * score_scale
        )
        weights = jnp.where(allowed[:, None, None, :], jnp.exp(scores), 0.0)
        totals = running[0] + jnp.sum(weights, axis=-1)
        mixed = running[1] + jnp.einsum(
            "qkgp,pkd->qkgd",
            weights.astype(jnp.bfloat16),
            value_piece.reshape(key_count, kv_heads, head_size),
            preferred_element_type=jnp.float32,
        )
        return (totals, mixed)

    start_state = (
        jnp.zeros((tok_rows, kv_heads, groups_per), jnp.float32),
        jnp.zeros((tok_rows, kv_heads, groups_per, head_size), jnp.float32),
    )
    pieces = (
        lax.all_gather(keys.reshape(tok_rows, kv_heads * head_size), "tp", axis=0, tiled=True),
        lax.all_gather(v_pre, "tp", axis=0, tiled=True),
    )
    key_count = pieces[0].shape[0]
    block_rows = 512

    def one_block(number, carried):
        begin_at = number * block_rows
        return key_block(carried, pieces[0], pieces[1], begin_at)

    totals, mixed = lax.fori_loop(0, key_count // block_rows, one_block, start_state)
    gates = jax.nn.sigmoid(gate_pre.astype(jnp.float32)).reshape(tok_rows, kv_heads, groups_per)
    prefill_out = (
        (mixed / totals[..., None] * gates[..., None])
        .astype(jnp.bfloat16)
        .reshape(tok_rows, query_heads * head_size)
    )
    new_queries = rotate(
        head_norm(q_new.reshape(req_count, query_heads, head_size).astype(jnp.float32), q_gain),
        lengths[0],
    )
    new_queries = new_queries.astype(jnp.bfloat16).reshape(
        req_count, kv_heads, groups_per, head_size
    )
    new_keys = rotate(
        head_norm(k_new.reshape(req_count, kv_heads, head_size).astype(jnp.float32), k_gain),
        lengths[0],
    ).astype(jnp.bfloat16)
    new_values = v_new.reshape(req_count, kv_heads, head_size)
    new_gates = jax.nn.sigmoid(gate_new.astype(jnp.float32)).reshape(
        req_count, kv_heads, groups_per
    )
    head_first = tp_index * kv_local
    request_ids = jnp.arange(req_count, dtype=jnp.int32)
    own_queries = lax.dynamic_slice_in_dim(new_queries, head_first, kv_local, 1)
    cache_keys, cache_values = (
        lax.all_to_all(keys, "tp", split_axis=1, concat_axis=0, tiled=True),
        lax.all_to_all(values, "tp", split_axis=1, concat_axis=0, tiled=True),
    )
    scores = (
        jnp.einsum("rkgd,pkd->rkgp", own_queries, cache_keys, preferred_element_type=jnp.float32)
        * score_scale
    )
    owned = segment[None, :] == request_ids[:, None]
    weights = jnp.where(owned[:, None, None, :], jnp.exp(scores), 0.0)
    weighted = jnp.einsum(
        "rkgp,pkd->rkgd",
        weights.astype(jnp.bfloat16),
        cache_values,
        preferred_element_type=jnp.float32,
    )
    dec_totals = jnp.sum(weights, axis=-1)
    dec_mixed = weighted
    own_keys = lax.dynamic_slice_in_dim(new_keys, head_first, kv_local, 1)
    own_values = lax.dynamic_slice_in_dim(new_values, head_first, kv_local, 1)
    own_gates = lax.dynamic_slice_in_dim(new_gates, head_first, kv_local, 1)
    self_weight = jnp.exp(
        jnp.einsum("rkgd,rkd->rkg", own_queries, own_keys, preferred_element_type=jnp.float32)
        * score_scale
    )
    dec_totals = dec_totals + self_weight
    dec_mixed = dec_mixed + self_weight[..., None] * own_values.astype(jnp.float32)[:, :, None, :]
    attended = (
        (dec_mixed / dec_totals[..., None] * own_gates[..., None])
        .astype(jnp.bfloat16)
        .reshape(req_count, kv_local * groups_per * head_size)
    )
    partial_out = jnp.dot(attended, w_out, preferred_element_type=jnp.float32)
    attn_rows = lax.psum(partial_out, "tp")
    hidden_state = resid.astype(jnp.float32) + attn_rows
    mean_sq = jnp.mean(hidden_state * hidden_state, axis=-1, keepdims=True)
    normed = (hidden_state * lax.rsqrt(mean_sq + norm_eps) * norm_gain).astype(jnp.bfloat16)
    units_local = w_gate.shape[1]
    paired = jnp.concatenate([w_gate, w_up], axis=1)
    columns = lax.all_to_all(normed, "req", split_axis=1, concat_axis=0, tiled=True)
    whole_sums = lax.psum(jnp.dot(columns, paired, preferred_element_type=jnp.float32), "req")
    hidden_units = (jax.nn.silu(whole_sums[:, :units_local]) * whole_sums[:, units_local:]).astype(
        jnp.bfloat16
    )
    down_part = jnp.dot(hidden_units, w_down, preferred_element_type=jnp.float32)
    back_part = lax.all_to_all(down_part, "req", split_axis=0, concat_axis=1, tiled=True)
    mlp_rows = lax.psum(back_part, "tp")
    decode_out = (hidden_state + mlp_rows).astype(jnp.bfloat16)
    return (prefill_out, decode_out)


f32 = jnp.float32
bf16 = jnp.bfloat16
lanes = 128
pay_rows = 28
back_rows = 12


def dot(a, b):
    return jnp.dot(a, b, preferred_element_type=f32)


def dot_nt(a, b):
    return lax.dot_general(a, b, (((1,), (1,)), ((), ())), preferred_element_type=f32)


def iota(shape, dim):
    return lax.broadcasted_iota(jnp.int32, shape, dim)


def rope_factors(angles):
    turns = jnp.floor(angles * (2.0 / np.pi) + 0.5)
    rest = angles - turns * 1.5703125
    rest = rest - turns * 4.837512969970703125e-4
    rest = rest - turns * 7.549789948768648e-8
    sq = rest * rest
    sine = ((-1.9515295891e-4 * sq + 8.3321608736e-3) * sq - 1.6666654611e-1) * sq * rest + rest
    cosine = (
        ((2.443315711809948e-5 * sq - 1.388731625493765e-3) * sq + 4.166664568298827e-2) * sq * sq
        - 0.5 * sq
        + 1.0
    )
    low = iota(angles.shape, 1) < lanes // 2
    quarter = turns.astype(jnp.int32) + jnp.where(low, 1, 0)
    both = jnp.where((quarter & 1) == 1, cosine, sine)
    both = jnp.where((quarter & 2) == 2, -both, both)
    swapped = pltpu.roll(both, lanes // 2, 1)
    return jnp.where(low, both, swapped), jnp.where(low, -swapped, both)


def norm_rope(values, gain, factors):
    mean_sq = jnp.mean(values * values, axis=-1, keepdims=True)
    normed = values * lax.rsqrt(mean_sq + norm_eps) * gain
    return (normed * factors[0] + pltpu.roll(normed, lanes // 2, 1) * factors[1]).astype(bf16)


def begin_of(indices, len_ref):
    begin = jnp.zeros_like(indices)
    end = 0
    for j in range(len_ref.shape[1] - 1):
        end = end + len_ref[0, j]
        begin = jnp.where(indices >= end, end, begin)
    return begin


def partial_kernel(
    len_hbm, k_hbm, v_hbm, qn_hbm, kn_hbm, vn_hbm, gn_hbm, resid_hbm, qg_hbm, kg_hbm, freq_hbm,
    w_hbm, gate_hbm, up_hbm,
    kv_hbm, pay_hbm, own_hbm, pair_hbm,
    kv_ref, pay_ref, own_ref, pair_ref, row_q, row_k, row_v, row_g, pay, len_ref, k_ref, v_ref, qn_ref, kn_ref, vn_ref, gn_ref,
    resid_ref, qg_ref, kg_ref, freq_ref, sems, out_sems,
):
    tp = lax.axis_index("tp")
    req = lax.axis_index("req")
    z, other = lax.div(req, 2), 1 - lax.rem(req, 2)
    width = own_ref.shape[1]
    units = pair_ref.shape[1] // 2
    cols = pl.ds(pl.multiple_of(z * width, lanes), width)
    theirs = pl.ds(pl.multiple_of(other * units, lanes), units)
    moves = (
        (len_hbm, len_ref), (freq_hbm, freq_ref), (k_hbm, k_ref), (kg_hbm, kg_ref),
        (qn_hbm, qn_ref), (kn_hbm, kn_ref), (vn_hbm, vn_ref), (gn_hbm, gn_ref), (qg_hbm, qg_ref),
        (v_hbm, v_ref), (resid_hbm, resid_ref),
        (gate_hbm.at[:, theirs], pair_ref.at[:, pl.ds(0, units)]),
        (up_hbm.at[:, theirs], pair_ref.at[:, pl.ds(units, units)]),
        (w_hbm.at[:, cols], own_ref),
    )
    copies = [pltpu.make_async_copy(a, b, sems.at[i]) for i, (a, b) in enumerate(moves)]
    for copy in copies:
        copy.start()
    ends = (
        (pair_ref, pair_hbm), (own_ref, own_hbm), (kv_ref, kv_hbm), (pay_ref, pay_hbm),
    )
    leave = [pltpu.make_async_copy(a, b, out_sems.at[i]) for i, (a, b) in enumerate(ends)]
    tok = k_ref.shape[0]
    rpg = qn_ref.shape[0]
    heads = qn_ref.shape[1] // lanes
    kvs = k_ref.shape[1] // lanes
    per = heads // kvs
    rows = heads * rpg
    for copy in copies[:2]:
        copy.wait()
    freq = freq_ref[...]
    tok_index = tp * tok + iota((tok, lanes), 0)
    factors = rope_factors((tok_index - begin_of(tok_index, len_ref)).astype(f32) * freq)
    for copy in copies[2:4]:
        copy.wait()
    kg = kg_ref[...]
    keys = []
    for k in range(kvs):
        at = slice(k * lanes, (k + 1) * lanes)
        keys.append(norm_rope(k_ref[:, at].astype(f32), kg, factors))
        kv_ref[:, at] = keys[-1]
    for copy in copies[4:11]:
        copy.wait()
    qg = qg_ref[...]
    kv_ref[:, kvs * lanes :] = v_ref[...]
    for copy in copies[11:]:
        copy.wait()
    for copy in leave[:3]:
        copy.start()
    qn, kn = qn_ref[...].astype(f32), kn_ref[...].astype(f32)
    vn, gn = vn_ref[...].astype(f32), gn_ref[...].astype(f32)
    for h in range(heads):
        at = slice(h * rpg, (h + 1) * rpg)
        kv = slice((h // per) * lanes, (h // per + 1) * lanes)
        row_q[at, :] = qn[:, h * lanes : (h + 1) * lanes]
        row_k[at, :] = kn[:, kv]
        row_v[at, :] = vn[:, kv]
        row_g[at, :] = jnp.broadcast_to(gn[:, h : h + 1], (rpg, lanes))
    row = iota((rows, lanes), 0)
    col = iota((rows, lanes), 1)
    head = row * 0
    for h in range(1, heads):
        head = jnp.where(row >= h * rpg, h, head)
    request = row - head * rpg
    length, first, last = row * 0, row * 0, row * 0
    end = 0
    for j in range(rpg):
        mine = request == j
        length = jnp.where(mine, len_ref[0, j], length)
        first = jnp.where(mine, end, first)
        end = end + len_ref[0, j]
        last = jnp.where(mine, end, last)
    new_factors = rope_factors(length.astype(f32) * freq)
    scale = lanes ** (-0.5)
    new_q = norm_rope(row_q[0:rows, :], qg, new_factors)
    new_k = norm_rope(row_k[0:rows, :], kg, new_factors)
    scores = jnp.zeros((rows, tok), f32)
    for k in range(kvs):
        mine = (head >= k * per) & (head < (k + 1) * per)
        scores = jnp.where(mine, dot_nt(new_q, keys[k]), scores)
    index = tp * tok + col
    weights = jnp.where((index >= first) & (index < last), jnp.exp(scores * scale), 0.0)
    totals = jnp.sum(weights, axis=-1, keepdims=True)
    rounded = weights.astype(bf16)
    mixed = jnp.zeros((rows, lanes), f32)
    for k in range(kvs):
        mine = (head >= k * per) & (head < (k + 1) * per)
        mixed = mixed + dot(
            jnp.where(mine, rounded, jnp.zeros_like(rounded)), v_ref[:, k * lanes : (k + 1) * lanes]
        )
    self_score = jnp.sum(new_q.astype(f32) * new_k.astype(f32), axis=-1, keepdims=True)
    self_weight = jnp.where(tp == 0, jnp.exp(self_score * scale), 0.0)
    totals = totals + self_weight
    mixed = (mixed + self_weight * row_v[0:rows, :]) * jax.nn.sigmoid(row_g[0:rows, :])
    total_row = jnp.sum(jnp.where(row == col, totals, 0.0), axis=0, keepdims=True)
    high = total_row.astype(bf16).astype(f32)
    rest = pltpu.roll(jnp.broadcast_to(total_row - high, (8, lanes)), lanes // 2, 1)
    pay[0:rows, :] = mixed
    pay[rows + rpg : rows + rpg + 1, :] = jnp.where(
        iota((1, lanes), 1) < lanes // 2, high, rest[0:1, :]
    )
    peers = pay_ref.shape[0]
    tps = lax.axis_size("tp")
    slices = resid_ref.shape[1] // (tps * lanes)
    for z in range(slices):
        at = pl.ds(pl.multiple_of((z * tps + tp) * lanes, lanes), lanes)
        pay[rows : rows + rpg, :] = resid_ref[:, at].astype(f32)
        for g in range(pay_ref.shape[1]):
            out = pay[4 * g : 4 * g + 4, :].astype(bf16)
            for peer in range(z * peers // slices, (z + 1) * peers // slices):
                pay_ref[peer, g] = out
    leave[3].start()
    for copy in leave:
        copy.wait()


def fetch_kernel(gate_hbm, up_hbm, ng_hbm, mine_ref, ng_ref, sems):
    units = mine_ref.shape[1] // 2
    width = ng_ref.shape[1]
    req = lax.axis_index("req")
    at = pl.ds(pl.multiple_of(lax.rem(req, 2) * units, lanes), units)
    cols = pl.ds(pl.multiple_of(lax.div(req, 2) * width, lanes), width)
    copies = (
        pltpu.make_async_copy(gate_hbm.at[:, at], mine_ref.at[:, pl.ds(0, units)], sems.at[0]),
        pltpu.make_async_copy(up_hbm.at[:, at], mine_ref.at[:, pl.ds(units, units)], sems.at[1]),
        pltpu.make_async_copy(ng_hbm.at[:, cols], ng_ref, sems.at[2]),
    )
    for copy in copies:
        copy.start()
    for copy in copies:
        copy.wait()


def columns_kernel(w_hbm, down_hbm, w_ref, down_ref, sems):
    width = w_ref.shape[1]
    units = down_ref.shape[0]
    req = lax.axis_index("req")
    cols = pl.ds(pl.multiple_of(lax.div(req, 2) * width, lanes), width)
    theirs = pl.ds(pl.multiple_of((1 - lax.rem(req, 2)) * units, lanes), units)
    copies = (
        pltpu.make_async_copy(w_hbm.at[:, cols], w_ref, sems.at[0]),
        pltpu.make_async_copy(down_hbm.at[theirs, :], down_ref, sems.at[1]),
    )
    for copy in copies:
        copy.start()
    for copy in copies:
        copy.wait()


def ready_kernel(*refs):
    refs[-1][...] = jnp.zeros_like(refs[-1])


def hidden_kernel(
    pay_ref, w0_ref, w1_ref, w2_ref, w3_ref, mine_ref, pair_ref, ng_ref, _,
    hid_ref, msg_ref, att, hid, xs, acc, out,
):
    tp = lax.axis_index("tp")
    req = lax.axis_index("req")
    tps = lax.axis_size("tp")
    z, y = lax.div(req, 2), lax.rem(req, 2)
    heads, toks = att.shape[0], hid_ref.shape[0]
    groups = pay_ref.shape[0] // tps
    rpg = toks // groups
    rows = heads * rpg
    diag = iota((rows, lanes), 0) == iota((rows, lanes), 1)
    quads = pay_ref.shape[1]
    for r in range(groups):
        for g in range(quads):
            total = jnp.zeros((4, lanes), f32)
            for t in range(tps):
                piece = pay_ref[r * tps + t, g].astype(f32)
                total = total + piece
                if g == quads - 1:
                    hid[r * rpg : (r + 1) * rpg, t * lanes : (t + 1) * lanes] = piece[:rpg, :]
            acc[r, 4 * g : 4 * g + 4, :] = total
    for r in range(groups):
        total_row = jnp.broadcast_to(acc[r, pay_rows - 1 : pay_rows, :], (rows, lanes))
        total_row = total_row + pltpu.roll(total_row, lanes // 2, 1)
        totals = jnp.sum(jnp.where(diag, total_row, 0.0), axis=-1, keepdims=True)
        acc[r, 0:rows, :] = acc[r, 0:rows, :] / totals
    for r in range(groups):
        for h in range(heads):
            att[h, r * rpg : (r + 1) * rpg, :] = acc[r, h * rpg : (h + 1) * rpg, :]
    state = hid[0:toks, :]
    per = heads // tps
    for d, w_ref in enumerate((w0_ref, w1_ref, w2_ref, w3_ref)):
        source = tp ^ d
        for j in range(per):
            state = state + dot(
                att[source * per + j, 0:toks, :].astype(bf16), w_ref[j * lanes : (j + 1) * lanes, :]
            )
    hid_ref[...] = state
    width = state.shape[1]
    half = width // 2
    sums = jnp.sum(state * state, axis=-1, keepdims=True)
    scaled = state * ng_ref[...]
    xs[0] = scaled[:, :half]
    xs[1] = scaled[:, half:]
    own, other = xs[y].astype(bf16), xs[1 - y].astype(bf16)
    units = pair_ref.shape[1] // 2
    gate = dot(own, mine_ref[:, :units]) + dot(other, pair_ref[:, :units])
    up = dot(own, mine_ref[:, units:]) + dot(other, pair_ref[:, units:])
    square = iota((toks, lanes), 0) == iota((toks, lanes), 1)
    sums_row = jnp.sum(jnp.where(square, sums, 0.0), axis=0, keepdims=True)
    high = sums_row.astype(bf16).astype(f32)
    blocks = units // lanes
    for i in range(blocks):
        at = slice(i * lanes, (i + 1) * lanes)
        out[i * toks : (i + 1) * toks, :] = gate[:, at]
        out[(blocks + i) * toks : (blocks + i + 1) * toks, :] = up[:, at]
    base = 2 * blocks * toks
    first = iota((8, lanes), 0)
    out[base : base + 8, :] = jnp.where(
        first == 0, high, jnp.where(first == 1, sums_row - high, 0.0)
    )
    msg_ref[...] = out[0 : msg_ref.shape[0], :].astype(bf16)


def down_kernel(m0_ref, m1_ref, m2_ref, m3_ref, hid_ref, down_ref, pair_ref, back_ref, pay, whole):
    tp = lax.axis_index("tp")
    tps = lax.axis_size("tp")
    y = lax.rem(lax.axis_index("req"), 2)
    units, half = pair_ref.shape
    toks, width = hid_ref.shape
    total = m0_ref[...].astype(f32)
    for m_ref in (m1_ref, m2_ref, m3_ref):
        total = total + m_ref[...].astype(f32)
    whole[0 : total.shape[0], :] = total
    blocks = units // lanes
    base = 2 * blocks * toks
    square = iota((toks, lanes), 0) == iota((toks, lanes), 1)
    sums_row = whole[base : base + 1, :] + whole[base + 1 : base + 2, :]
    sums = jnp.sum(
        jnp.where(square, jnp.broadcast_to(sums_row, (toks, lanes)), 0.0), axis=-1, keepdims=True
    )
    factor = lax.rsqrt(sums / (width * 4) + norm_eps)
    pieces = []
    for i in range(blocks):
        gate = whole[i * toks : (i + 1) * toks, :] * factor
        up = whole[(blocks + i) * toks : (blocks + i + 1) * toks, :] * factor
        pieces.append((gate / (1.0 + jnp.exp(-gate)) * up).astype(bf16))
    hidden = jnp.concatenate(pieces, axis=1)
    own_rows = pl.ds(pl.multiple_of(y * units, lanes), units)
    mine, theirs = dot(hidden, down_ref[own_rows, :]), dot(hidden, pair_ref[...])
    part = (jnp.where(y == 0, mine, theirs), jnp.where(y == 0, theirs, mine))
    chunks = width // lanes
    groups = pay.shape[0]
    rpg = toks // groups
    for c in range(chunks):
        at = (c * lanes) % half
        block = part[c * lanes // half][:, at : at + lanes]
        adds = (y == 0) & (tp == c)
        block = block + jnp.where(adds, hid_ref[:, c * lanes : (c + 1) * lanes], 0.0)
        for r in range(groups):
            pay[r, c * rpg : (c + 1) * rpg, :] = block[r * rpg : (r + 1) * rpg, :]
    for r in range(groups):
        for g in range(back_ref.shape[1]):
            out = pay[r, 4 * g : 4 * g + 4, :].astype(bf16)
            for t in range(tps):
                back_ref[r * tps + t, g] = out


def final_kernel(back_ref, out_ref, acc, rows_out):
    tps = lax.axis_size("tp")
    peers = back_ref.shape[0]
    rpg, width = out_ref.shape
    slices = acc.shape[0]
    group = peers // slices
    chunks = width // (slices * lanes)
    for z in range(slices):
        for g in range(back_ref.shape[1]):
            total = back_ref[z * group, g].astype(f32)
            for p in range(1, group):
                total = total + back_ref[z * group + p, g].astype(f32)
            acc[z, 4 * g : 4 * g + 4, :] = total
    for z in range(slices):
        for c in range(chunks):
            at = slice((z * chunks + c) * lanes, (z * chunks + c + 1) * lanes)
            rows_out[0:rpg, at] = acc[z, c * rpg : (c + 1) * rpg, :]
    out_ref[...] = rows_out[0:rpg, :].astype(bf16)


def prefill_kernel(
    len_ref, q_ref, g_ref, kv0_ref, kv1_ref, kv2_ref, kv3_ref, qg_ref, freq_ref, out_ref, mid_ref
):
    tp = lax.axis_index("tp")
    tok = q_ref.shape[0]
    heads = q_ref.shape[1] // lanes
    kvs = kv0_ref.shape[1] // (2 * lanes)
    per = heads // kvs
    third = tp == 2
    mid_ref[...] = jnp.where(third, kv3_ref[...], kv1_ref[...])
    blocks = ((tp, kv0_ref), (jnp.where(third, tp ^ 3, tp ^ 1), mid_ref), (tp ^ 2, kv2_ref))
    tok_index = tp * tok + iota((tok, lanes), 0)
    begin = begin_of(tok_index, len_ref)
    factors = rope_factors((tok_index - begin).astype(f32) * freq_ref[...])
    col = iota((tok, tok), 1)
    allowed = []
    for block, _ in blocks:
        key_index = block * tok + col
        allowed.append((key_index >= begin) & (key_index <= tok_index))
    gates = jax.nn.sigmoid(g_ref[...].astype(f32))
    qg = qg_ref[...]
    scale = lanes ** (-0.5)
    for h in range(heads):
        k = h // per
        at = slice(h * lanes, (h + 1) * lanes)
        query = norm_rope(q_ref[:, at].astype(f32), qg, factors)
        totals = jnp.zeros((tok, 1), f32)
        mixed = jnp.zeros((tok, lanes), f32)
        for b, (_, kv_ref) in enumerate(blocks):
            scores = dot_nt(query, kv_ref[:, k * lanes : (k + 1) * lanes])
            weights = jnp.where(allowed[b], jnp.exp(scores * scale), 0.0)
            totals = totals + jnp.sum(weights, axis=-1, keepdims=True)
            mixed = mixed + dot(
                weights.astype(bf16), kv_ref[:, (kvs + k) * lanes : (kvs + k + 1) * lanes]
            )
        out_ref[:, at] = (mixed / totals * gates[:, h : h + 1]).astype(bf16)


def room(rows):
    return (rows + 15) // 8 * 8


def call(body, out_shape, args, scratch=(), hbm=False, out_any=False, smem=0, flops=0, limit=12):
    specs = [pl.BlockSpec(memory_space=pltpu.SMEM)] * smem
    space = pltpu.HBM if hbm else pltpu.VMEM
    specs += [pl.BlockSpec(memory_space=space)] * (len(args) - smem)
    size = sum(a.size * a.dtype.itemsize for a in args)
    return pl.pallas_call(
        body,
        out_shape=out_shape,
        in_specs=specs,
        out_specs=jax.tree.map(
            lambda _: pl.BlockSpec(memory_space=pl.ANY if out_any else pltpu.VMEM), out_shape
        ),
        scratch_shapes=[pltpu.VMEM(s, f32) if isinstance(s, tuple) else s for s in scratch],
        compiler_params=pltpu.CompilerParams(vmem_limit_bytes=limit * 2**20),
        cost_estimate=pl.CostEstimate(flops=flops, bytes_accessed=size, transcendentals=0),
    )(*args)


def hold(arrays, flops):
    return pl.pallas_call(
        ready_kernel,
        out_shape=jax.ShapeDtypeStruct((8, lanes), f32),
        in_specs=[pl.BlockSpec(memory_space=pl.ANY)] * len(arrays),
        out_specs=pl.BlockSpec(memory_space=pltpu.VMEM),
        compiler_params=pltpu.CompilerParams(vmem_limit_bytes=2**20),
        cost_estimate=pl.CostEstimate(flops=flops, bytes_accessed=0, transcendentals=0),
    )(*arrays)


def local(
    q_pre,
    gate_pre,
    k_pre,
    v_pre,
    q_gain,
    k_gain,
    lengths,
    q_new,
    gate_new,
    k_new,
    v_new,
    resid,
    w_out,
    norm_gain,
    w_gate,
    w_up,
    w_down,
):
    tps, reqs = lax.axis_size("tp"), lax.axis_size("req")
    tok = q_pre.shape[0]
    rpg, width = resid.shape
    slices = reqs // 2
    head_size = q_gain.shape[0]
    heads = gate_pre.shape[1]
    part = width // slices if slices else 0
    if not (slices == 4 and tps == 4 and head_size == lanes == tok and part == tps * lanes):
        return general(
            q_pre, gate_pre, k_pre, v_pre, q_gain, k_gain, lengths, q_new, gate_new, k_new, v_new,
            resid, w_out, norm_gain, w_gate, w_up, w_down,
        )
    peers = tps * reqs
    toks = rpg * reqs
    units = w_gate.shape[1] // 2
    req = lax.axis_index("req")
    z, y = req // 2, req % 2
    freqs = rope_base ** (-(np.arange(head_size // 2) * 2.0 / head_size))
    freqs = jnp.asarray(np.concatenate([freqs, freqs])[None, :], f32)
    qg, kg = q_gain[None, :], k_gain[None, :]

    def cross(array, by):
        return lax.ppermute(array, "tp", [(i, i ^ by) for i in range(tps)])

    def swap(array):
        return lax.ppermute(array, "req", [(i, i ^ 1) for i in range(reqs)])

    def along(array, by):
        return lax.ppermute(array, "req", [(i, i ^ (2 * by)) for i in range(reqs)])

    inputs = (
        lengths, k_pre, v_pre, q_new, k_new, v_new, gate_new, resid, qg, kg, freqs,
        w_out, w_gate, w_up,
    )
    outputs = (
        jax.ShapeDtypeStruct((tok, 2 * k_pre.shape[1]), bf16),
        jax.ShapeDtypeStruct((peers, pay_rows // 4, 4, lanes), bf16),
        jax.ShapeDtypeStruct((w_out.shape[0], part), bf16),
        jax.ShapeDtypeStruct((w_gate.shape[0], 2 * units), bf16),
    )
    kv, pay, w_own, pair = call(
        partial_kernel,
        outputs,
        inputs,
        scratch=[pltpu.VMEM(o.shape, o.dtype) for o in outputs]
        + [(room(heads * rpg), lanes)] * 4
        + [(room(pay_rows), lanes), pltpu.SMEM(lengths.shape, jnp.int32)]
        + [pltpu.VMEM(a.shape, a.dtype) for a in inputs[1:11]]
        + [pltpu.SemaphoreType.DMA((len(inputs),)), pltpu.SemaphoreType.DMA((len(outputs),))],
        hbm=True,
        out_any=True,
        flops=10**7,
        limit=56,
    )
    w_far = cross(w_own, 2)
    pair = swap(pair)
    half = jax.ShapeDtypeStruct((w_gate.shape[0], 2 * units), bf16)
    mine, ng = call(
        fetch_kernel,
        (half, jax.ShapeDtypeStruct((1, part), f32)),
        (w_gate, w_up, norm_gain[None, :]),
        hbm=True,
        scratch=[pltpu.SemaphoreType.DMA((3,))],
    )
    w_here, down_pair = call(
        columns_kernel,
        (
            jax.ShapeDtypeStruct(w_own.shape, bf16),
            jax.ShapeDtypeStruct((units, w_down.shape[1]), bf16),
        ),
        (w_out, w_down),
        hbm=True,
        scratch=[pltpu.SemaphoreType.DMA((2,))],
    )
    late_far, _, _ = lax.optimization_barrier((w_far, mine, w_here))
    w_near, w_both = cross(w_own, 1), cross(late_far, 1)
    kv_near = cross(kv, 1)
    late_kv, _ = lax.optimization_barrier((kv, w_far))
    kv_far = cross(late_kv, 2)
    late_down, _ = lax.optimization_barrier((down_pair, pair))
    down_pair = swap(late_down)
    got = lax.all_to_all(pay, ("req", "tp"), 0, 0, tiled=True)
    landed = hold((pair,), 2 * 10**9)
    token = hold((landed, w_near, w_both), 10**9)
    msg_shape = (2 * units // lanes * toks + 8, lanes)
    hid, msg = call(
        hidden_kernel,
        (
            jax.ShapeDtypeStruct((toks, part), f32),
            jax.ShapeDtypeStruct(msg_shape, bf16),
        ),
        (got, w_here, w_near, w_far, w_both, mine, pair, ng, token),
        scratch=[
            (heads, room(toks), lanes),
            (room(toks), part),
            (2, toks, part // 2),
            (reqs, room(pay_rows), lanes),
            (room(msg_shape[0]), lanes),
        ],
        flops=10**7,
    )
    msgs = [msg] + [along(msg, d) for d in (3, 2, 1)]
    kv_both = cross(kv_far, 1)
    prefill_out = call(
        prefill_kernel,
        jax.ShapeDtypeStruct(q_pre.shape, bf16),
        (lengths, q_pre, gate_pre, kv, kv_near, kv_far, kv_both, qg, freqs),
        scratch=[pltpu.VMEM(kv.shape, bf16)],
        smem=1,
        flops=10**9,
    )
    back = call(
        down_kernel,
        jax.ShapeDtypeStruct((peers, back_rows // 4, 4, lanes), bf16),
        (*msgs, hid, w_down, down_pair),
        scratch=[(reqs, room(back_rows), lanes), (room(msg_shape[0]), lanes)],
        flops=3 * 10**9,
    )
    returned = lax.all_to_all(back, ("req", "tp"), 0, 0, tiled=True)
    returned, prefill_out = lax.optimization_barrier((returned, prefill_out))
    decode_out = call(
        final_kernel,
        jax.ShapeDtypeStruct((rpg, width), bf16),
        (returned,),
        scratch=[(slices, room(back_rows), lanes), (room(rpg), width)],
        flops=10**6,
    )
    return (prefill_out, decode_out)


def solution(mesh):
    return jax.shard_map(
        local,
        mesh=mesh,
        in_specs=(
            P(("req", "tp"), None),
            P(("req", "tp"), None),
            P(("req", "tp"), None),
            P(("req", "tp"), None),
            P(),
            P(),
            P("req", None),
            P("req", None),
            P("req", None),
            P("req", None),
            P("req", None),
            P("req", None),
            P("tp", None),
            P(),
            P("req", "tp"),
            P("req", "tp"),
            P("tp", "req"),
        ),
        out_specs=(P(("req", "tp"), None), P("req", None)),
        check_vma=False,
    )
```
